32 devices in a mesh: dp: 8 (over z, x), tensor: 4 (over y, core).
Axes of the slice: x: 2, y: 2, z: 4, core: 2. Of those that a mesh axis runs over, the one named last changes fastest.
Arguments:
- x_in: float32 [8192, 1024], P(('dp', 'tensor')), may hold values from -6 to 6
- cotangent: float32 [8192, 1024], P(('dp', 'tensor')), may hold values from -6 to 6
- lengths: int32 [8], P('dp'), may hold values from 512 to 1024, as said below
- norm_gains: float32 [5, 1024], replicated, may hold values from 0.5 to 1.5
- ffn_first: bfloat16 [2, 1024, 4096], P(None, None, 'tensor'), may hold values from -0.1875 to 0.1875
- attn_qkv: bfloat16 [3, 1024, 1024], P(None, None, 'tensor'), may hold values from -0.1875 to 0.1875
- attn_out: bfloat16 [1024, 1024], P(None, 'tensor'), may hold values from -0.75 to 0.75
- rel_table: float32 [73, 128], replicated, may hold values from -6 to 6
- conv_proj: bfloat16 [3, 1024, 1024], P(None, None, 'tensor'), may hold values from -0.1875 to 0.1875
- depthwise: float32 [5, 1024], P(None, 'tensor'), may hold values from -2.5 to 2.5
- bn_gain: float32 [1024], P('tensor'), may hold values from 0.25 to 1.75
- bn_bias: float32 [1024], P('tensor'), may hold values from -1 to 1
- running: float32 [2, 1024], P(None, 'tensor'), may hold values from 0.1 to 1
- ffn_second: bfloat16 [2, 1024, 4096], P(None, None, 'tensor'), may hold values from -0.1875 to 0.1875
Outputs:
- block_out: float32 [8192, 1024], P(('dp', 'tensor'))
- grad_input: float32 [8192, 1024], P(('dp', 'tensor'))
- grad_norm_gains: float32 [5, 1024], replicated
- grad_ffn_first: float32 [2, 1024, 4096], P(None, 'dp', 'tensor')
- grad_attn_qkv: float32 [3, 1024, 1024], P(None, 'dp', 'tensor')
- grad_attn_out: float32 [1024, 1024], P('dp', 'tensor')
- grad_rel_table: float32 [73, 128], replicated
- grad_conv_proj: float32 [3, 1024, 1024], P(None, 'dp', 'tensor')
- grad_depthwise: float32 [5, 1024], P(None, 'tensor')
- grad_bn_gain: float32 [1024], P('tensor')
- grad_bn_bias: float32 [1024], P('tensor')
- new_running: float32 [2, 1024], P(None, 'tensor')
- grad_ffn_second: float32 [2, 1024, 4096], P(None, 'dp', 'tensor')
The draws below stay inside these ranges and needn't reach their ends.
Inputs may be any that keep to these rules, and one draw needn't show every extreme that they name: `lengths`: at least one utterance has exactly 1024 frames.
All inputs are finite; a program needn't handle non-finite values.
Results may differ from the reference program's by a relative error of at most 0.04.
Values may be sent and summed in bfloat16 or wider, within the bound.
No kernel may reach another device: no remote copies, remote signals or barrier semaphores. Data moves between devices by JAX's collectives and lax.ppermute only.
A program may use at most 192 MiB of HBM per device.

```python
import math
import jax
import jax.numpy as jnp
from jax import lax

D = 1024
HEADS = 8
HEAD = 128
FF = 4096
KERNEL = 5
LEFT = 64
RIGHT = 8
SLOT = 1024
UTTS = 8
FRAMES = 8192
REL = 73


def draw_lengths(key, part):
    first_key, second_key = jax.random.split(jax.random.fold_in(key, 11))
    drawn = jax.random.randint(first_key, (UTTS,), SLOT // 2, SLOT + 1)
    longest = jax.random.randint(second_key, (), 0, UTTS)
    return jnp.where(jnp.arange(UTTS) == longest, SLOT, drawn).astype(jnp.int32)


def levels(rng, shape, cuts, low, top_value):
    level, own = 1.0, jax.random.fold_in(rng, 6)
    for axis_at, shards_of in cuts:
        heights = jnp.exp(jax.random.uniform(jax.random.fold_in(own, axis_at), (shards_of,), jnp.float32, low / len(cuts), top_value / len(cuts)))
        level = level * jnp.repeat(heights, shape[axis_at] // shards_of).reshape([-1 if axis == axis_at else 1 for axis in range(len(shape))])
    return level


def gaussian(key, extent, spread, reach, pieces=(), dtype=jnp.bfloat16):
    values = spread * jax.random.normal(key, extent, jnp.float32)
    if pieces:
        values = values * levels(key, extent, pieces, -0.22, 0.18)
    return jnp.clip(values, -reach, reach).astype(dtype)


def setup_inputs(seed: int = 0) -> dict:
    key_of = jax.random.split(jax.random.key(seed), 15)
    return {
        "x_in": gaussian(key_of[0], (FRAMES, D), 1.0, 6.0, ((0, 32),), jnp.float32),
        "cotangent": gaussian(key_of[1], (FRAMES, D), 1.0, 6.0, ((0, 32),), jnp.float32),
        "lengths": draw_lengths(jax.random.fold_in(key_of[14], 71), 0),
        "norm_gains": jnp.clip(1.0 + 0.1 * jax.random.normal(key_of[3], (5, D), jnp.float32), 0.5, 1.5),
        "ffn_first": gaussian(key_of[4], (2, D, FF), D ** -0.5, 0.1875, ((2, 4),)),
        "attn_qkv": gaussian(key_of[5], (3, D, D), D ** -0.5, 0.1875, ((2, 4),)),
        "attn_out": gaussian(key_of[6], (D, D), (D // 16) ** -0.5, 0.75, ((1, 4),)),
        "rel_table": gaussian(key_of[7], (REL, HEAD), 1.0, 6.0, (), jnp.float32),
        "conv_proj": gaussian(key_of[8], (3, D, D), D ** -0.5, 0.1875, ((2, 4),)),
        "depthwise": gaussian(key_of[9], (KERNEL, D), KERNEL ** -0.5, 2.5, ((1, 4),), jnp.float32),
        "bn_gain": jnp.clip(1.0 + 0.15 * jax.random.normal(key_of[10], (D,), jnp.float32), 0.25, 1.75),
        "bn_bias": jnp.clip(jax.random.uniform(key_of[11], (D,), jnp.float32, -1.0, 1.0) * levels(key_of[11], (D,), ((0, 4),), -0.4, 0.0), -1.0, 1.0),
        "running": jnp.clip(jnp.exp(math.log(1.0) - 2.3025851 * jax.random.uniform(key_of[12], (2, D), jnp.float32) ** levels(key_of[12], (2, D), ((1, 4),), -0.2, 0.2)), 0.1, 1.0),
        "ffn_second": gaussian(key_of[13], (2, D, FF), D ** -0.5, 0.1875, ((2, 4),)),
    }


@jax.custom_vjp
def low(v):
    return lax.optimization_barrier(v.astype(jnp.bfloat16)).astype(jnp.float32)

@jax.custom_vjp
def low_back(v):
    return v

def low_keep(v):
    return (low(v), None)

def low_pass(kept, grad):
    return (grad,)

def back_keep(v):
    return (v, None)

def back_low(kept, grad):
    return (low(grad),)
low.defvjp(low_keep, low_pass)
low_back.defvjp(back_keep, back_low)
eps_norm = 1e-05
momentum = 0.5
highest = lax.Precision.HIGHEST

def matmul(left_op, right_op):
    return jnp.dot(left_op, right_op, precision=highest, preferred_element_type=jnp.float32)

def layer_norm(residual, scaling):
    average = lax.optimization_barrier(jnp.mean(residual, axis=-1, keepdims=True))
    centred = residual - average
    variance = lax.optimization_barrier(jnp.mean(centred * centred, axis=-1, keepdims=True))
    return centred * lax.rsqrt(variance + eps_norm) * scaling

def feed_forward(residual, scaling, weights):
    normed = low(layer_norm(residual, scaling))
    preact = low_back(matmul(normed, weights[0]))
    hidden = low(jax.nn.silu(preact))
    return low_back(matmul(hidden, weights[1].T))

def utterance_mix(queries, keys_all, values, rel_table, length):
    factor = HEAD ** (-0.5)
    position = jnp.arange(SLOT)
    distance = jnp.clip(position[None, :] - position[:, None], -LEFT, RIGHT) + LEFT
    content = jnp.einsum('qhe,khe->hqk', queries, keys_all, precision=highest)
    relative = jnp.einsum('qhe,re->hqr', queries, rel_table, precision=highest)
    bias_term = jnp.take_along_axis(relative, jnp.broadcast_to(distance[None], content.shape), axis=2)
    scores = low_back(factor * (content + bias_term))
    scores = jnp.where((position < length)[None, None, :], scores, -1e+30)
    probs_low = low(jax.nn.softmax(scores, axis=-1))
    return jnp.einsum('hqk,khe->qhe', probs_low, values, precision=highest)

def attention(residual, scaling, qkv_w, out_w, rel_table, lengths):
    normed = low(layer_norm(residual, scaling))
    shape_all = (UTTS, SLOT, HEADS, HEAD)
    queries = low(low_back(matmul(normed, qkv_w[0]))).reshape(shape_all)
    keys_all = low(low_back(matmul(normed, qkv_w[1]))).reshape(shape_all)
    values = low(low_back(matmul(normed, qkv_w[2]))).reshape(shape_all)
    mix_one = jax.checkpoint(utterance_mix)
    mixed = lax.map(lambda packed: mix_one(packed[0], packed[1], packed[2], rel_table, packed[3]), (queries, keys_all, values, lengths))
    heads_out = low(low_back(mixed.reshape(FRAMES, D)))
    return low_back(matmul(heads_out, out_w.T))

def convolution(residual, scaling, conv_w, kernel_w, bn_gain, bn_bias, valid):
    normed = low(layer_norm(residual, scaling))
    linear = low_back(matmul(normed, conv_w[0]))
    gating = low_back(matmul(normed, conv_w[1]))
    masked = linear * jax.nn.sigmoid(gating) * valid[:, None]
    margin = KERNEL // 2
    framed = jnp.pad(masked.reshape(UTTS, SLOT, D), ((0, 0), (margin, margin), (0, 0)))
    mixture = kernel_w[0] * framed[:, 0:SLOT]
    for tap_index in range(1, KERNEL):
        mixture = mixture + kernel_w[tap_index] * framed[:, tap_index:tap_index + SLOT]
    mixture = mixture.reshape(FRAMES, D)
    frame_count = jnp.sum(valid)
    batch_mean = lax.optimization_barrier(jnp.sum(mixture * valid[:, None], axis=0)) / frame_count
    batch_var = lax.optimization_barrier(jnp.sum(mixture * mixture * valid[:, None], axis=0)) / frame_count - batch_mean * batch_mean
    shifted = (mixture - batch_mean) * lax.rsqrt(batch_var + eps_norm) * bn_gain + bn_bias
    active = low(jax.nn.silu(shifted))
    return (low_back(matmul(active, conv_w[2].T)), (batch_mean, batch_var, frame_count))

def forward(params, lengths, valid):
    x_in, norm_gains, ffn_first, attn_qkv, attn_out, rel_table, conv_proj, depthwise, bn_gain, bn_bias, ffn_second = params
    step_ffn = jax.checkpoint(feed_forward)
    after_first = x_in + 0.5 * step_ffn(x_in, norm_gains[0], ffn_first)
    after_attn = after_first + attention(after_first, norm_gains[1], attn_qkv, attn_out, rel_table, lengths)
    change, statistics = convolution(after_attn, norm_gains[2], conv_proj, depthwise, bn_gain, bn_bias, valid)
    after_conv = after_attn + change
    after_last = after_conv + 0.5 * step_ffn(after_conv, norm_gains[3], ffn_second)
    return (layer_norm(after_last, norm_gains[4]) * valid[:, None], statistics)

def reference(x_in, cotangent, lengths, norm_gains, ffn_first, attn_qkv, attn_out, rel_table, conv_proj, depthwise, bn_gain, bn_bias, running, ffn_second):
    valid = (jnp.arange(SLOT)[None, :] < lengths[:, None]).astype(jnp.float32).reshape(FRAMES)
    floats = (x_in, norm_gains, ffn_first.astype(jnp.float32), attn_qkv.astype(jnp.float32), attn_out.astype(jnp.float32), rel_table, conv_proj.astype(jnp.float32), depthwise, bn_gain, bn_bias, ffn_second.astype(jnp.float32))

    def closed(params):
        return forward(params, lengths, valid)
    block_out, pull_back, statistics = jax.vjp(closed, floats, has_aux=True)
    gradients = pull_back(cotangent)[0]
    batch_mean, batch_var, frame_count = statistics
    updated = jnp.stack([(1.0 - momentum) * running[0] + momentum * batch_mean, (1.0 - momentum) * running[1] + momentum * batch_var * frame_count / (frame_count - 1.0)])
    return (block_out, gradients[0], gradients[1], gradients[2], gradients[3], gradients[4], gradients[5], gradients[6], gradients[7], gradients[8], gradients[9], updated, gradients[10])
```

```python
import functools

import jax
import jax.numpy as jnp
from jax import lax
from jax.experimental import pallas as pl
from jax.experimental.pallas import tpu as pltpu
from jax.sharding import PartitionSpec as P

HEAD = 128
KERNEL = 5
LEFT = 64
RIGHT = 8
SLOT = 1024
REL = 73
MARGIN = 16
SUB = 128
BLK = 256
WIN = 3 * SUB
WRAP = 512
LOG2E = 1.4426950408889634
VMEM_CAP = 48 * 1024 * 1024

eps_norm = 1e-05
momentum = 0.5
bf16 = jnp.bfloat16
f32 = jnp.float32


def nn(left_op, right_op):
    return lax.dot_general(
        left_op, right_op, (((1,), (0,)), ((), ())), preferred_element_type=f32
    )


def nt(left_op, right_op):
    return lax.dot_general(
        left_op, right_op, (((1,), (1,)), ((), ())), preferred_element_type=f32
    )


def tn(left_op, right_op):
    return lax.dot_general(
        left_op, right_op, (((0,), (0,)), ((), ())), preferred_element_type=f32
    )


def window_table(rel_table):
    u=jnp.arange(WRAP)
    dist=jnp.where(u<=WIN, jnp.clip(u-SUB,-LEFT,RIGHT), -LEFT)+LEFT
    ext=rel_table[dist]
    hi=ext.astype(jnp.bfloat16)
    lo=(ext-hi.astype(jnp.float32)).astype(jnp.bfloat16)
    return hi,lo

def order_in(dst, src, who, rows):
    for j in range(SLOT//rows):
        dst[j*rows:(j+1)*rows,:]=src[pl.ds(pl.multiple_of((j^who)*rows,rows),rows),:]

def attend_kernel(rows, who_ref, len_ref, q_ref, k_ref, v_ref, hi_ref, lo_ref, o_ref, p_ref, qs, ks, vs):
    who=who_ref[0]
    length=len_ref[0]
    order_in(qs,q_ref.at[0],who,rows); order_in(ks,k_ref.at[0],who,rows); order_in(vs,v_ref.at[0],who,rows)
    factor=HEAD**(-0.5)*LOG2E
    tail=lax.broadcasted_iota(jnp.int32,(SUB,SLOT//2),1)+SLOT//2<length
    for base in range(0,SLOT,BLK):
        q=qs[base:base+BLK,:]
        content=nt(q,ks[...])
        spread=nt(q,hi_ref[...])+nt(q,lo_ref[...])
        for off in range(0,BLK,SUB):
            i0=base+off
            e=spread[off:off+SUB]
            rolled=pltpu.roll(e,0,1,stride=1,stride_axis=0)
            lo_c=max(i0-SUB,0); hi_c=min(i0+2*SUB,SLOT)
            parts=[]
            if lo_c>0: parts.append(content[off:off+SUB,:lo_c]+e[:,0:1])
            parts.append(content[off:off+SUB,lo_c:hi_c]+rolled[:,lo_c-(i0-SUB):hi_c-(i0-SUB)])
            if hi_c<SLOT: parts.append(content[off:off+SUB,hi_c:]+e[:,WIN-1:WIN])
            logit=jnp.concatenate(parts,axis=1)*factor
            logit=jnp.concatenate([logit[:,:SLOT//2],jnp.where(tail,logit[:,SLOT//2:],-1e30)],axis=1)
            peak=jnp.max(logit,axis=1,keepdims=True)
            ex=jnp.exp2(logit-peak)
            tot=jnp.sum(ex,axis=1,keepdims=True)
            p_ref[0,i0:i0+SUB,:]=(ex*(1.0/tot)).astype(jnp.bfloat16)
        out=nn(p_ref[0,base:base+BLK,:],vs[...]).astype(jnp.bfloat16)
        for part in range(0,BLK,rows) if rows<BLK else (0,):
            n=min(rows,BLK)
            j=(base+part)//rows; inner=(base+part)%rows
            o_ref[pl.ds(pl.multiple_of((j^who)*rows+inner,n),n),:]=out[part:part+n]

def attend(qkv, who, length, rel_table, rows):
    heads=qkv.shape[2]//HEAD
    hi,lo=window_table(rel_table)
    spec=lambda m: pl.BlockSpec((1,SLOT,HEAD),lambda h,m=m:(m,0,h))
    smem=pl.BlockSpec(memory_space=pltpu.SMEM)
    tab=pl.BlockSpec((WRAP,HEAD),lambda h:(0,0))
    return pl.pallas_call(
        functools.partial(attend_kernel,rows),
        grid=(heads,),
        in_specs=[smem,smem,spec(0),spec(1),spec(2),tab,tab],
        out_specs=[pl.BlockSpec((SLOT,HEAD),lambda h:(0,h)),pl.BlockSpec((1,SLOT,SLOT),lambda h:(h,0,0))],
        out_shape=[jax.ShapeDtypeStruct((SLOT,heads*HEAD),jnp.bfloat16),jax.ShapeDtypeStruct((heads,SLOT,SLOT),jnp.bfloat16)],
        scratch_shapes=[pltpu.VMEM((SLOT,HEAD),jnp.bfloat16)]*3,
        compiler_params=pltpu.CompilerParams(vmem_limit_bytes=VMEM_CAP),
        cost_estimate=pl.CostEstimate(flops=heads*4*SLOT*SLOT*HEAD*2,bytes_accessed=heads*SLOT*SLOT*2,transcendentals=heads*SLOT*SLOT),
        name="attend",
    )(who,length,qkv,qkv,qkv,hi,lo)

def attend_back_kernel(rows, who_ref, q_ref, k_ref, v_ref, g_ref, p_ref, hi_ref, lo_ref, dq_ref, dk_ref, dv_ref, dt_ref, ds_ref, qs, ks, vs, gs, dkt, dvt):
    who=who_ref[0]
    for dst,src in ((qs,q_ref.at[0]),(ks,k_ref.at[0]),(vs,v_ref.at[0]),(gs,g_ref)):
        order_in(dst,src,who,rows)
    factor=HEAD**(-0.5)
    first=hi_ref[0:1,:].astype(jnp.float32)+lo_ref[0:1,:].astype(jnp.float32)
    final=hi_ref[WIN-1:WIN,:].astype(jnp.float32)+lo_ref[WIN-1:WIN,:].astype(jnp.float32)
    zero=jnp.zeros((SUB,SUB),jnp.float32)
    flip=(lax.broadcasted_iota(jnp.int32,(SUB,SUB),0)+lax.broadcasted_iota(jnp.int32,(SUB,SUB),1)==SUB-1).astype(jnp.bfloat16)
    table_acc=jnp.zeros((HEAD,WRAP),jnp.float32)
    left_acc=jnp.zeros((1,HEAD),jnp.float32)
    right_acc=jnp.zeros((1,HEAD),jnp.float32)
    for base in range(0,SLOT,BLK):
        q=qs[base:base+BLK,:]
        g=gs[base:base+BLK,:]
        pb=p_ref[0,base:base+BLK,:]
        p=pb.astype(jnp.float32)
        dp=nt(g,vs[...])
        delta=jnp.sum(p*dp,axis=1,keepdims=True)
        dsb=(p*(dp-delta)).astype(jnp.bfloat16)
        dv_part=tn(g,pb)
        dk_part=tn(q,dsb)
        if base==0:
            dvt[...]=dv_part; dkt[...]=dk_part
        else:
            dvt[...]+=dv_part; dkt[...]+=dk_part
        dq=nn(dsb,ks[...])
        ds=dsb.astype(jnp.float32)
        qf=q.astype(jnp.float32)
        extra=[]
        for off in range(0,BLK,SUB):
            i0=base+off
            d=ds[off:off+SUB]
            lo_c=max(i0-SUB,0); hi_c=min(i0+2*SUB,SLOT)
            turned=nn(flip,dsb[off:off+SUB,lo_c:hi_c])
            win=[zero]*((lo_c-(i0-SUB))//SUB)+[turned]+[zero]*((i0+2*SUB-hi_c)//SUB+1)
            moved=pltpu.roll(jnp.concatenate(win,axis=1),WRAP-SUB+1,1,stride=1,stride_axis=0)
            u=nn(flip,moved.astype(jnp.bfloat16)).astype(jnp.bfloat16)
            add=nn(u,hi_ref[...])+nn(u,lo_ref[...])
            table_acc=table_acc+tn(q[off:off+SUB],u)
            if lo_c>0:
                s=jnp.sum(d[:,:lo_c],axis=1,keepdims=True)
                add=add+s*first
                left_acc=left_acc+jnp.sum(s*qf[off:off+SUB],axis=0,keepdims=True)
            if hi_c<SLOT:
                s=jnp.sum(d[:,hi_c:],axis=1,keepdims=True)
                add=add+s*final
                right_acc=right_acc+jnp.sum(s*qf[off:off+SUB],axis=0,keepdims=True)
            extra.append(add)
        dq=((dq+jnp.concatenate(extra,axis=0))*factor).astype(jnp.bfloat16)
        for part in range(0,BLK,rows) if rows<BLK else (0,):
            n=min(rows,BLK)
            j=(base+part)//rows; inner=(base+part)%rows
            dq_ref[0,pl.ds(pl.multiple_of((j^who)*rows+inner,n),n),:]=dq[part:part+n]
    dt_ref[0]=table_acc*factor
    ds_ref[0]=jnp.concatenate([left_acc,right_acc,jnp.zeros((6,HEAD),jnp.float32)],axis=0)*factor
    for j in range(SLOT//rows):
        sl=pl.ds(pl.multiple_of((j^who)*rows,rows),rows)
        dk_ref[0,sl,:]=(jnp.transpose(dkt[:,j*rows:(j+1)*rows])*factor).astype(jnp.bfloat16)
        dv_ref[0,sl,:]=jnp.transpose(dvt[:,j*rows:(j+1)*rows]).astype(jnp.bfloat16)

def attend_back(qkv, grad, probs, who, rel_table, rows):
    heads=qkv.shape[2]//HEAD
    hi,lo=window_table(rel_table)
    spec=lambda m: pl.BlockSpec((1,SLOT,HEAD),lambda h,m=m:(m,0,h))
    smem=pl.BlockSpec(memory_space=pltpu.SMEM)
    tab=pl.BlockSpec((WRAP,HEAD),lambda h:(0,0))
    out=pl.BlockSpec((1,SLOT,HEAD),lambda h:(0,0,h))
    shape=jax.ShapeDtypeStruct((1,SLOT,heads*HEAD),jnp.bfloat16)
    dq,dk,dv,dt,ends=pl.pallas_call(
        functools.partial(attend_back_kernel,rows),
        grid=(heads,),
        in_specs=[smem,spec(0),spec(1),spec(2),pl.BlockSpec((SLOT,HEAD),lambda h:(0,h)),pl.BlockSpec((1,SLOT,SLOT),lambda h:(h,0,0)),tab,tab],
        out_specs=[out,out,out,pl.BlockSpec((1,HEAD,WRAP),lambda h:(h,0,0)),pl.BlockSpec((1,8,HEAD),lambda h:(h,0,0))],
        out_shape=[shape,shape,shape,jax.ShapeDtypeStruct((heads,HEAD,WRAP),jnp.float32),jax.ShapeDtypeStruct((heads,8,HEAD),jnp.float32)],
        scratch_shapes=[pltpu.VMEM((SLOT,HEAD),jnp.bfloat16)]*4+[pltpu.VMEM((HEAD,SLOT),jnp.float32)]*2,
        compiler_params=pltpu.CompilerParams(vmem_limit_bytes=VMEM_CAP),
        cost_estimate=pl.CostEstimate(flops=heads*6*SLOT*SLOT*HEAD*2,bytes_accessed=heads*SLOT*SLOT*2,transcendentals=0),
        name="attend_back",
    )(who,qkv,qkv,qkv,grad,probs,hi,lo)
    wide=jnp.sum(dt,axis=0).T
    ends=jnp.sum(ends,axis=0)
    near=SUB-LEFT; far=SUB+RIGHT
    left=jnp.sum(wide[:near+1],axis=0)+jnp.sum(wide[WIN+1:],axis=0)+ends[0]
    right=jnp.sum(wide[far:WIN+1],axis=0)+ends[1]
    return dq[0],dk[0],dv[0],jnp.concatenate([left[None],wide[near+1:far],right[None]],axis=0)


class Links:
    def __init__(self, dp, tensor):
        self.dp, self.tensor, self.ny = dp, tensor, tensor // 2
        masks = [1 << bit for bit in range(dp.bit_length() - 1)]
        if len(masks) > 2:
            masks[2] = 6
        self.masks = masks

    def core(self, value):
        return lax.ppermute(value, "tensor", [(i, i ^ 1) for i in range(self.tensor)])

    def chip(self, value, k):
        return lax.ppermute(value, "tensor", [(i, i ^ (2 * k)) for i in range(self.tensor)])

    def group(self, value, mask):
        return lax.ppermute(value, "dp", [(i, i ^ mask) for i in range(self.dp)])

    def sum_group(self, value):
        for mask in self.masks:
            value = value + self.group(value, mask)
        return value

    def sum_chips(self, pieces):
        stacked = jnp.stack(pieces)
        total = stacked
        for k in range(1, self.ny):
            other = self.chip(stacked, k)
            total = total + jnp.stack([other[r ^ k] for r in range(self.ny)])
        return [total[r] for r in range(self.ny)]

    def widen(self, own):
        return jnp.concatenate([own, self.core(own)], axis=0)

    def narrow(self, partial):
        rows = partial.shape[0] // 2
        return partial[:rows].astype(f32) + self.core(partial[rows:]).astype(f32)

    def gather_chips(self, own):
        return [own] + [self.chip(own, k) for k in range(1, self.ny)]

    def order(self):
        return list(range(1, self.ny)) + [0]

    def scatter_chips(self, parts):
        total = parts[0]
        for k in range(1, self.ny):
            total = total + self.chip(parts[k].astype(bf16), k).astype(f32)
        return total

    def spread_chips(self, parts):
        sent = [part.astype(bf16) for part in parts]
        totals = list(parts)
        for k in range(1, self.ny):
            for r in range(self.ny):
                totals[r] = totals[r] + self.chip(sent[r ^ k], k).astype(f32)
        return totals

    def halo(self, own_rows):
        count = own_rows.shape[0]
        y = lax.axis_index("tensor") // 2
        head, foot = own_rows[:MARGIN], own_rows[count - MARGIN :]
        if self.ny == 2:
            other = self.chip(jnp.where(y == 0, foot, head), 1)
            zero = jnp.zeros_like(other)
            return jnp.where(y == 0, zero, other), jnp.where(y == 0, other, zero)
        down = [(i, i + 2) for i in range(self.tensor - 2)]
        up = [(i + 2, i) for i in range(self.tensor - 2)]
        return lax.ppermute(foot, "tensor", down), lax.ppermute(head, "tensor", up)

    def in_order(self, own):
        c = lax.axis_index("tensor") % 2
        mate = self.core(own)
        rows = jnp.where(
            c == 0, jnp.concatenate([own, mate], axis=0), jnp.concatenate([mate, own], axis=0)
        )
        count = own.shape[0]
        y = lax.axis_index("tensor") // 2
        before, after = self.halo(rows)
        return jnp.concatenate([before, rows, after], axis=0)

    def out_order(self, partial):
        c = lax.axis_index("tensor") % 2
        rows = partial.shape[0] // 2
        own = lax.dynamic_slice_in_dim(partial, c * rows, rows)
        mate = lax.dynamic_slice_in_dim(partial, (1 - c) * rows, rows)
        return own.astype(f32) + self.core(mate).astype(f32)

    def reduce_grad(self, grad, turn):
        if self.dp == 1:
            return grad.astype(f32)
        count = len(self.masks)
        masks = [self.masks[(turn + i) % count] for i in range(count)]
        blocks = grad.reshape(self.dp, grad.shape[0] // self.dp, grad.shape[1])
        me = lax.axis_index("dp")

        def pick(offsets):
            return jnp.concatenate(
                [lax.dynamic_index_in_dim(blocks, me ^ off, 0, keepdims=True) for off in offsets]
            )

        offsets = [0]
        for mask in masks[:0:-1]:
            offsets = offsets + [off ^ mask for off in offsets]
        kept = pick(offsets).astype(f32)
        sent = pick([off ^ masks[0] for off in offsets])
        kept = kept + self.group(sent.astype(bf16), masks[0]).astype(f32)
        for mask in masks[1:]:
            half = kept.shape[0] // 2
            kept = kept[:half] + self.group(kept[half:].astype(bf16), mask).astype(f32)
        return kept[0]


def moments(rows):
    centred = rows - jnp.mean(rows, axis=1, keepdims=True)
    inverse = lax.rsqrt(jnp.mean(centred * centred, axis=1, keepdims=True) + eps_norm)
    return centred * inverse, inverse


def norm_back(upstream, rows, scaling):
    normed, inverse = moments(rows)
    weighted = upstream * scaling
    first_mean = jnp.mean(weighted, axis=1, keepdims=True)
    second_mean = jnp.mean(weighted * normed, axis=1, keepdims=True)
    return inverse * (weighted - first_mean - normed * second_mean)


def gain_sum(upstream, rows):
    return jnp.sum(upstream * moments(rows)[0], axis=0)


def normalized(rows, scaling):
    return (moments(rows)[0] * scaling).astype(bf16)


def silu_slope(preact):
    logistic = jax.nn.sigmoid(preact)
    return logistic * (1.0 + preact * (1.0 - logistic))


def feed_forward(links, rows, scaling, weights):
    parts, stored = {}, {}
    for k in range(links.ny):
        inputs = links.widen(normalized(rows[k], scaling))
        preact = nn(inputs, weights[0])
        hidden = jax.nn.silu(preact).astype(bf16)
        parts[k] = links.narrow(nt(hidden, weights[1]).astype(bf16))
        stored[k] = (inputs, preact.astype(bf16), hidden)
    return [parts[k] for k in range(links.ny)], stored


def feed_back(links, upstream, weights, stored):
    parts, seen = {}, {}
    for k in links.order():
        inputs, preact, hidden = stored[k]
        upper = links.widen((0.5 * upstream[k]).astype(bf16))
        grad_pre = (nn(upper, weights[1]) * silu_slope(preact.astype(f32))).astype(bf16)
        parts[k] = links.narrow(nt(grad_pre, weights[0]).astype(bf16))
        seen[k] = (inputs, grad_pre, upper, hidden)
    whole = [jnp.concatenate([seen[k][i] for k in range(links.ny)]) for i in range(4)]
    grads = (tn(whole[0], whole[1]).astype(bf16), tn(whole[2], whole[3]).astype(bf16))
    return [parts[k] for k in range(links.ny)], grads


def per_device(
    links,
    x_in,
    cotangent,
    lengths,
    norm_gains,
    ffn_first,
    attn_qkv,
    attn_out,
    rel_table,
    conv_proj,
    depthwise,
    bn_gain,
    bn_bias,
    running,
    ffn_second,
):
    ny = links.ny
    rows = x_in.shape[0]
    width = x_in.shape[1]
    channels = bn_gain.shape[0]
    who = lax.axis_index("tensor")
    y = who // 2
    length = lengths[0]

    me = lax.axis_index("dp")
    share = width // links.dp
    piece = lax.dynamic_slice_in_dim(conv_proj, me * share, share, axis=1)
    conv_w = [[conv_proj[m] for m in range(3)]]
    for k in range(1, ny):
        other = links.chip(piece, k).reshape(3 * share, channels)
        other = lax.all_gather(other, "dp", axis=0, tiled=True)
        other = other.reshape(links.dp, 3, share, channels)
        conv_w.append([other[:, m].reshape(width, channels) for m in range(3)])
    conv_w = [jnp.concatenate([conv_w[k][m] for k in range(ny)], axis=1) for m in range(3)]
    small = jnp.concatenate([depthwise, bn_gain[None], bn_bias[None], jnp.zeros((1, channels), f32)])
    small = jnp.concatenate(links.gather_chips(small), axis=1)
    taps, scale_bn, bias_bn = small[:KERNEL], small[KERNEL], small[KERNEL + 1]

    resid = [x_in] + [other.astype(f32) for other in links.gather_chips(x_in.astype(bf16))[1:]]
    parts, stored_first = feed_forward(links, resid, norm_gains[0], ffn_first)
    change = links.spread_chips(parts)
    first = [resid[k] + 0.5 * change[k] for k in range(ny)]

    attn_in = [links.widen(normalized(first[k], norm_gains[1])) for k in range(ny)]
    qkv = jnp.concatenate(
        [
            jnp.stack([nn(attn_in[k], attn_qkv[m]).astype(bf16) for m in range(3)])
            for k in range(ny)
        ],
        axis=1,
    )
    who_arr = who.reshape(1).astype(jnp.int32)
    heads_out, probs = attend(qkv, who_arr, lengths, rel_table, rows)
    parts = {}
    for k in links.order():
        piece_k = heads_out[2 * rows * k : 2 * rows * (k + 1)]
        parts[k] = links.narrow(nt(piece_k, attn_out).astype(bf16))
    after_attn = first[0] + links.scatter_chips(parts)

    count = 2 * rows
    lo, hi = MARGIN, MARGIN + count
    position = y * count - MARGIN + jnp.arange(count + 2 * MARGIN)
    valid = ((position >= 0) & (position < length)).astype(f32)[:, None]
    conv_in = links.in_order(normalized(after_attn, norm_gains[2]))
    linear = nn(conv_in, conv_w[0])
    gating = jax.nn.sigmoid(nn(conv_in, conv_w[1]))
    glu = linear * gating * valid

    def shifted_by(array, offset):
        wide = jnp.pad(array, ((2, 2), (0, 0)))
        return wide[2 + offset : 2 + offset + array.shape[0]]

    mixture = sum(taps[j] * shifted_by(glu, j - 2) for j in range(KERNEL))
    inside = valid[lo:hi] * mixture[lo:hi]
    tallies = jnp.concatenate(
        [
            jnp.sum(inside, axis=0)[None],
            jnp.sum(inside * mixture[lo:hi], axis=0)[None],
            jnp.broadcast_to(jnp.sum(valid[lo:hi]), (1, inside.shape[1])),
            jnp.zeros((5, inside.shape[1]), f32),
        ]
    )

    def sum_stats(array):
        cols = [array[:, k * channels : (k + 1) * channels] for k in range(ny)]
        return links.sum_group(jnp.concatenate(links.sum_chips(cols), axis=1))

    tallies = sum_stats(tallies)
    frame_count = tallies[2, 0]
    batch_mean = tallies[0] / frame_count
    batch_var = tallies[1] / frame_count - batch_mean * batch_mean
    batch_inv = lax.rsqrt(batch_var + eps_norm)
    updated = jnp.stack(
        [
            (1.0 - momentum) * running[0] + momentum * batch_mean[:channels],
            (1.0 - momentum) * running[1]
            + momentum * batch_var[:channels] * frame_count / (frame_count - 1.0),
        ]
    )
    centred = (mixture - batch_mean) * batch_inv
    shifted = centred * scale_bn + bias_bn
    active = jax.nn.silu(shifted[lo:hi]).astype(bf16)
    after_conv = after_attn + links.out_order(nt(active, conv_w[2]).astype(bf16))

    upstream_in = links.gather_chips(cotangent.astype(bf16))
    resid = [after_conv] + [o.astype(f32) for o in links.gather_chips(after_conv.astype(bf16))[1:]]
    parts, stored_last = feed_forward(links, resid, norm_gains[3], ffn_second)
    change = links.spread_chips(parts)
    last = [resid[k] + 0.5 * change[k] for k in range(ny)]
    c = who % 2
    own_valid = [
        ((((y ^ k) * 2 + c) * rows + jnp.arange(rows)) < length).astype(f32)[:, None]
        for k in range(ny)
    ]
    output = moments(last[0])[0] * norm_gains[4] * own_valid[0]
    upper = [cotangent] + [other.astype(f32) for other in upstream_in[1:]]
    upper = [upper[k] * own_valid[k] for k in range(ny)]
    gain_five = gain_sum(upper[0], last[0])
    grad = [norm_back(upper[k], last[k], norm_gains[4]) for k in range(ny)]

    parts, grads_last = feed_back(links, grad, ffn_second, stored_last)
    grad_scaled = links.scatter_chips(parts)
    gain_four = gain_sum(grad_scaled, after_conv)
    grad = grad[0] + norm_back(grad_scaled, after_conv, norm_gains[3])

    upper = links.in_order(grad.astype(bf16))
    grad_shift = nn(upper, conv_w[2]) * silu_slope(shifted) * valid
    inner = grad_shift[lo:hi]
    tallies = jnp.concatenate(
        [
            jnp.sum(inner * centred[lo:hi], axis=0)[None],
            jnp.sum(inner, axis=0)[None],
            jnp.zeros((6, inner.shape[1]), f32),
        ]
    )
    tallies = sum_stats(tallies)
    gain_grad, bias_grad = tallies[0], tallies[1]
    grad_mix = (
        valid
        * (scale_bn * batch_inv)
        * (grad_shift - (bias_grad + centred * gain_grad) / frame_count)
    )
    grad_glu = sum(taps[j] * shifted_by(grad_mix, 2 - j) for j in range(KERNEL))[lo:hi]
    grad_glu = grad_glu * valid[lo:hi]
    kernel_grad = jnp.stack(
        [
            jnp.sum(grad_mix[lo:hi] * glu[lo + j - 2 : hi + j - 2], axis=0)
            for j in range(KERNEL)
        ]
    )
    gates = gating[lo:hi]
    grad_linear = (grad_glu * gates).astype(bf16)
    grad_gating = (grad_glu * linear[lo:hi] * gates * (1.0 - gates)).astype(bf16)
    partial = nt(grad_linear, conv_w[0]) + nt(grad_gating, conv_w[1])
    grad_scaled = links.out_order(partial.astype(bf16))
    conv_grads = [
        tn(conv_in[lo:hi], grad_linear).astype(bf16),
        tn(conv_in[lo:hi], grad_gating).astype(bf16),
        tn(upper[lo:hi], active).astype(bf16),
    ]
    gain_three = gain_sum(grad_scaled, after_attn)
    grad = grad + norm_back(grad_scaled, after_attn, norm_gains[2])

    upper = links.gather_chips(grad.astype(bf16))
    grad = [grad] + [other.astype(f32) for other in upper[1:]]
    upper = jnp.concatenate([links.widen(upper[k]) for k in range(ny)])
    grad_heads = nn(upper, attn_out).astype(bf16)
    out_grad = tn(upper, heads_out).astype(bf16)
    grad_q, grad_k, grad_v, table_grad = attend_back(
        qkv, grad_heads, probs, who_arr, rel_table, rows
    )
    members = (grad_q, grad_k, grad_v)
    parts = {}
    for k in links.order():
        partial = sum(
            nt(members[m][2 * rows * k : 2 * rows * (k + 1)], attn_qkv[m]) for m in range(3)
        )
        parts[k] = links.narrow(partial.astype(bf16))
    inputs = jnp.concatenate(attn_in)
    qkv_grads = [tn(inputs, members[m]).astype(bf16) for m in range(3)]
    change = links.spread_chips([parts[k] for k in range(ny)])
    gain_two = gain_sum(change[0], first[0])
    grad = [grad[k] + norm_back(change[k], first[k], norm_gains[1]) for k in range(ny)]

    parts, grads_first = feed_back(links, grad, ffn_first, stored_first)
    grad_scaled = links.scatter_chips(parts)
    gain_one = gain_sum(grad_scaled, x_in)
    grad_input = grad[0] + norm_back(grad_scaled, x_in, norm_gains[0])

    first_sum = jnp.stack([links.reduce_grad(grads_first[m], m) for m in range(2)])
    last_sum = jnp.stack([links.reduce_grad(grads_last[m], m + 1) for m in range(2)])
    wide = jnp.concatenate(qkv_grads + [out_grad], axis=1)
    wide = links.reduce_grad(wide, 2)
    heads_cols = attn_qkv.shape[2]
    qkv_sum = jnp.stack([wide[:, m * heads_cols : (m + 1) * heads_cols] for m in range(3)])
    out_sum = wide[:, 3 * heads_cols :]
    conv_sum = links.reduce_grad(jnp.concatenate(conv_grads, axis=1), 1)
    conv_sum = conv_sum.reshape(share, 3, ny, channels)
    total = conv_sum[:, :, 0]
    for k in range(1, ny):
        total = total + links.chip(conv_sum[:, :, k].astype(bf16), k).astype(f32)
    conv_sum = jnp.swapaxes(total, 0, 1)

    kernel_grad = sum_stats(jnp.pad(kernel_grad, ((0, 3), (0, 0))))[:KERNEL, :channels]
    gains = jnp.stack([gain_one, gain_two, gain_three, gain_four, gain_five]).reshape(-1, HEAD)
    bundle = jnp.concatenate([gains, table_grad])
    bundle = jnp.pad(bundle, ((0, -bundle.shape[0] % 8), (0, 0)))
    bundle = bundle + links.core(bundle)
    for k in [1 << bit for bit in range(ny.bit_length() - 1)]:
        bundle = bundle + links.chip(bundle, k)
    bundle = links.sum_group(bundle)
    return (
        output,
        grad_input,
        bundle[: gains.shape[0]].reshape(5, width),
        first_sum,
        qkv_sum,
        out_sum,
        bundle[gains.shape[0] : gains.shape[0] + REL],
        conv_sum,
        kernel_grad,
        gain_grad[:channels],
        bias_grad[:channels],
        updated,
        last_sum,
    )


def solution(mesh):
    links = Links(mesh.shape["dp"], mesh.shape["tensor"])
    placed = (
        P(("dp", "tensor"), None),
        P(("dp", "tensor"), None),
        P("dp"),
        P(),
        P(None, None, "tensor"),
        P(None, None, "tensor"),
        P(None, "tensor"),
        P(),
        P(None, None, "tensor"),
        P(None, "tensor"),
        P("tensor"),
        P("tensor"),
        P(None, "tensor"),
        P(None, None, "tensor"),
    )
    return jax.shard_map(
        functools.partial(per_device, links),
        mesh=mesh,
        in_specs=placed,
        out_specs=(
            P(("dp", "tensor"), None),
            P(("dp", "tensor"), None),
            P(),
            P(None, "dp", "tensor"),
            P(None, "dp", "tensor"),
            P("dp", "tensor"),
            P(),
            P(None, "dp", "tensor"),
            P(None, "tensor"),
            P("tensor"),
            P("tensor"),
            P(None, "tensor"),
            P(None, "dp", "tensor"),
        ),
        check_vma=False,
    )
```

```python
import functools

import jax
import jax.numpy as jnp
from jax import lax
from jax.experimental import pallas as pl
from jax.experimental.pallas import tpu as pltpu
from jax.sharding import PartitionSpec as P

HEAD = 128
KERNEL = 5
LEFT = 64
RIGHT = 8
SLOT = 1024
REL = 73
MARGIN = 16
SUB = 128
BLK = 256
WIN = 3 * SUB
WRAP = 512
LOG2E = 1.4426950408889634
VMEM_CAP = 32 * 1024 * 1024

eps_norm = 1e-05
momentum = 0.5
bf16 = jnp.bfloat16
f32 = jnp.float32


def nn(left_op, right_op):
    return lax.dot_general(
        left_op, right_op, (((1,), (0,)), ((), ())), preferred_element_type=f32
    )


def nt(left_op, right_op):
    return lax.dot_general(
        left_op, right_op, (((1,), (1,)), ((), ())), preferred_element_type=f32
    )


def tn(left_op, right_op):
    return lax.dot_general(
        left_op, right_op, (((0,), (0,)), ((), ())), preferred_element_type=f32
    )


def window_table(rel_table):
    near,far=SUB-LEFT,SUB+RIGHT
    width=rel_table.shape[1]
    ext=jnp.concatenate([
        jnp.broadcast_to(rel_table[:1],(near,width)),
        rel_table,
        jnp.broadcast_to(rel_table[REL-1:],(WIN-far,width)),
        jnp.broadcast_to(rel_table[:1],(WRAP-WIN-1,width)),
    ])
    hi=ext.astype(jnp.bfloat16)
    lo=(ext-hi.astype(jnp.float32)).astype(jnp.bfloat16)
    return hi,lo

def order_in(dst, src, who, rows):
    for j in range(SLOT//rows):
        dst[j*rows:(j+1)*rows,:]=src[pl.ds(pl.multiple_of((j^who)*rows,rows),rows),:]

def attend_kernel(rows, who_ref, len_ref, q_ref, k_ref, v_ref, hi_ref, lo_ref, o_ref, p_ref, qs, ks, vs):
    who=who_ref[0]
    length=len_ref[0]
    order_in(qs,q_ref.at[0],who,rows); order_in(ks,k_ref.at[0],who,rows); order_in(vs,v_ref.at[0],who,rows)
    factor=HEAD**(-0.5)*LOG2E
    tail=lax.broadcasted_iota(jnp.int32,(SUB,SLOT//2),1)+SLOT//2<length
    for base in range(0,SLOT,BLK):
        q=qs[base:base+BLK,:]
        content=nt(q,ks[...])
        spread=nt(q,hi_ref[...])+nt(q,lo_ref[...])
        for off in range(0,BLK,SUB):
            i0=base+off
            e=spread[off:off+SUB]
            rolled=pltpu.roll(e,0,1,stride=1,stride_axis=0)
            lo_c=max(i0-SUB,0); hi_c=min(i0+2*SUB,SLOT)
            parts=[]
            if lo_c>0: parts.append(content[off:off+SUB,:lo_c]+e[:,0:1])
            parts.append(content[off:off+SUB,lo_c:hi_c]+rolled[:,lo_c-(i0-SUB):hi_c-(i0-SUB)])
            if hi_c<SLOT: parts.append(content[off:off+SUB,hi_c:]+e[:,WIN-1:WIN])
            logit=jnp.concatenate(parts,axis=1)*factor
            logit=jnp.concatenate([logit[:,:SLOT//2],jnp.where(tail,logit[:,SLOT//2:],-1e30)],axis=1)
            peak=jnp.max(logit,axis=1,keepdims=True)
            ex=jnp.exp2(logit-peak)
            tot=jnp.sum(ex,axis=1,keepdims=True)
            p_ref[0,i0:i0+SUB,:]=(ex*(1.0/tot)).astype(jnp.bfloat16)
        out=nn(p_ref[0,base:base+BLK,:],vs[...]).astype(jnp.bfloat16)
        for part in range(0,BLK,rows) if rows<BLK else (0,):
            n=min(rows,BLK)
            j=(base+part)//rows; inner=(base+part)%rows
            o_ref[pl.ds(pl.multiple_of((j^who)*rows+inner,n),n),:]=out[part:part+n]

def attend(qkv, who, length, rel_table, rows):
    heads=qkv.shape[2]//HEAD
    hi,lo=window_table(rel_table)
    spec=lambda m: pl.BlockSpec((1,SLOT,HEAD),lambda h,m=m:(m,0,h))
    smem=pl.BlockSpec(memory_space=pltpu.SMEM)
    tab=pl.BlockSpec((WRAP,HEAD),lambda h:(0,0))
    return pl.pallas_call(
        functools.partial(attend_kernel,rows),
        grid=(heads,),
        in_specs=[smem,smem,spec(0),spec(1),spec(2),tab,tab],
        out_specs=[pl.BlockSpec((SLOT,HEAD),lambda h:(0,h)),pl.BlockSpec((1,SLOT,SLOT),lambda h:(h,0,0))],
        out_shape=[jax.ShapeDtypeStruct((SLOT,heads*HEAD),jnp.bfloat16),jax.ShapeDtypeStruct((heads,SLOT,SLOT),jnp.bfloat16)],
        scratch_shapes=[pltpu.VMEM((SLOT,HEAD),jnp.bfloat16)]*3,
        compiler_params=pltpu.CompilerParams(vmem_limit_bytes=VMEM_CAP),
        cost_estimate=pl.CostEstimate(flops=1<<20,bytes_accessed=1<<20,transcendentals=0),
        name="attend",
    )(who,length,qkv,qkv,qkv,hi,lo)

def attend_back_kernel(rows, who_ref, q_ref, k_ref, v_ref, g_ref, p_ref, hi_ref, lo_ref, d_ref, dt_ref, ds_ref, qs, ks, vs, gs, dkt, dvt):
    who=who_ref[0]
    for dst,src in ((qs,q_ref.at[0]),(ks,k_ref.at[0]),(vs,v_ref.at[0]),(gs,g_ref)):
        order_in(dst,src,who,rows)
    factor=HEAD**(-0.5)
    first=hi_ref[0:1,:].astype(jnp.float32)+lo_ref[0:1,:].astype(jnp.float32)
    final=hi_ref[WIN-1:WIN,:].astype(jnp.float32)+lo_ref[WIN-1:WIN,:].astype(jnp.float32)
    zero=jnp.zeros((SUB,SUB),jnp.float32)
    flip=(lax.broadcasted_iota(jnp.int32,(SUB,SUB),0)+lax.broadcasted_iota(jnp.int32,(SUB,SUB),1)==SUB-1).astype(jnp.bfloat16)
    table_acc=jnp.zeros((HEAD,WRAP),jnp.float32)
    left_acc=jnp.zeros((1,HEAD),jnp.float32)
    right_acc=jnp.zeros((1,HEAD),jnp.float32)
    for base in range(0,SLOT,BLK):
        q=qs[base:base+BLK,:]
        g=gs[base:base+BLK,:]
        pb=p_ref[0,base:base+BLK,:]
        p=pb.astype(jnp.float32)
        dp=nt(g,vs[...])
        delta=jnp.sum(p*dp,axis=1,keepdims=True)
        dsb=(p*(dp-delta)).astype(jnp.bfloat16)
        dv_part=tn(g,pb)
        dk_part=tn(q,dsb)
        if base==0:
            dvt[...]=dv_part; dkt[...]=dk_part
        else:
            dvt[...]+=dv_part; dkt[...]+=dk_part
        dq=nn(dsb,ks[...])
        ds=dsb.astype(jnp.float32)
        qf=q.astype(jnp.float32)
        extra=[]
        for off in range(0,BLK,SUB):
            i0=base+off
            d=ds[off:off+SUB]
            lo_c=max(i0-SUB,0); hi_c=min(i0+2*SUB,SLOT)
            turned=nn(flip,dsb[off:off+SUB,lo_c:hi_c])
            win=[zero]*((lo_c-(i0-SUB))//SUB)+[turned]+[zero]*((i0+2*SUB-hi_c)//SUB+1)
            moved=pltpu.roll(jnp.concatenate(win,axis=1),WRAP-SUB+1,1,stride=1,stride_axis=0)
            u=nn(flip,moved.astype(jnp.bfloat16)).astype(jnp.bfloat16)
            add=nn(u,hi_ref[...])+nn(u,lo_ref[...])
            table_acc=table_acc+tn(q[off:off+SUB],u)
            if lo_c>0:
                s=jnp.sum(d[:,:lo_c],axis=1,keepdims=True)
                add=add+s*first
                left_acc=left_acc+jnp.sum(s*qf[off:off+SUB],axis=0,keepdims=True)
            if hi_c<SLOT:
                s=jnp.sum(d[:,hi_c:],axis=1,keepdims=True)
                add=add+s*final
                right_acc=right_acc+jnp.sum(s*qf[off:off+SUB],axis=0,keepdims=True)
            extra.append(add)
        dq=((dq+jnp.concatenate(extra,axis=0))*factor).astype(jnp.bfloat16)
        for part in range(0,BLK,rows) if rows<BLK else (0,):
            n=min(rows,BLK)
            j=(base+part)//rows; inner=(base+part)%rows
            d_ref[0,pl.ds(pl.multiple_of((j^who)*rows+inner,n),n),:]=dq[part:part+n]
    dt_ref[0]=table_acc*factor
    ds_ref[0]=jnp.concatenate([left_acc,right_acc,jnp.zeros((6,HEAD),jnp.float32)],axis=0)*factor
    for j in range(SLOT//rows):
        sl=pl.ds(pl.multiple_of((j^who)*rows,rows),rows)
        d_ref[1,sl,:]=(jnp.transpose(dkt[:,j*rows:(j+1)*rows])*factor).astype(jnp.bfloat16)
        d_ref[2,sl,:]=jnp.transpose(dvt[:,j*rows:(j+1)*rows]).astype(jnp.bfloat16)

def attend_back(qkv, grad, probs, who, rel_table, rows):
    heads=qkv.shape[2]//HEAD
    hi,lo=window_table(rel_table)
    spec=lambda m: pl.BlockSpec((1,SLOT,HEAD),lambda h,m=m:(m,0,h))
    smem=pl.BlockSpec(memory_space=pltpu.SMEM)
    tab=pl.BlockSpec((WRAP,HEAD),lambda h:(0,0))
    out=pl.BlockSpec((3,SLOT,HEAD),lambda h:(0,0,h))
    shape=jax.ShapeDtypeStruct((3,SLOT,heads*HEAD),jnp.bfloat16)
    members,dt,ends=pl.pallas_call(
        functools.partial(attend_back_kernel,rows),
        grid=(heads,),
        in_specs=[smem,spec(0),spec(1),spec(2),pl.BlockSpec((SLOT,HEAD),lambda h:(0,h)),pl.BlockSpec((1,SLOT,SLOT),lambda h:(h,0,0)),tab,tab],
        out_specs=[out,pl.BlockSpec((1,HEAD,WRAP),lambda h:(h,0,0)),pl.BlockSpec((1,8,HEAD),lambda h:(h,0,0))],
        out_shape=[shape,jax.ShapeDtypeStruct((heads,HEAD,WRAP),jnp.float32),jax.ShapeDtypeStruct((heads,8,HEAD),jnp.float32)],
        scratch_shapes=[pltpu.VMEM((SLOT,HEAD),jnp.bfloat16)]*4+[pltpu.VMEM((HEAD,SLOT),jnp.float32)]*2,
        compiler_params=pltpu.CompilerParams(vmem_limit_bytes=VMEM_CAP),
        cost_estimate=pl.CostEstimate(flops=1<<20,bytes_accessed=1<<20,transcendentals=0),
        name="attend_back",
    )(who,qkv,qkv,qkv,grad,probs,hi,lo)
    wide=jnp.sum(dt,axis=0).T
    ends=jnp.sum(ends,axis=0)
    near=SUB-LEFT; far=SUB+RIGHT
    left=jnp.sum(wide[:near+1],axis=0)+jnp.sum(wide[WIN+1:],axis=0)+ends[0]
    right=jnp.sum(wide[far:WIN+1],axis=0)+ends[1]
    return members,jnp.concatenate([left[None],wide[near+1:far],right[None]],axis=0)


def run(kernel, outs, ins, after=(), name=None, grid=None, in_specs=None, out_specs=None, scratch=(), aliases=None):
    count = len(ins)
    waits = len(after)

    def body(*refs):
        kernel(*refs[:count], *refs[count + waits :])

    whole = pl.BlockSpec(memory_space=pltpu.VMEM)
    specs = list(in_specs) if in_specs is not None else [whole] * count
    specs = [whole if spec is None else spec for spec in specs]
    out_specs = list(out_specs) if out_specs is not None else [whole] * len(outs)
    extra = {} if grid is None else {"grid": grid}
    return pl.pallas_call(
        body,
        in_specs=specs + [pl.BlockSpec(memory_space=pl.ANY)] * waits,
        out_specs=out_specs,
        out_shape=[jax.ShapeDtypeStruct(shape, dtype) for shape, dtype in outs],
        scratch_shapes=list(scratch),
        input_output_aliases=aliases or {},
        compiler_params=pltpu.CompilerParams(vmem_limit_bytes=VMEM_CAP),
        cost_estimate=pl.CostEstimate(flops=1 << 20, bytes_accessed=1 << 20, transcendentals=0),
        name=name,
        **extra,
    )(*ins, *after)


SMEM_SPEC = pl.BlockSpec(memory_space=pltpu.SMEM)


def moments(rows):
    centred = rows - jnp.mean(rows, axis=1, keepdims=True)
    inverse = lax.rsqrt(jnp.mean(centred * centred, axis=1, keepdims=True) + eps_norm)
    return centred * inverse, inverse


def back(weighted, normed, inverse):
    first_mean = jnp.mean(weighted, axis=1, keepdims=True)
    second_mean = jnp.mean(weighted * normed, axis=1, keepdims=True)
    return inverse * (weighted - first_mean - normed * second_mean)


def wide(ref):
    return ref[...].astype(f32)


def add_up(parts, name, after=()):
    shape = parts[0].shape

    def kernel(*refs):
        total = wide(refs[0])
        for ref in refs[1:-1]:
            total = total + wide(ref)
        refs[-1][...] = total.astype(bf16)

    return run(kernel, [(shape, bf16)], parts, after, name)[0]


def norm_rows(resid, parts, factor, gain, name, after=(), keep=True, low=False, also=None):
    shape = resid.shape
    count = len(parts)
    ins = [resid, gain] + list(parts) + ([also] if also is not None else [])
    outs = [(shape, bf16)] + [(shape, f32)] * keep + [(shape, bf16)] * low
    outs = outs + ([(shape, bf16)] if also is not None else [])

    def kernel(resid_ref, gain_ref, *refs):
        rows = wide(resid_ref)
        if count:
            total = wide(refs[0])
            for ref in refs[1:count]:
                total = total + wide(ref)
            rows = rows + factor * total
        out = list(refs[count + (also is not None) :])
        out.pop(0)[...] = (moments(rows)[0] * gain_ref[...]).astype(bf16)
        if keep:
            out.pop(0)[...] = rows
        if low:
            out.pop(0)[...] = rows.astype(bf16)
        if also is not None:
            out.pop(0)[...] = refs[count][...].astype(bf16)

    return run(kernel, outs, ins, after, name)


def norm_last(resid, parts, gain, upper, begin, length, name, full, after=()):
    shape = resid.shape
    count = len(parts)
    outs = [(shape, bf16)]
    if full:
        outs = outs + [(shape, f32), (shape, f32), ((8, shape[1]), f32)]

    def kernel(begin_ref, length_ref, resid_ref, gain_ref, upper_ref, *refs):
        total = wide(refs[0])
        for ref in refs[1:count]:
            total = total + wide(ref)
        rows = wide(resid_ref) + 0.5 * total
        normed, inverse = moments(rows)
        place = lax.broadcasted_iota(jnp.int32, (shape[0], 1), 0) + begin_ref[0]
        valid = (place < length_ref[0]).astype(f32)
        seen = wide(upper_ref) * valid
        grad = back(seen * gain_ref[...], normed, inverse)
        refs[count][...] = (0.5 * grad).astype(bf16)
        if full:
            refs[count + 1][...] = grad
            refs[count + 2][...] = normed * gain_ref[...] * valid
            refs[count + 3][...] = jnp.broadcast_to(
                jnp.sum(seen * normed, axis=0, keepdims=True), (8, shape[1])
            )

    ins = [begin, length, resid, gain, upper] + list(parts)
    specs = [SMEM_SPEC, SMEM_SPEC] + [None] * (3 + count)
    return run(kernel, outs, ins, after, name, in_specs=specs)


def norm_grad(rows_in, parts, gain, grad, name, after=(), factor=None, keep=True, sums=True):
    shape = rows_in.shape
    count = len(parts)
    outs = [(shape, bf16)] * (factor is not None) + [(shape, f32)] * keep
    outs = outs + [((8, shape[1]), f32)] * sums

    def kernel(rows_ref, gain_ref, grad_ref, *refs):
        total = wide(refs[0])
        for ref in refs[1:count]:
            total = total + wide(ref)
        normed, inverse = moments(wide(rows_ref))
        result = wide(grad_ref) + back(total * gain_ref[...], normed, inverse)
        out = list(refs[count:])
        if factor is not None:
            out.pop(0)[...] = (factor * result).astype(bf16)
        if keep:
            out.pop(0)[...] = result
        if sums:
            out.pop(0)[...] = jnp.broadcast_to(
                jnp.sum(total * normed, axis=0, keepdims=True), (8, shape[1])
            )

    return run(kernel, outs, [rows_in, gain, grad] + list(parts), after, name)


def tile_of(total, most):
    return most if total % most == 0 else total


def feed(own, mate, weights, name, after=()):
    rows, width = own.shape
    hidden = weights.shape[2]
    tile = tile_of(hidden, 256)
    steps = hidden // tile

    def kernel(own_ref, mate_ref, in_ref, out_ref, p_own, p_mate, pre, hid, acc):
        step = pl.program_id(0)
        value = nn(jnp.concatenate([own_ref[...], mate_ref[...]], axis=0), in_ref[0])
        act = (value / (1.0 + jnp.exp(-value))).astype(bf16)
        pre[...] = value.astype(bf16)
        hid[...] = act
        part = nt(act, out_ref[0])

        @pl.when(step == 0)
        def _():
            acc[...] = part

        @pl.when(step > 0)
        def _():
            acc[...] += part

        @pl.when(step == steps - 1)
        def _():
            p_own[...] = acc[:rows].astype(bf16)
            p_mate[...] = acc[rows:].astype(bf16)

    fixed = pl.BlockSpec((rows, width), lambda i: (0, 0))
    cols = pl.BlockSpec((2 * rows, tile), lambda i: (0, i))
    weight = [pl.BlockSpec((1, width, tile), lambda i, m=m: (m, 0, i)) for m in range(2)]
    return run(
        kernel,
        [((rows, width), bf16)] * 2 + [((2 * rows, hidden), bf16)] * 2,
        [own, mate, weights, weights],
        after,
        name,
        grid=(steps,),
        in_specs=[fixed, fixed] + weight,
        out_specs=[fixed, fixed, cols, cols],
        scratch=[pltpu.VMEM((2 * rows, width), f32)],
    )


def feed_grad(own, mate, pre, weights, name, after=()):
    rows, width = own.shape
    hidden = weights.shape[2]
    tile = tile_of(hidden, 256)
    steps = hidden // tile

    def kernel(own_ref, mate_ref, pre_ref, in_ref, out_ref, p_own, p_mate, down, acc):
        step = pl.program_id(0)
        value = nn(jnp.concatenate([own_ref[...], mate_ref[...]], axis=0), out_ref[0])
        preact = wide(pre_ref)
        logistic = 1.0 / (1.0 + jnp.exp(-preact))
        slope = logistic * (1.0 + preact * (1.0 - logistic))
        grad = (value * slope).astype(bf16)
        down[...] = grad
        part = nt(grad, in_ref[0])

        @pl.when(step == 0)
        def _():
            acc[...] = part

        @pl.when(step > 0)
        def _():
            acc[...] += part

        @pl.when(step == steps - 1)
        def _():
            p_own[...] = acc[:rows].astype(bf16)
            p_mate[...] = acc[rows:].astype(bf16)

    fixed = pl.BlockSpec((rows, width), lambda i: (0, 0))
    cols = pl.BlockSpec((2 * rows, tile), lambda i: (0, i))
    weight = [pl.BlockSpec((1, width, tile), lambda i, m=m: (m, 0, i)) for m in range(2)]
    return run(
        kernel,
        [((rows, width), bf16)] * 2 + [((2 * rows, hidden), bf16)],
        [own, mate, pre, weights, weights],
        after,
        name,
        grid=(steps,),
        in_specs=[fixed, fixed, cols] + weight,
        out_specs=[fixed, fixed, cols],
        scratch=[pltpu.VMEM((2 * rows, width), f32)],
    )


def qkv_rows(own, mate, weights, k, total, held, name, after=()):
    rows, width = own.shape
    cols = weights.shape[2]

    def kernel(own_ref, mate_ref, w_ref, *refs):
        value = nn(jnp.concatenate([own_ref[...], mate_ref[...]], axis=0), w_ref[0])
        refs[-1][0] = value.astype(bf16)

    fixed = pl.BlockSpec((rows, width), lambda i: (0, 0))
    ins = [own, mate, weights] + ([held] if held is not None else [])
    specs = [fixed, fixed, pl.BlockSpec((1, width, cols), lambda i: (i, 0, 0))]
    specs = specs + [pl.BlockSpec(memory_space=pl.ANY)] * (held is not None)
    return run(
        kernel,
        [((3, total, cols), bf16)],
        ins,
        after,
        name,
        grid=(3,),
        in_specs=specs,
        out_specs=[pl.BlockSpec((1, 2 * rows, cols), lambda i: (i, k, 0))],
        aliases={3: 0} if held is not None else None,
    )[0]


def heads_rows(own, mate, weight, k, total, held, name, after=()):
    rows, width = own.shape
    cols = weight.shape[1]

    def kernel(own_ref, mate_ref, w_ref, *refs):
        value = nn(jnp.concatenate([own_ref[...], mate_ref[...]], axis=0), w_ref[...])
        refs[-1][...] = value.astype(bf16)

    fixed = pl.BlockSpec((rows, width), lambda i: (0, 0))
    ins = [own, mate, weight] + ([held] if held is not None else [])
    specs = [fixed, fixed, pl.BlockSpec((width, cols), lambda i: (0, 0))]
    specs = specs + [pl.BlockSpec(memory_space=pl.ANY)] * (held is not None)
    return run(
        kernel,
        [((total, cols), bf16)],
        ins,
        after,
        name,
        grid=(1,),
        in_specs=specs,
        out_specs=[pl.BlockSpec((2 * rows, cols), lambda i: (k, 0))],
        aliases={3: 0} if held is not None else None,
    )[0]


def out_rows(values, weight, k, rows, name, after=()):
    width, cols = weight.shape

    def kernel(value_ref, w_ref, p_own, p_mate):
        part = nt(value_ref[...], w_ref[...])
        p_own[...] = part[:rows].astype(bf16)
        p_mate[...] = part[rows:].astype(bf16)

    fixed = pl.BlockSpec((rows, width), lambda i: (0, 0))
    return run(
        kernel,
        [((rows, width), bf16)] * 2,
        [values, weight],
        after,
        name,
        grid=(1,),
        in_specs=[
            pl.BlockSpec((2 * rows, cols), lambda i: (k, 0)),
            pl.BlockSpec((width, cols), lambda i: (0, 0)),
        ],
        out_specs=[fixed, fixed],
    )


def members_rows(members, weights, k, rows, name, after=()):
    width, cols = weights.shape[1:]

    def kernel(value_ref, w_ref, p_own, p_mate):
        part = nt(value_ref[0], w_ref[0])
        for m in range(1, 3):
            part = part + nt(value_ref[m], w_ref[m])
        p_own[...] = part[:rows].astype(bf16)
        p_mate[...] = part[rows:].astype(bf16)

    fixed = pl.BlockSpec((rows, width), lambda i: (0, 0))
    return run(
        kernel,
        [((rows, width), bf16)] * 2,
        [members, weights],
        after,
        name,
        grid=(1,),
        in_specs=[
            pl.BlockSpec((3, 2 * rows, cols), lambda i: (0, k, 0)),
            pl.BlockSpec((3, width, cols), lambda i: (0, 0, 0)),
        ],
        out_specs=[fixed, fixed],
    )


def outer_halves(links, jobs, turn, name, after=()):
    offsets, masks = links.offsets(turn)
    width = jobs[0][0][0].shape[1]
    share = width // links.dp
    me = lax.axis_index("dp").reshape(1).astype(jnp.int32)
    if share % 128:
        whole = jnp.concatenate(
            [
                tn(
                    jnp.concatenate(left),
                    jnp.concatenate([r[0][r[1]] if isinstance(r, tuple) else r for r in right]),
                )
                for left, right in jobs
            ],
            axis=1,
        ).astype(bf16)
        blocks = whole.reshape(links.dp, share, whole.shape[1])

        def pick(which):
            return jnp.concatenate(
                [lax.dynamic_index_in_dim(blocks, me[0] ^ off, 0, keepdims=False) for off in which]
            )

        return pick([off ^ masks[0] for off in offsets]), pick(offsets)
    ins = [me]
    plan = []
    for left, right in jobs:
        picks = [item[1] if isinstance(item, tuple) else None for item in right]
        arrays = [item[0] if isinstance(item, tuple) else item for item in right]
        plan.append((len(left), picks, arrays[0].shape[-1]))
        ins = ins + list(left) + arrays
    total = sum(cols for _, _, cols in plan)
    half = len(offsets)

    def kernel(me_ref, *refs):
        who = me_ref[0]
        sent_ref, kept_ref = refs[-2], refs[-1]
        at, column = 0, 0
        for n_left, picks, cols in plan:
            left = refs[at : at + n_left]
            right = refs[at + n_left : at + n_left + len(picks)]
            at = at + n_left + len(picks)
            rights = [ref[...] if m is None else ref[m] for ref, m in zip(right, picks)]
            rights = rights[0] if len(picks) == 1 else jnp.concatenate(rights, axis=0)
            for flip, dest in ((masks[0], sent_ref), (0, kept_ref)):
                picked = []
                for off in offsets:
                    where = pl.ds(pl.multiple_of((who ^ off ^ flip) * share, 128), share)
                    parts = [ref[:, where] for ref in left]
                    picked.append(parts[0] if n_left == 1 else jnp.concatenate(parts, axis=0))
                picked = picked[0] if half == 1 else jnp.concatenate(picked, axis=1)
                dest[:, column : column + cols] = tn(picked, rights).astype(bf16)
            column = column + cols

    return run(
        kernel,
        [((half * share, total), bf16)] * 2,
        ins,
        after,
        name,
        in_specs=[SMEM_SPEC] + [None] * (len(ins) - 1),
    )


def halve(kept, came, name, after=()):
    count, cols = kept.shape
    half = count // 2

    def kernel(kept_ref, came_ref, sent_out, kept_out):
        total = wide(kept_ref) + wide(came_ref)
        kept_out[...] = total[:half].astype(bf16)
        sent_out[...] = total[half:].astype(bf16)

    return run(kernel, [((half, cols), bf16)] * 2, [kept, came], after, name)


def halves(ref_own, ref_mate, c):
    own, mate = ref_own[...], ref_mate[...]
    first = jnp.where(c == 0, own, mate)
    second = jnp.where(c == 0, mate, own)
    return first, second


def shift_rows(value, offset):
    if offset == 0:
        return value
    return pltpu.roll(value, (-offset) % value.shape[0], 0)


def place_mask(count, y, length):
    place = lax.broadcasted_iota(jnp.int32, (count + 2 * MARGIN, 1), 0) + (y * count - MARGIN)
    return ((place >= 0) & (place < length)).astype(f32)


def bordered(own_ref, mate_ref, before, after, who, ny):
    y, c = who // 2, who % 2
    first, second = halves(own_ref, mate_ref, c)
    above = wide(before[0])
    for ref in before[1:]:
        above = above + wide(ref)
    below = wide(after[0])
    for ref in after[1:]:
        below = below + wide(ref)
    above = jnp.where(y > 0, above, 0.0).astype(bf16)
    below = jnp.where(y < ny - 1, below, 0.0).astype(bf16)
    return jnp.concatenate([above, first, second, below], axis=0)


def conv_mix(ny, who, length, own, mate, before, after_rows, weights, taps, name, after=()):
    rows, width = own.shape
    cols = taps.shape[1]
    count = 2 * rows
    lo, hi = MARGIN, MARGIN + count
    n_before = len(before)

    def kernel(who_ref, len_ref, own_ref, mate_ref, w0, w1, taps_ref, *refs):
        rows_in = bordered(own_ref, mate_ref, refs[:n_before], refs[n_before:-4], who_ref[0], ny)
        lin_ref, gate_ref, mix_ref, tally_ref = refs[-4:]
        valid = place_mask(count, who_ref[0] // 2, len_ref[0])
        linear = nn(rows_in, w0[...])
        gating = 1.0 / (1.0 + jnp.exp(-nn(rows_in, w1[...])))
        lin_ref[...] = linear
        gate_ref[...] = gating
        glu = linear * gating * valid
        mixture = taps_ref[0:1, :] * shift_rows(glu, -2)
        for j in range(1, KERNEL):
            mixture = mixture + taps_ref[j : j + 1, :] * shift_rows(glu, j - 2)
        mix_ref[...] = mixture
        inside = (valid * mixture)[lo:hi]
        tally_ref[...] = jnp.concatenate(
            [
                jnp.sum(inside, axis=0, keepdims=True),
                jnp.sum(inside * mixture[lo:hi], axis=0, keepdims=True),
                jnp.broadcast_to(jnp.sum(valid[lo:hi], axis=0, keepdims=True), (1, cols)),
                jnp.zeros((5, cols), f32),
            ],
            axis=0,
        )

    ins = [who, length, own, mate, weights[0], weights[1], taps] + list(before) + list(after_rows)
    shape = (count + 2 * MARGIN, cols)
    return run(
        kernel,
        [(shape, f32)] * 3 + [((8, cols), f32)],
        ins,
        after,
        name,
        in_specs=[SMEM_SPEC, SMEM_SPEC] + [None] * (len(ins) - 2),
    )


def batch_terms(tally_ref):
    count = tally_ref[2:3, :]
    mean = tally_ref[0:1, :] / count
    var = tally_ref[1:2, :] / count - mean * mean
    return count, mean, var, lax.rsqrt(var + eps_norm)


def conv_out(who, mixture, tallies, affine, running, weight, rows, name, after=()):
    width, cols = weight.shape
    channels = running.shape[1]
    lo, mid, hi = MARGIN, MARGIN + rows, MARGIN + 2 * rows

    def kernel(who_ref, mix_ref, tally_ref, affine_ref, run_ref, w_ref, act_ref, p_own, p_mate, new_ref):
        c = who_ref[0] % 2
        count, mean, var, inverse = batch_terms(tally_ref)
        own = pl.ds(pl.multiple_of(lo + c * rows, 16), rows)
        mate = pl.ds(pl.multiple_of(lo + (1 - c) * rows, 16), rows)
        mixture = jnp.concatenate([mix_ref[own, :], mix_ref[mate, :]], axis=0)
        shifted = (mixture - mean) * inverse * affine_ref[0:1, :] + affine_ref[1:2, :]
        active = (shifted / (1.0 + jnp.exp(-shifted))).astype(bf16)
        act_ref[...] = active
        part = nt(active, w_ref[...])
        p_own[...] = part[:rows].astype(bf16)
        p_mate[...] = part[rows:].astype(bf16)
        grown = var * count / (count - 1.0)
        new_ref[...] = (1.0 - momentum) * run_ref[...] + momentum * jnp.concatenate(
            [mean[:, :channels], grown[:, :channels]], axis=0
        )

    return run(
        kernel,
        [((2 * rows, cols), bf16), ((rows, width), bf16), ((rows, width), bf16), (running.shape, f32)],
        [who, mixture, tallies, affine, running, weight],
        after,
        name,
        in_specs=[SMEM_SPEC] + [None] * 5,
    )


def conv_shift_grad(ny, who, length, own, mate, before, after_rows, mixture, tallies, affine, weight, name, after=()):
    rows, width = own.shape
    cols = weight.shape[1]
    count = 2 * rows
    lo, hi = MARGIN, MARGIN + count
    n_before = len(before)

    def kernel(who_ref, len_ref, own_ref, mate_ref, mix_ref, tally_ref, affine_ref, w_ref, *refs):
        rows_in = bordered(own_ref, mate_ref, refs[:n_before], refs[n_before:-2], who_ref[0], ny)
        dz_ref, out_ref = refs[-2:]
        valid = place_mask(count, who_ref[0] // 2, len_ref[0])
        _, mean, _, inverse = batch_terms(tally_ref)
        centred = (mix_ref[...] - mean) * inverse
        shifted = centred * affine_ref[0:1, :] + affine_ref[1:2, :]
        logistic = 1.0 / (1.0 + jnp.exp(-shifted))
        slope = logistic * (1.0 + shifted * (1.0 - logistic))
        grad = jnp.where(valid > 0.0, nn(rows_in, w_ref[...]) * slope, 0.0)
        dz_ref[...] = grad
        inner = grad[lo:hi]
        out_ref[...] = jnp.concatenate(
            [
                jnp.sum(inner * centred[lo:hi], axis=0, keepdims=True),
                jnp.sum(inner, axis=0, keepdims=True),
                jnp.zeros((6, cols), f32),
            ],
            axis=0,
        )

    ins = [who, length, own, mate, mixture, tallies, affine, weight] + list(before) + list(after_rows)
    return run(
        kernel,
        [(mixture.shape, f32), ((8, cols), f32)],
        ins,
        after,
        name,
        in_specs=[SMEM_SPEC, SMEM_SPEC] + [None] * (len(ins) - 2),
    )


def conv_in_grad(who, length, dz, mixture, tallies, sums, affine, taps, linear, gating, weights, rows, name, after=()):
    width, cols = weights[0].shape
    count = 2 * rows
    lo, mid, hi = MARGIN, MARGIN + rows, MARGIN + count

    def kernel(who_ref, len_ref, dz_ref, mix_ref, tally_ref, sum_ref, affine_ref, taps_ref, lin_ref, gate_ref, w0, w1, dl_ref, dg_ref, p_own, p_mate, tap_ref):
        c = who_ref[0] % 2
        valid = place_mask(count, who_ref[0] // 2, len_ref[0])
        total, mean, _, inverse = batch_terms(tally_ref)
        centred = (mix_ref[...] - mean) * inverse
        shrink = affine_ref[0:1, :] * inverse
        mixed = (sum_ref[1:2, :] + centred * sum_ref[0:1, :]) / total
        grad_mix = jnp.where(valid > 0.0, shrink * (dz_ref[...] - mixed), 0.0)
        grad_glu = taps_ref[0:1, :] * shift_rows(grad_mix, 2)
        for j in range(1, KERNEL):
            grad_glu = grad_glu + taps_ref[j : j + 1, :] * shift_rows(grad_mix, 2 - j)
        linear = lin_ref[...]
        gating = gate_ref[...]
        glu = linear * gating * valid
        inner = grad_mix[lo:hi]
        tap_ref[...] = jnp.concatenate(
            [
                jnp.sum(inner * shift_rows(glu, j - 2)[lo:hi], axis=0, keepdims=True)
                for j in range(KERNEL)
            ]
            + [jnp.zeros((8 - KERNEL, cols), f32)],
            axis=0,
        )
        held = grad_glu * valid * gating
        grad_linear = held.astype(bf16)
        grad_gate = (held * linear * (1.0 - gating)).astype(bf16)

        def turned(value):
            first, second = value[lo:mid], value[mid:hi]
            return jnp.concatenate(
                [jnp.where(c == 0, first, second), jnp.where(c == 0, second, first)], axis=0
            )

        grad_linear = turned(grad_linear)
        grad_gate = turned(grad_gate)
        dl_ref[...] = grad_linear
        dg_ref[...] = grad_gate
        part = nt(grad_linear, w0[...]) + nt(grad_gate, w1[...])
        p_own[...] = part[:rows].astype(bf16)
        p_mate[...] = part[rows:].astype(bf16)

    return run(
        kernel,
        [((count, cols), bf16)] * 2 + [((rows, width), bf16)] * 2 + [((8, cols), f32)],
        [who, length, dz, mixture, tallies, sums, affine, taps, linear, gating, weights[0], weights[1]],
        after,
        name,
        in_specs=[SMEM_SPEC, SMEM_SPEC] + [None] * 10,
    )


class Links:
    def __init__(self, dp, tensor):
        self.dp, self.tensor, self.ny = dp, tensor, tensor // 2
        masks = [1 << bit for bit in range(dp.bit_length() - 1)]
        if len(masks) > 2:
            masks[2] = 6
        self.masks = masks

    def core(self, value):
        return lax.ppermute(value, "tensor", [(i, i ^ 1) for i in range(self.tensor)])

    def chip(self, value, k):
        return lax.ppermute(value, "tensor", [(i, i ^ (2 * k)) for i in range(self.tensor)])

    def group(self, value, mask):
        return lax.ppermute(value, "dp", [(i, i ^ mask) for i in range(self.dp)])

    def sum_group(self, value):
        for mask in self.masks:
            value = value + self.group(value, mask)
        return value

    def sum_stats(self, value, channels):
        def cols(array, k):
            return array[:, k * channels : (k + 1) * channels]

        total = value
        for k in range(1, self.ny):
            other = self.chip(value, k)
            total = total + jnp.concatenate([cols(other, r ^ k) for r in range(self.ny)], axis=1)
        return self.sum_group(total)

    def offsets(self, turn):
        count = len(self.masks)
        masks = [self.masks[(turn + i) % count] for i in range(count)]
        offsets = [0]
        for mask in masks[:0:-1]:
            offsets = offsets + [off ^ mask for off in offsets]
        return offsets, masks

    def borders(self, own, mate):
        count = own.shape[0]
        who = lax.axis_index("tensor")
        y, c = who // 2, who % 2
        if self.ny == 2:
            edge = lax.dynamic_slice_in_dim(own, (1 - y) * (count - MARGIN), MARGIN)
            straight = lax.ppermute(edge, "tensor", [(1, 3), (2, 0)])
            across = lax.ppermute(edge, "tensor", [(1, 2), (2, 1)])
            return [straight, across], [straight, across]
        head = jnp.where(c == 0, own, mate)[:MARGIN]
        foot = jnp.where(c == 0, mate, own)[count - MARGIN :]
        down = [(i, i + 2) for i in range(self.tensor - 2)]
        up = [(i + 2, i) for i in range(self.tensor - 2)]
        return [lax.ppermute(foot, "tensor", down)], [lax.ppermute(head, "tensor", up)]


class Halving:
    def __init__(self, links, halves, turn, name):
        self.links, self.name = links, name
        self.masks = links.offsets(turn)[1]
        self.sent, self.kept = halves
        self.first = self.sent
        self.at = 0
        self.send()

    def send(self):
        self.came = self.links.group(self.sent, self.masks[self.at])
        self.at += 1

    def step(self, after=()):
        if self.at < len(self.masks):
            self.sent, self.kept = halve(self.kept, self.came, self.name + "_half", after)
            self.send()
        return self.kept

    def finish(self):
        while self.at < len(self.masks):
            self.step()
        return self.kept, self.came


def finish_pair(first, second, name, after=()):
    ins = list(first.finish() + second.finish())
    shape = ins[0].shape

    def kernel(a, b, c, d, out):
        out[0] = wide(a) + wide(b)
        out[1] = wide(c) + wide(d)

    return run(kernel, [((2,) + shape, f32)], ins, after, name)[0]


def finish_heads(pending, cols, name, after=()):
    ins = list(pending.finish())
    share = ins[0].shape[0]

    def kernel(a, b, three, one):
        total = wide(a) + wide(b)
        for m in range(3):
            three[m] = total[:, m * cols : (m + 1) * cols]
        one[...] = total[:, 3 * cols :]

    return run(kernel, [((3, share, cols), f32), ((share, cols), f32)], ins, after, name)


def finish_conv(links, pending, channels, name, after=()):
    ins = list(pending.finish())
    share = ins[0].shape[0]
    ny = links.ny

    def split(a, b, own, *others):
        total = wide(a) + wide(b)
        for m in range(3):
            for k in range(ny):
                at = (m * ny + k) * channels
                piece = total[:, at : at + channels]
                if k == 0:
                    own[m] = piece
                else:
                    others[k - 1][m] = piece.astype(bf16)

    shape = (3, share, channels)
    parts = run(split, [(shape, f32)] + [(shape, bf16)] * (ny - 1), ins, after, name)
    came = [links.chip(parts[k], k) for k in range(1, ny)]

    def close(*refs):
        total = refs[0][...]
        for ref in refs[1:-1]:
            total = total + wide(ref)
        refs[-1][...] = total

    return run(close, [(shape, f32)], [parts[0]] + came, (), name + "_close")[0]


def per_device(
    links,
    x_in,
    cotangent,
    lengths,
    norm_gains,
    ffn_first,
    attn_qkv,
    attn_out,
    rel_table,
    conv_proj,
    depthwise,
    bn_gain,
    bn_bias,
    running,
    ffn_second,
):
    ny = links.ny
    others = list(range(1, ny))
    rows, width = x_in.shape
    channels = bn_gain.shape[0]
    who = lax.axis_index("tensor").astype(jnp.int32)
    who_arr = who.reshape(1)
    y, c = who // 2, who % 2
    gain = [norm_gains[i : i + 1] for i in range(5)]
    begin = [(((y ^ k) * 2 + c) * rows).reshape(1) for k in range(ny)]

    me = lax.axis_index("dp")
    share = width // links.dp
    piece = lax.dynamic_slice_in_dim(conv_proj, me * share, share, axis=1)
    conv_w = [[conv_proj[m] for m in range(3)]]
    for k in others:
        blocks = links.chip(piece, k)[None]
        order = [0]
        for mask in links.masks:
            blocks = jnp.concatenate([blocks, links.group(blocks, mask)])
            order = order + [off ^ mask for off in order]
        where = {off: at for at, off in enumerate(order)}
        table = jnp.array([where[off] for off in range(links.dp)], jnp.int32)
        rows_of = [
            lax.dynamic_index_in_dim(blocks, table[me ^ b], 0, keepdims=False)
            for b in range(links.dp)
        ]
        whole = jnp.concatenate(rows_of, axis=1)
        conv_w.append([whole[m] for m in range(3)])
    conv_w = [jnp.concatenate([conv_w[k][m] for k in range(ny)], axis=1) for m in range(3)]
    small = jnp.concatenate([depthwise, bn_gain[None], bn_bias[None], jnp.zeros((1, channels), f32)])
    small = jnp.concatenate([small] + [links.chip(small, k) for k in others], axis=1)
    affine = small[KERNEL : KERNEL + 2]

    def send_sums(parts, name, after=()):
        return add_up([parts[0], links.core(parts[1])], name, after)

    normed, x_low = norm_rows(x_in, [], 0.0, gain[0], "ln_in", keep=False, low=True)
    x_rows = [x_in] + [links.chip(x_low, k) for k in others]
    na_first, kept_first, sums, came = {}, {}, {}, {}
    token = ()
    for k in range(ny):
        if k:
            (normed,) = norm_rows(x_rows[k], [], 0.0, gain[0], "ln_in", token, keep=False)
        na_first[k] = (normed, links.core(normed))
        p_own, p_mate, pre, hid = feed(*na_first[k], ffn_first, "ffn_one")
        kept_first[k] = (pre, hid)
        sums[k] = send_sums((p_own, p_mate), "ffn_one_sum")
        token = (sums[k],)

    def all_parts(sums, k):
        return [sums[k]] + [links.chip(sums[k ^ j], j) for j in others]

    token = ()
    na_attn, first, qkv, cot_low = {}, {}, None, None
    for k in others + [0]:
        also = cotangent if k == 0 else None
        made = norm_rows(
            x_rows[k], all_parts(sums, k), 0.5, gain[1], "ln_attn", token, also=also
        )
        na_attn[k] = (made[0], links.core(made[0]))
        first[k] = made[1]
        if k == 0:
            cot_low = made[2]
        qkv = qkv_rows(*na_attn[k], attn_qkv, k, SLOT, qkv, "qkv")
        token = (qkv,)
    cot_rows = [cotangent] + [links.chip(cot_low, k) for k in others]
    heads_out, probs = attend(qkv, who_arr, lengths, rel_table, rows)
    token = ()
    arrived = []
    for k in others:
        total = send_sums(out_rows(heads_out, attn_out, k, rows, "out_proj", token), "out_sum")
        arrived.append(links.chip(total, k))
        token = (total,)
    p_own, p_mate = out_rows(heads_out, attn_out, 0, rows, "out_proj", token)
    conv_own, after_attn = norm_rows(
        first[0], [p_own, links.core(p_mate)] + arrived, 1.0, gain[2], "ln_conv"
    )

    conv_mate = links.core(conv_own)
    before, after_rows = links.borders(conv_own, conv_mate)
    linear, gating, mixture, tallies = conv_mix(
        ny, who_arr, lengths, conv_own, conv_mate, before, after_rows, conv_w, small[:KERNEL], "conv_mix"
    )
    tallies = links.sum_stats(tallies, channels)
    active, p_own, p_mate, updated = conv_out(
        who_arr, mixture, tallies, affine, running, conv_w[2], rows, "conv_out"
    )
    normed, after_conv, low = norm_rows(
        after_attn, [p_own, links.core(p_mate)], 1.0, gain[3], "ln_ffn_two", low=True
    )

    x_rows = [after_conv] + [links.chip(low, k) for k in others]
    na_last, kept_last, sums = {}, {}, {}
    token = ()
    for k in range(ny):
        if k:
            (normed,) = norm_rows(x_rows[k], [], 0.0, gain[3], "ln_ffn_two", token, keep=False)
        na_last[k] = (normed, links.core(normed))
        p_own, p_mate, pre, hid = feed(*na_last[k], ffn_second, "ffn_two")
        kept_last[k] = (pre, hid)
        sums[k] = send_sums((p_own, p_mate), "ffn_two_sum")
        token = (sums[k],)

    token = ()
    upper, down, arrived = {}, {}, []
    for k in others + [0]:
        made = norm_last(
            x_rows[k],
            all_parts(sums, k),
            gain[4],
            cot_rows[k],
            begin[k],
            lengths,
            "ln_last",
            k == 0,
            token,
        )
        upper[k] = (made[0], links.core(made[0]))
        p_own, p_mate, down[k] = feed_grad(*upper[k], kept_last[k][0], ffn_second, "ffn_two_grad")
        if k:
            total = send_sums((p_own, p_mate), "ffn_two_grad_sum")
            arrived.append(links.chip(total, k))
            token = (total,)
        else:
            grad, output, gain_five = made[1:]
            parts = [p_own, links.core(p_mate)]

    def row_blocks(pairs):
        return [block for k in range(ny) for block in pairs[k]]

    wait_out = outer_halves(
        links, [(row_blocks(upper), [kept_last[k][1] for k in range(ny)])], 0, "ffn_two_out", (p_mate,)
    )
    wait_in = outer_halves(
        links, [(row_blocks(na_last), [down[k] for k in range(ny)])], 1, "ffn_two_in", (p_mate,)
    )
    low, grad, gain_four = norm_grad(
        after_conv, parts + arrived, gain[3], grad, "back_ffn_two", (wait_out[0], wait_in[0]), factor=1.0
    )

    up_own = low
    up_mate = links.core(low)
    before, after_rows = links.borders(up_own, up_mate)
    dz, sums = conv_shift_grad(
        ny, who_arr, lengths, up_own, up_mate, before, after_rows, mixture, tallies, affine, conv_w[2], "conv_dz"
    )
    bn_grads = links.sum_stats(sums, channels)
    grad_linear, grad_gate, p_own, p_mate, tap_grad = conv_in_grad(
        who_arr, lengths, dz, mixture, tallies, bn_grads, affine, small[:KERNEL], linear, gating, conv_w, rows, "conv_din"
    )
    low, grad, gain_three = norm_grad(
        after_attn, [p_own, links.core(p_mate)], gain[2], grad, "back_conv", factor=1.0
    )

    pend_two_out = Halving(links, wait_out, 0, "ffn_two_out")
    pend_two_in = Halving(links, wait_in, 1, "ffn_two_in")

    g_rows = [low] + [links.chip(low, k) for k in others]
    conv_halves = outer_halves(
        links,
        [
            ([conv_own, conv_mate], [grad_linear]),
            ([conv_own, conv_mate], [grad_gate]),
            ([up_own, up_mate], [active]),
        ],
        2,
        "conv_w",
        (low,),
    )
    pend_conv = Halving(links, conv_halves, 2, "conv_w")
    grad_heads = None
    upper_attn = {}
    for k in range(ny):
        upper_attn[k] = (g_rows[k], links.core(g_rows[k]))
        grad_heads = heads_rows(*upper_attn[k], attn_out, k, SLOT, grad_heads, "dheads")
    members, table_grad = attend_back(qkv, grad_heads, probs, who_arr, rel_table, rows)
    token = ()
    sums = {}
    for k in range(ny):
        sums[k] = send_sums(members_rows(members, attn_qkv, k, rows, "dqkv", token), "dqkv_sum")
        token = (sums[k],)
    heads_halves = outer_halves(
        links,
        [(row_blocks(na_attn), [(members, m)]) for m in range(3)]
        + [(row_blocks(upper_attn), [heads_out])],
        0,
        "attn_w",
        token,
    )
    pend_heads = Halving(links, heads_halves, 0, "attn_w")

    token = (heads_halves[0],)
    upper, down, arrived = {}, {}, []
    for k in others + [0]:
        made = norm_grad(
            first[k],
            all_parts(sums, k),
            gain[1],
            grad if k == 0 else g_rows[k],
            "back_attn",
            token,
            factor=0.5,
            keep=k == 0,
            sums=k == 0,
        )
        upper[k] = (made[0], links.core(made[0]))
        p_own, p_mate, down[k] = feed_grad(*upper[k], kept_first[k][0], ffn_first, "ffn_one_grad")
        if k:
            total = send_sums((p_own, p_mate), "ffn_one_grad_sum")
            arrived.append(links.chip(total, k))
            token = (total,)
        else:
            grad, gain_two = made[1:]
            parts = [p_own, links.core(p_mate)]
    halves_in = outer_halves(
        links, [(row_blocks(na_first), [down[k] for k in range(ny)])], 1, "ffn_one_in", (p_mate,)
    )
    pend_one_in = Halving(links, halves_in, 1, "ffn_one_in")
    halves_out = outer_halves(
        links,
        [(row_blocks(upper), [kept_first[k][1] for k in range(ny)])],
        2,
        "ffn_one_out",
        (halves_in[0],),
    )
    pend_one_out = Halving(links, halves_out, 2, "ffn_one_out")
    grad_input, gain_one = norm_grad(
        x_in, parts + arrived, gain[0], grad, "back_ffn_one", (halves_out[0],)
    )

    last_sum = finish_pair(pend_two_in, pend_two_out, "ffn_two_end")
    conv_sum = finish_conv(links, pend_conv, channels, "conv_end")
    qkv_sum, out_sum = finish_heads(pend_heads, attn_qkv.shape[2], "attn_end")
    first_sum = finish_pair(pend_one_in, pend_one_out, "ffn_one_end")

    kernel_grad = links.sum_stats(tap_grad, channels)[:KERNEL, :channels]
    gains = [gain_one, gain_two, gain_three, gain_four, gain_five]
    gains = jnp.stack([part[0] for part in gains]).reshape(-1, HEAD)
    bundle = jnp.concatenate([gains, table_grad])
    bundle = jnp.pad(bundle, ((0, -bundle.shape[0] % 8), (0, 0)))
    bundle = bundle + links.core(bundle)
    for k in [1 << bit for bit in range(ny.bit_length() - 1)]:
        bundle = bundle + links.chip(bundle, k)
    bundle = links.sum_group(bundle)
    return (
        output,
        grad_input,
        bundle[: gains.shape[0]].reshape(5, width),
        first_sum,
        qkv_sum,
        out_sum,
        bundle[gains.shape[0] : gains.shape[0] + REL],
        conv_sum,
        kernel_grad,
        bn_grads[0, :channels],
        bn_grads[1, :channels],
        updated,
        last_sum,
    )


def solution(mesh):
    links = Links(mesh.shape["dp"], mesh.shape["tensor"])
    placed = (
        P(("dp", "tensor"), None),
        P(("dp", "tensor"), None),
        P("dp"),
        P(),
        P(None, None, "tensor"),
        P(None, None, "tensor"),
        P(None, "tensor"),
        P(),
        P(None, None, "tensor"),
        P(None, "tensor"),
        P("tensor"),
        P("tensor"),
        P(None, "tensor"),
        P(None, None, "tensor"),
    )
    return jax.shard_map(
        functools.partial(per_device, links),
        mesh=mesh,
        in_specs=placed,
        out_specs=(
            P(("dp", "tensor"), None),
            P(("dp", "tensor"), None),
            P(),
            P(None, "dp", "tensor"),
            P(None, "dp", "tensor"),
            P("dp", "tensor"),
            P(),
            P(None, "dp", "tensor"),
            P(None, "tensor"),
            P("tensor"),
            P("tensor"),
            P(None, "tensor"),
            P(None, "dp", "tensor"),
        ),
        check_vma=False,
    )
```

```python
import functools

import jax
import jax.numpy as jnp
from jax import lax
from jax.experimental import pallas as pl
from jax.experimental.pallas import tpu as pltpu
from jax.sharding import PartitionSpec as P

HEAD = 128
KERNEL = 5
LEFT = 64
RIGHT = 8
SLOT = 1024
REL = 73
MARGIN = 16
SUB = 128
BLK = 256
WIN = 3 * SUB
WRAP = 512
LOG2E = 1.4426950408889634
VMEM_CAP = 32 * 1024 * 1024

eps_norm = 1e-05
momentum = 0.5
bf16 = jnp.bfloat16
f32 = jnp.float32


def nn(left_op, right_op):
    return lax.dot_general(
        left_op, right_op, (((1,), (0,)), ((), ())), preferred_element_type=f32
    )


def nt(left_op, right_op):
    return lax.dot_general(
        left_op, right_op, (((1,), (1,)), ((), ())), preferred_element_type=f32
    )


def tn(left_op, right_op):
    return lax.dot_general(
        left_op, right_op, (((0,), (0,)), ((), ())), preferred_element_type=f32
    )


def window_table(rel_table):
    near,far=SUB-LEFT,SUB+RIGHT
    width=rel_table.shape[1]
    ext=jnp.concatenate([
        jnp.broadcast_to(rel_table[:1],(near,width)),
        rel_table,
        jnp.broadcast_to(rel_table[REL-1:],(WIN-far,width)),
        jnp.broadcast_to(rel_table[:1],(WRAP-WIN-1,width)),
    ])
    hi=ext.astype(jnp.bfloat16)
    lo=(ext-hi.astype(jnp.float32)).astype(jnp.bfloat16)
    return hi,lo

def order_in(dst, src, who, rows):
    for j in range(SLOT//rows):
        dst[j*rows:(j+1)*rows,:]=src[pl.ds(pl.multiple_of((j^who)*rows,rows),rows),:]

def attend_kernel(rows, who_ref, len_ref, q_ref, k_ref, v_ref, hi_ref, lo_ref, o_ref, p_ref, qs, ks, vs):
    who=who_ref[0]
    length=len_ref[0]
    order_in(qs,q_ref.at[0],who,rows); order_in(ks,k_ref.at[0],who,rows); order_in(vs,v_ref.at[0],who,rows)
    factor=HEAD**(-0.5)*LOG2E
    tail=lax.broadcasted_iota(jnp.int32,(SUB,SLOT//2),1)+SLOT//2<length
    for base in range(0,SLOT,BLK):
        q=qs[base:base+BLK,:]
        content=nt(q,ks[...])
        spread=nt(q,hi_ref[...])+nt(q,lo_ref[...])
        for off in range(0,BLK,SUB):
            i0=base+off
            e=spread[off:off+SUB]
            rolled=pltpu.roll(e,0,1,stride=1,stride_axis=0)
            lo_c=max(i0-SUB,0); hi_c=min(i0+2*SUB,SLOT)
            parts=[]
            if lo_c>0: parts.append(content[off:off+SUB,:lo_c]+e[:,0:1])
            parts.append(content[off:off+SUB,lo_c:hi_c]+rolled[:,lo_c-(i0-SUB):hi_c-(i0-SUB)])
            if hi_c<SLOT: parts.append(content[off:off+SUB,hi_c:]+e[:,WIN-1:WIN])
            logit=jnp.concatenate(parts,axis=1)*factor
            logit=jnp.concatenate([logit[:,:SLOT//2],jnp.where(tail,logit[:,SLOT//2:],-1e30)],axis=1)
            peak=jnp.max(logit,axis=1,keepdims=True)
            ex=jnp.exp2(logit-peak)
            tot=jnp.sum(ex,axis=1,keepdims=True)
            p_ref[0,i0:i0+SUB,:]=(ex*(1.0/tot)).astype(jnp.bfloat16)
        out=nn(p_ref[0,base:base+BLK,:],vs[...]).astype(jnp.bfloat16)
        for part in range(0,BLK,rows) if rows<BLK else (0,):
            n=min(rows,BLK)
            j=(base+part)//rows; inner=(base+part)%rows
            o_ref[pl.ds(pl.multiple_of((j^who)*rows+inner,n),n),:]=out[part:part+n]

def attend(qkv, who, length, rel_table, rows):
    heads=qkv.shape[2]//HEAD
    hi,lo=window_table(rel_table)
    spec=lambda m: pl.BlockSpec((1,SLOT,HEAD),lambda h,m=m:(m,0,h))
    smem=pl.BlockSpec(memory_space=pltpu.SMEM)
    tab=pl.BlockSpec((WRAP,HEAD),lambda h:(0,0))
    return pl.pallas_call(
        functools.partial(attend_kernel,rows),
        grid=(heads,),
        in_specs=[smem,smem,spec(0),spec(1),spec(2),tab,tab],
        out_specs=[pl.BlockSpec((SLOT,HEAD),lambda h:(0,h)),pl.BlockSpec((1,SLOT,SLOT),lambda h:(h,0,0))],
        out_shape=[jax.ShapeDtypeStruct((SLOT,heads*HEAD),jnp.bfloat16),jax.ShapeDtypeStruct((heads,SLOT,SLOT),jnp.bfloat16)],
        scratch_shapes=[pltpu.VMEM((SLOT,HEAD),jnp.bfloat16)]*3,
        compiler_params=pltpu.CompilerParams(vmem_limit_bytes=28<<20),
        cost_estimate=pl.CostEstimate(flops=int(heads*32*SLOT*SLOT*HEAD*WORK),bytes_accessed=1<<20,transcendentals=0),
        name="attend",
    )(who,length,qkv,qkv,qkv,hi,lo)

def attend_back_kernel(rows, who_ref, q_ref, k_ref, v_ref, g_ref, p_ref, hi_ref, lo_ref, d_ref, dt_ref, ds_ref, qs, ks, vs, gs, dkt, dvt):
    who=who_ref[0]
    for dst,src in ((qs,q_ref.at[0]),(ks,k_ref.at[0]),(vs,v_ref.at[0]),(gs,g_ref)):
        order_in(dst,src,who,rows)
    factor=HEAD**(-0.5)
    first=hi_ref[0:1,:].astype(jnp.float32)+lo_ref[0:1,:].astype(jnp.float32)
    final=hi_ref[WIN-1:WIN,:].astype(jnp.float32)+lo_ref[WIN-1:WIN,:].astype(jnp.float32)
    zero=jnp.zeros((SUB,SUB),jnp.float32)
    flip=(lax.broadcasted_iota(jnp.int32,(SUB,SUB),0)+lax.broadcasted_iota(jnp.int32,(SUB,SUB),1)==SUB-1).astype(jnp.bfloat16)
    table_acc=jnp.zeros((HEAD,WRAP),jnp.float32)
    left_acc=jnp.zeros((1,HEAD),jnp.float32)
    right_acc=jnp.zeros((1,HEAD),jnp.float32)
    for base in range(0,SLOT,BLK):
        q=qs[base:base+BLK,:]
        g=gs[base:base+BLK,:]
        pb=p_ref[0,base:base+BLK,:]
        p=pb.astype(jnp.float32)
        dp=nt(g,vs[...])
        delta=jnp.sum(p*dp,axis=1,keepdims=True)
        dsb=(p*(dp-delta)).astype(jnp.bfloat16)
        dv_part=tn(g,pb)
        dk_part=tn(q,dsb)
        if base==0:
            dvt[...]=dv_part; dkt[...]=dk_part
        else:
            dvt[...]+=dv_part; dkt[...]+=dk_part
        dq=nn(dsb,ks[...])
        ds=dsb.astype(jnp.float32)
        qf=q.astype(jnp.float32)
        extra=[]
        for off in range(0,BLK,SUB):
            i0=base+off
            d=ds[off:off+SUB]
            lo_c=max(i0-SUB,0); hi_c=min(i0+2*SUB,SLOT)
            turned=nn(flip,dsb[off:off+SUB,lo_c:hi_c])
            win=[zero]*((lo_c-(i0-SUB))//SUB)+[turned]+[zero]*((i0+2*SUB-hi_c)//SUB+1)
            moved=pltpu.roll(jnp.concatenate(win,axis=1),WRAP-SUB+1,1,stride=1,stride_axis=0)
            u=nn(flip,moved.astype(jnp.bfloat16)).astype(jnp.bfloat16)
            add=nn(u,hi_ref[...])+nn(u,lo_ref[...])
            table_acc=table_acc+tn(q[off:off+SUB],u)
            if lo_c>0:
                s=jnp.sum(d[:,:lo_c],axis=1,keepdims=True)
                add=add+s*first
                left_acc=left_acc+jnp.sum(s*qf[off:off+SUB],axis=0,keepdims=True)
            if hi_c<SLOT:
                s=jnp.sum(d[:,hi_c:],axis=1,keepdims=True)
                add=add+s*final
                right_acc=right_acc+jnp.sum(s*qf[off:off+SUB],axis=0,keepdims=True)
            extra.append(add)
        dq=((dq+jnp.concatenate(extra,axis=0))*factor).astype(jnp.bfloat16)
        for part in range(0,BLK,rows) if rows<BLK else (0,):
            n=min(rows,BLK)
            j=(base+part)//rows; inner=(base+part)%rows
            d_ref[0,pl.ds(pl.multiple_of((j^who)*rows+inner,n),n),:]=dq[part:part+n]
    dt_ref[0]=table_acc*factor
    ds_ref[0]=jnp.concatenate([left_acc,right_acc,jnp.zeros((6,HEAD),jnp.float32)],axis=0)*factor
    for j in range(SLOT//rows):
        sl=pl.ds(pl.multiple_of((j^who)*rows,rows),rows)
        d_ref[1,sl,:]=(jnp.transpose(dkt[:,j*rows:(j+1)*rows])*factor).astype(jnp.bfloat16)
        d_ref[2,sl,:]=jnp.transpose(dvt[:,j*rows:(j+1)*rows]).astype(jnp.bfloat16)

def attend_back(qkv, grad, probs, who, rel_table, rows):
    heads=qkv.shape[2]//HEAD
    hi,lo=window_table(rel_table)
    spec=lambda m: pl.BlockSpec((1,SLOT,HEAD),lambda h,m=m:(m,0,h))
    smem=pl.BlockSpec(memory_space=pltpu.SMEM)
    tab=pl.BlockSpec((WRAP,HEAD),lambda h:(0,0))
    out=pl.BlockSpec((3,SLOT,HEAD),lambda h:(0,0,h))
    shape=jax.ShapeDtypeStruct((3,SLOT,heads*HEAD),jnp.bfloat16)
    members,dt,ends=pl.pallas_call(
        functools.partial(attend_back_kernel,rows),
        grid=(heads,),
        in_specs=[smem,spec(0),spec(1),spec(2),pl.BlockSpec((SLOT,HEAD),lambda h:(0,h)),pl.BlockSpec((1,SLOT,SLOT),lambda h:(h,0,0)),tab,tab],
        out_specs=[out,pl.BlockSpec((1,HEAD,WRAP),lambda h:(h,0,0)),pl.BlockSpec((1,8,HEAD),lambda h:(h,0,0))],
        out_shape=[shape,jax.ShapeDtypeStruct((heads,HEAD,WRAP),jnp.float32),jax.ShapeDtypeStruct((heads,8,HEAD),jnp.float32)],
        scratch_shapes=[pltpu.VMEM((SLOT,HEAD),jnp.bfloat16)]*4+[pltpu.VMEM((HEAD,SLOT),jnp.float32)]*2,
        compiler_params=pltpu.CompilerParams(vmem_limit_bytes=28<<20),
        cost_estimate=pl.CostEstimate(flops=int(heads*50*SLOT*SLOT*HEAD*WORK),bytes_accessed=1<<20,transcendentals=0),
        name="attend_back",
    )(who,qkv,qkv,qkv,grad,probs,hi,lo)
    wide=jnp.sum(dt,axis=0).T
    ends=jnp.sum(ends,axis=0)
    near=SUB-LEFT; far=SUB+RIGHT
    left=jnp.sum(wide[:near+1],axis=0)+jnp.sum(wide[WIN+1:],axis=0)+ends[0]
    right=jnp.sum(wide[far:WIN+1],axis=0)+ends[1]
    return members,jnp.concatenate([left[None],wide[near+1:far],right[None]],axis=0)


WORK = 3.0


class Stack:
    def __init__(self, refs):
        self.refs = refs

    def __getitem__(self, index):
        return jnp.concatenate([ref[index] for ref in self.refs], axis=0)


def run(
    kernel,
    outs,
    ins,
    after=(),
    name=None,
    grid=None,
    in_specs=None,
    out_specs=None,
    scratch=(),
    aliases=None,
    room=24,
    work=1 << 20,
):
    waits = len(after)
    sizes = [len(item) if isinstance(item, list) else 0 for item in ins]

    def body(*refs):
        args, at = [], 0
        for size in sizes:
            args.append(Stack(refs[at : at + size]) if size else refs[at])
            at += max(size, 1)
        kernel(*args, *refs[at + waits :])

    def full(shape):
        return pl.BlockSpec(tuple(shape), lambda i: (0,) * len(shape))

    if grid is None:
        grid = (1,)
    given = list(in_specs) if in_specs is not None else [None] * len(ins)
    specs, flat, start = [], [], []
    for item, spec, size in zip(ins, given, sizes):
        start.append(len(flat))
        if spec is None:
            spec = full((item[0] if size else item).shape)
        elif size:
            shape = spec.block_shape
            spec = pl.BlockSpec((shape[0] // size,) + tuple(shape[1:]), spec.index_map)
        specs += [spec] * max(size, 1)
        flat += item if size else [item]
    ins = flat
    out_specs = list(out_specs) if out_specs is not None else [full(s) for s, _ in outs]
    return pl.pallas_call(
        body,
        in_specs=specs + [pl.BlockSpec(memory_space=pl.ANY)] * waits,
        out_specs=out_specs,
        out_shape=[jax.ShapeDtypeStruct(shape, dtype) for shape, dtype in outs],
        scratch_shapes=list(scratch),
        input_output_aliases={start[i]: o for i, o in (aliases or {}).items()},
        compiler_params=pltpu.CompilerParams(vmem_limit_bytes=room << 20),
        cost_estimate=pl.CostEstimate(flops=int(work * WORK), bytes_accessed=1 << 20, transcendentals=0),
        name=name,
        grid=grid,
    )(*ins, *after)


SMEM_SPEC = pl.BlockSpec(memory_space=pltpu.SMEM)


def moments(rows):
    centred = rows - jnp.mean(rows, axis=1, keepdims=True)
    inverse = lax.rsqrt(jnp.mean(centred * centred, axis=1, keepdims=True) + eps_norm)
    return centred * inverse, inverse


def back(weighted, normed, inverse):
    first_mean = jnp.mean(weighted, axis=1, keepdims=True)
    second_mean = jnp.mean(weighted * normed, axis=1, keepdims=True)
    return inverse * (weighted - first_mean - normed * second_mean)


def wide(ref):
    return ref[...].astype(f32)


def add_up(parts, name, after=()):
    shape = parts[0].shape

    def kernel(*refs):
        total = wide(refs[0])
        for ref in refs[1:-1]:
            total = total + wide(ref)
        refs[-1][...] = total.astype(bf16)

    return run(kernel, [(shape, bf16)], parts, after, name)[0]


def norm_rows(resid, parts, factor, gain, name, after=(), keep=True, low=False, also=None):
    shape = resid.shape
    count = len(parts)
    ins = [resid, gain] + list(parts) + ([also] if also is not None else [])
    outs = [(shape, bf16)] + [(shape, f32)] * keep + [(shape, bf16)] * low
    outs = outs + ([(shape, bf16)] if also is not None else [])

    def kernel(resid_ref, gain_ref, *refs):
        rows = wide(resid_ref)
        if count:
            total = wide(refs[0])
            for ref in refs[1:count]:
                total = total + wide(ref)
            rows = rows + factor * total
        out = list(refs[count + (also is not None) :])
        out.pop(0)[...] = (moments(rows)[0] * gain_ref[...]).astype(bf16)
        if keep:
            out.pop(0)[...] = rows
        if low:
            out.pop(0)[...] = rows.astype(bf16)
        if also is not None:
            out.pop(0)[...] = refs[count][...].astype(bf16)

    return run(kernel, outs, ins, after, name)


def norm_last(resid, parts, gain, upper, begin, length, name, full, after=()):
    shape = resid.shape
    count = len(parts)
    outs = [(shape, bf16)]
    if full:
        outs = outs + [(shape, f32), (shape, f32), ((8, shape[1]), f32)]

    def kernel(begin_ref, length_ref, resid_ref, gain_ref, upper_ref, *refs):
        total = wide(refs[0])
        for ref in refs[1:count]:
            total = total + wide(ref)
        rows = wide(resid_ref) + 0.5 * total
        normed, inverse = moments(rows)
        place = lax.broadcasted_iota(jnp.int32, (shape[0], 1), 0) + begin_ref[0]
        valid = (place < length_ref[0]).astype(f32)
        seen = wide(upper_ref) * valid
        grad = back(seen * gain_ref[...], normed, inverse)
        refs[count][...] = (0.5 * grad).astype(bf16)
        if full:
            refs[count + 1][...] = grad
            refs[count + 2][...] = normed * gain_ref[...] * valid
            refs[count + 3][...] = jnp.broadcast_to(
                jnp.sum(seen * normed, axis=0, keepdims=True), (8, shape[1])
            )

    ins = [begin, length, resid, gain, upper] + list(parts)
    specs = [SMEM_SPEC, SMEM_SPEC] + [None] * (3 + count)
    return run(kernel, outs, ins, after, name, in_specs=specs)


def norm_grad(rows_in, parts, gain, grad, name, after=(), factor=None, keep=True, sums=True):
    shape = rows_in.shape
    count = len(parts)
    outs = [(shape, bf16)] * (factor is not None) + [(shape, f32)] * keep
    outs = outs + [((8, shape[1]), f32)] * sums

    def kernel(rows_ref, gain_ref, grad_ref, *refs):
        total = wide(refs[0])
        for ref in refs[1:count]:
            total = total + wide(ref)
        normed, inverse = moments(wide(rows_ref))
        result = wide(grad_ref) + back(total * gain_ref[...], normed, inverse)
        out = list(refs[count:])
        if factor is not None:
            out.pop(0)[...] = (factor * result).astype(bf16)
        if keep:
            out.pop(0)[...] = result
        if sums:
            out.pop(0)[...] = jnp.broadcast_to(
                jnp.sum(total * normed, axis=0, keepdims=True), (8, shape[1])
            )

    return run(kernel, outs, [rows_in, gain, grad] + list(parts), after, name)


def tile_of(total, most):
    return most if total % most == 0 else total


def feed(own, mate, weights, name, after=()):
    rows, width = own.shape
    hidden = weights.shape[2]
    tile = tile_of(hidden, 1024)
    steps = hidden // tile

    def kernel(own_ref, mate_ref, in_ref, out_ref, p_own, p_mate, pre, hid, seen, acc=None):
        step = pl.program_id(0)
        both = jnp.concatenate([own_ref[...], mate_ref[...]], axis=0)
        seen[...] = both
        value = nn(both, in_ref[0])
        act = (value / (1.0 + jnp.exp(-value))).astype(bf16)
        pre[...] = value.astype(bf16)
        hid[...] = act
        part = nt(act, out_ref[0])
        if steps == 1:
            p_own[...] = part[:rows].astype(bf16)
            p_mate[...] = part[rows:].astype(bf16)
            return

        @pl.when(step == 0)
        def _():
            acc[...] = part

        @pl.when(step > 0)
        def _():
            acc[...] += part

        @pl.when(step == steps - 1)
        def _():
            p_own[...] = acc[:rows].astype(bf16)
            p_mate[...] = acc[rows:].astype(bf16)

    fixed = pl.BlockSpec((rows, width), lambda i: (0, 0))
    cols = pl.BlockSpec((2 * rows, tile), lambda i: (0, i))
    weight = [pl.BlockSpec((1, width, tile), lambda i, m=m: (m, 0, i)) for m in range(2)]
    return run(
        kernel,
        [((rows, width), bf16)] * 2 + [((2 * rows, hidden), bf16)] * 2 + [((2 * rows, width), bf16)],
        [own, mate, weights, weights],
        after,
        name,
        grid=(steps,),
        in_specs=[fixed, fixed] + weight,
        out_specs=[fixed, fixed, cols, cols, pl.BlockSpec((2 * rows, width), lambda i: (0, 0))],
        scratch=[pltpu.VMEM((2 * rows, width), f32)] if steps > 1 else (),
        room=28,
        work=8 * rows * width * hidden,
    )


def feed_grad(own, mate, pre, weights, name, after=()):
    rows, width = own.shape
    hidden = weights.shape[2]
    tile = tile_of(hidden, 1024)
    steps = hidden // tile

    def kernel(own_ref, mate_ref, pre_ref, in_ref, out_ref, p_own, p_mate, down, seen, acc=None):
        step = pl.program_id(0)
        both = jnp.concatenate([own_ref[...], mate_ref[...]], axis=0)
        seen[...] = both
        value = nn(both, out_ref[0])
        preact = wide(pre_ref)
        logistic = 1.0 / (1.0 + jnp.exp(-preact))
        slope = logistic * (1.0 + preact * (1.0 - logistic))
        grad = (value * slope).astype(bf16)
        down[...] = grad
        part = nt(grad, in_ref[0])
        if steps == 1:
            p_own[...] = part[:rows].astype(bf16)
            p_mate[...] = part[rows:].astype(bf16)
            return

        @pl.when(step == 0)
        def _():
            acc[...] = part

        @pl.when(step > 0)
        def _():
            acc[...] += part

        @pl.when(step == steps - 1)
        def _():
            p_own[...] = acc[:rows].astype(bf16)
            p_mate[...] = acc[rows:].astype(bf16)

    fixed = pl.BlockSpec((rows, width), lambda i: (0, 0))
    cols = pl.BlockSpec((2 * rows, tile), lambda i: (0, i))
    weight = [pl.BlockSpec((1, width, tile), lambda i, m=m: (m, 0, i)) for m in range(2)]
    return run(
        kernel,
        [((rows, width), bf16)] * 2 + [((2 * rows, hidden), bf16), ((2 * rows, width), bf16)],
        [own, mate, pre, weights, weights],
        after,
        name,
        grid=(steps,),
        in_specs=[fixed, fixed, cols] + weight,
        out_specs=[fixed, fixed, cols, pl.BlockSpec((2 * rows, width), lambda i: (0, 0))],
        scratch=[pltpu.VMEM((2 * rows, width), f32)] if steps > 1 else (),
        room=28,
        work=8 * rows * width * hidden,
    )


def qkv_rows(own, mate, weights, k, total, held, name, after=()):
    rows, width = own.shape
    cols = weights.shape[2]

    def kernel(own_ref, mate_ref, w_ref, *refs):
        both = jnp.concatenate([own_ref[...], mate_ref[...]], axis=0)
        refs[-1][...] = both
        refs[-2][0] = nn(both, w_ref[0]).astype(bf16)

    fixed = pl.BlockSpec((rows, width), lambda i: (0, 0))
    ins = [own, mate, weights] + ([held] if held is not None else [])
    specs = [fixed, fixed, pl.BlockSpec((1, width, cols), lambda i: (i, 0, 0))]
    specs = specs + [pl.BlockSpec(memory_space=pl.ANY)] * (held is not None)
    return run(
        kernel,
        [((3, total, cols), bf16), ((2 * rows, width), bf16)],
        ins,
        after,
        name,
        grid=(3,),
        in_specs=specs,
        out_specs=[
            pl.BlockSpec((1, 2 * rows, cols), lambda i: (i, k, 0)),
            pl.BlockSpec((2 * rows, width), lambda i: (0, 0)),
        ],
        work=12 * rows * width * cols,
        aliases={3: 0} if held is not None else None,
    )


def heads_rows(own, mate, weight, k, total, held, name, after=()):
    rows, width = own.shape
    cols = weight.shape[1]

    def kernel(own_ref, mate_ref, w_ref, *refs):
        both = jnp.concatenate([own_ref[...], mate_ref[...]], axis=0)
        refs[-1][...] = both
        refs[-2][...] = nn(both, w_ref[...]).astype(bf16)

    fixed = pl.BlockSpec((rows, width), lambda i: (0, 0))
    ins = [own, mate, weight] + ([held] if held is not None else [])
    specs = [fixed, fixed, pl.BlockSpec((width, cols), lambda i: (0, 0))]
    specs = specs + [pl.BlockSpec(memory_space=pl.ANY)] * (held is not None)
    return run(
        kernel,
        [((total, cols), bf16), ((2 * rows, width), bf16)],
        ins,
        after,
        name,
        grid=(1,),
        in_specs=specs,
        out_specs=[
            pl.BlockSpec((2 * rows, cols), lambda i: (k, 0)),
            pl.BlockSpec((2 * rows, width), lambda i: (0, 0)),
        ],
        work=4 * rows * width * cols,
        aliases={3: 0} if held is not None else None,
    )


def out_rows(values, weight, k, rows, name, after=()):
    width, cols = weight.shape

    def kernel(value_ref, w_ref, p_own, p_mate):
        part = nt(value_ref[...], w_ref[...])
        p_own[...] = part[:rows].astype(bf16)
        p_mate[...] = part[rows:].astype(bf16)

    fixed = pl.BlockSpec((rows, width), lambda i: (0, 0))
    return run(
        kernel,
        [((rows, width), bf16)] * 2,
        [values, weight],
        after,
        name,
        grid=(1,),
        in_specs=[
            pl.BlockSpec((2 * rows, cols), lambda i: (k, 0)),
            pl.BlockSpec((width, cols), lambda i: (0, 0)),
        ],
        out_specs=[fixed, fixed],
        work=4 * rows * width * cols,
    )


def members_rows(members, weights, k, rows, name, after=()):
    width, cols = weights.shape[1:]

    def kernel(value_ref, w_ref, p_own, p_mate):
        part = nt(value_ref[0], w_ref[0])
        for m in range(1, 3):
            part = part + nt(value_ref[m], w_ref[m])
        p_own[...] = part[:rows].astype(bf16)
        p_mate[...] = part[rows:].astype(bf16)

    fixed = pl.BlockSpec((rows, width), lambda i: (0, 0))
    return run(
        kernel,
        [((rows, width), bf16)] * 2,
        [members, weights],
        after,
        name,
        grid=(1,),
        in_specs=[
            pl.BlockSpec((3, 2 * rows, cols), lambda i: (0, k, 0)),
            pl.BlockSpec((3, width, cols), lambda i: (0, 0, 0)),
        ],
        out_specs=[fixed, fixed],
        work=12 * rows * width * cols,
    )


def part(array, m=None, begin=0, end=None):
    value = array[...] if m is None else array[m]
    return value if end is None else value[:, begin:end]


def plain(item):
    return item[0] if isinstance(item, tuple) else item


def spot(item):
    return item[1:] if isinstance(item, tuple) else ()


def span(item):
    return item[3] - item[2] if len(spot(item)) > 1 else plain(item).shape[-1]


def lay_out(jobs):
    plan, ins = [], []
    for left, rights in jobs:
        picks = [[spot(item) for item in right] for right in rights]
        plan.append((len(left), picks, sum(span(right[0]) for right in rights)))
        ins = ins + list(left) + [plain(item) for right in rights for item in right]
    return plan, ins


def sides(plan, refs):
    at = 0
    for n_left, picks, cols in plan:
        left = refs[at : at + n_left]
        at = at + n_left
        columns = []
        for places in picks:
            values = []
            for place in places:
                values.append(part(refs[at], *place))
                at = at + 1
            columns.append(values[0] if len(values) == 1 else jnp.concatenate(values, axis=0))
        yield left, columns[0] if len(columns) == 1 else jnp.concatenate(columns, axis=1), cols


def outer(jobs, name, after=()):
    plan, ins = lay_out(jobs)
    total = sum(cols for _, _, cols in plan)
    width = jobs[0][0][0].shape[1]

    def kernel(*refs):
        column = 0
        for left, rights, cols in sides(plan, refs):
            rows = [ref[...] for ref in left]
            rows = rows[0] if len(rows) == 1 else jnp.concatenate(rows, axis=0)
            refs[-1][:, column : column + cols] = tn(rows, rights).astype(bf16)
            column = column + cols

    work = sum(2 * width * cols * sum(r.shape[0] for r in left) for (left, _), (_, _, cols) in zip(jobs, plan))
    return run(kernel, [((width, total), bf16)], ins, after, name, room=36, work=work)[0]


def outer_halves(links, jobs, turn, name, after=()):
    offsets, masks = links.offsets(turn)
    width = jobs[0][0][0].shape[1]
    share = width // links.dp
    me = lax.axis_index("dp").reshape(1).astype(jnp.int32)

    plan, ins = lay_out(jobs)
    ins = [me] + ins
    total = sum(cols for _, _, cols in plan)
    half = len(offsets)

    def kernel(me_ref, *refs):
        who = me_ref[0]
        sent_ref, kept_ref = refs[-2], refs[-1]
        column = 0
        for left, rights, cols in sides(plan, refs):
            for flip, dest in ((masks[0], sent_ref), (0, kept_ref)):
                picked = []
                for off in offsets:
                    where = pl.ds(pl.multiple_of((who ^ off ^ flip) * share, 128), share)
                    parts = [ref[:, where] for ref in left]
                    picked.append(parts[0] if len(parts) == 1 else jnp.concatenate(parts, axis=0))
                picked = picked[0] if half == 1 else jnp.concatenate(picked, axis=1)
                dest[:, column : column + cols] = tn(picked, rights).astype(bf16)
            column = column + cols

    return run(
        kernel,
        [((half * share, total), bf16)] * 2,
        ins,
        after,
        name,
        in_specs=[SMEM_SPEC] + [None] * (len(ins) - 1),
        room=24,
        work=2 * SLOT * width * total,
    )


def halve_all(pairs, name, after=()):
    shapes = [(kept.shape[0] // 2, kept.shape[1]) for kept, _ in pairs]
    count = len(pairs)

    def kernel(*refs):
        for i in range(count):
            total = wide(refs[2 * i]) + wide(refs[2 * i + 1])
            half = shapes[i][0]
            refs[2 * count + 2 * i][...] = total[half:].astype(bf16)
            refs[2 * count + 2 * i + 1][...] = total[:half].astype(bf16)

    outs = [(shape, bf16) for shape in shapes for _ in range(2)]
    made = run(kernel, outs, [array for pair in pairs for array in pair], after, name)
    return [(made[2 * i], made[2 * i + 1]) for i in range(count)]


def halves(ref_own, ref_mate, c):
    own, mate = ref_own[...], ref_mate[...]
    first = jnp.where(c == 0, own, mate)
    second = jnp.where(c == 0, mate, own)
    return first, second


def shift_rows(value, offset):
    if offset == 0:
        return value
    return pltpu.roll(value, (-offset) % value.shape[0], 0)


def place_mask(count, y, length):
    place = lax.broadcasted_iota(jnp.int32, (count + 2 * MARGIN, 1), 0) + (y * count - MARGIN)
    return ((place >= 0) & (place < length)).astype(f32)


def bordered(own_ref, mate_ref, before, after, who, ny):
    y, c = who // 2, who % 2
    first, second = halves(own_ref, mate_ref, c)
    above = wide(before[0])
    for ref in before[1:]:
        above = above + wide(ref)
    below = wide(after[0])
    for ref in after[1:]:
        below = below + wide(ref)
    above = jnp.where(y > 0, above, 0.0).astype(bf16)
    below = jnp.where(y < ny - 1, below, 0.0).astype(bf16)
    return jnp.concatenate([above, first, second, below], axis=0)


def conv_mix(ny, who, length, own, mate, before, after_rows, weights, taps, name, after=()):
    rows, width = own.shape
    cols = taps.shape[1]
    count = 2 * rows
    lo, hi = MARGIN, MARGIN + count
    n_before = len(before)

    def kernel(who_ref, len_ref, own_ref, mate_ref, w0, w1, taps_ref, *refs):
        rows_in = bordered(own_ref, mate_ref, refs[:n_before], refs[n_before:-5], who_ref[0], ny)
        lin_ref, gate_ref, mix_ref, tally_ref, seen_ref = refs[-5:]
        seen_ref[...] = jnp.concatenate([own_ref[...], mate_ref[...]], axis=0)
        valid = place_mask(count, who_ref[0] // 2, len_ref[0])
        linear = nn(rows_in, w0[...])
        gating = 1.0 / (1.0 + jnp.exp(-nn(rows_in, w1[...])))
        lin_ref[...] = linear
        gate_ref[...] = gating
        glu = linear * gating * valid
        mixture = taps_ref[0:1, :] * shift_rows(glu, -2)
        for j in range(1, KERNEL):
            mixture = mixture + taps_ref[j : j + 1, :] * shift_rows(glu, j - 2)
        mix_ref[...] = mixture
        inside = (valid * mixture)[lo:hi]
        tally_ref[...] = jnp.concatenate(
            [
                jnp.sum(inside, axis=0, keepdims=True),
                jnp.sum(inside * mixture[lo:hi], axis=0, keepdims=True),
                jnp.broadcast_to(jnp.sum(valid[lo:hi], axis=0, keepdims=True), (1, cols)),
                jnp.zeros((5, cols), f32),
            ],
            axis=0,
        )

    ins = [who, length, own, mate, weights[0], weights[1], taps] + list(before) + list(after_rows)
    shape = (count + 2 * MARGIN, cols)
    return run(
        kernel,
        [(shape, f32)] * 3 + [((8, cols), f32), ((count, width), bf16)],
        ins,
        after,
        name,
        in_specs=[SMEM_SPEC, SMEM_SPEC] + [None] * (len(ins) - 2),
        room=28,
        work=4 * count * width * cols,
    )


def batch_terms(tally_ref):
    count = tally_ref[2:3, :]
    mean = tally_ref[0:1, :] / count
    var = tally_ref[1:2, :] / count - mean * mean
    return count, mean, var, lax.rsqrt(var + eps_norm)


def conv_out(who, mixture, tallies, affine, running, weight, rows, name, after=()):
    width, cols = weight.shape
    channels = running.shape[1]
    lo, mid, hi = MARGIN, MARGIN + rows, MARGIN + 2 * rows

    def kernel(who_ref, mix_ref, tally_ref, affine_ref, run_ref, w_ref, act_ref, p_own, p_mate, new_ref):
        c = who_ref[0] % 2
        count, mean, var, inverse = batch_terms(tally_ref)
        own = pl.ds(pl.multiple_of(lo + c * rows, 16), rows)
        mate = pl.ds(pl.multiple_of(lo + (1 - c) * rows, 16), rows)
        mixture = jnp.concatenate([mix_ref[own, :], mix_ref[mate, :]], axis=0)
        shifted = (mixture - mean) * inverse * affine_ref[0:1, :] + affine_ref[1:2, :]
        active = (shifted / (1.0 + jnp.exp(-shifted))).astype(bf16)
        act_ref[...] = active
        part = nt(active, w_ref[...])
        p_own[...] = part[:rows].astype(bf16)
        p_mate[...] = part[rows:].astype(bf16)
        grown = var * count / (count - 1.0)
        new_ref[...] = (1.0 - momentum) * run_ref[...] + momentum * jnp.concatenate(
            [mean[:, :channels], grown[:, :channels]], axis=0
        )

    return run(
        kernel,
        [((2 * rows, cols), bf16), ((rows, width), bf16), ((rows, width), bf16), (running.shape, f32)],
        [who, mixture, tallies, affine, running, weight],
        after,
        name,
        in_specs=[SMEM_SPEC] + [None] * 5,
        room=24,
        work=4 * rows * width * cols,
    )


def conv_shift_grad(ny, who, length, own, mate, before, after_rows, mixture, tallies, affine, weight, name, after=()):
    rows, width = own.shape
    cols = weight.shape[1]
    count = 2 * rows
    lo, hi = MARGIN, MARGIN + count
    n_before = len(before)

    def kernel(who_ref, len_ref, own_ref, mate_ref, mix_ref, tally_ref, affine_ref, w_ref, *refs):
        rows_in = bordered(own_ref, mate_ref, refs[:n_before], refs[n_before:-3], who_ref[0], ny)
        dz_ref, out_ref, seen_ref = refs[-3:]
        seen_ref[...] = jnp.concatenate([own_ref[...], mate_ref[...]], axis=0)
        valid = place_mask(count, who_ref[0] // 2, len_ref[0])
        _, mean, _, inverse = batch_terms(tally_ref)
        centred = (mix_ref[...] - mean) * inverse
        shifted = centred * affine_ref[0:1, :] + affine_ref[1:2, :]
        logistic = 1.0 / (1.0 + jnp.exp(-shifted))
        slope = logistic * (1.0 + shifted * (1.0 - logistic))
        grad = jnp.where(valid > 0.0, nn(rows_in, w_ref[...]) * slope, 0.0)
        dz_ref[...] = grad
        inner = grad[lo:hi]
        out_ref[...] = jnp.concatenate(
            [
                jnp.sum(inner * centred[lo:hi], axis=0, keepdims=True),
                jnp.sum(inner, axis=0, keepdims=True),
                jnp.zeros((6, cols), f32),
            ],
            axis=0,
        )

    ins = [who, length, own, mate, mixture, tallies, affine, weight] + list(before) + list(after_rows)
    return run(
        kernel,
        [(mixture.shape, f32), ((8, cols), f32), ((count, width), bf16)],
        ins,
        after,
        name,
        in_specs=[SMEM_SPEC, SMEM_SPEC] + [None] * (len(ins) - 2),
        room=28,
        work=4 * count * width * cols,
    )


def conv_in_grad(who, length, dz, mixture, tallies, sums, affine, taps, linear, gating, weights, rows, name, after=()):
    width, cols = weights[0].shape
    count = 2 * rows
    lo, mid, hi = MARGIN, MARGIN + rows, MARGIN + count

    def kernel(who_ref, len_ref, dz_ref, mix_ref, tally_ref, sum_ref, affine_ref, taps_ref, lin_ref, gate_ref, w0, w1, dl_ref, dg_ref, p_own, p_mate, tap_ref):
        c = who_ref[0] % 2
        valid = place_mask(count, who_ref[0] // 2, len_ref[0])
        total, mean, _, inverse = batch_terms(tally_ref)
        centred = (mix_ref[...] - mean) * inverse
        shrink = affine_ref[0:1, :] * inverse
        mixed = (sum_ref[1:2, :] + centred * sum_ref[0:1, :]) / total
        grad_mix = jnp.where(valid > 0.0, shrink * (dz_ref[...] - mixed), 0.0)
        grad_glu = taps_ref[0:1, :] * shift_rows(grad_mix, 2)
        for j in range(1, KERNEL):
            grad_glu = grad_glu + taps_ref[j : j + 1, :] * shift_rows(grad_mix, 2 - j)
        linear = lin_ref[...]
        gating = gate_ref[...]
        glu = linear * gating * valid
        inner = grad_mix[lo:hi]
        tap_ref[...] = jnp.concatenate(
            [
                jnp.sum(inner * shift_rows(glu, j - 2)[lo:hi], axis=0, keepdims=True)
                for j in range(KERNEL)
            ]
            + [jnp.zeros((8 - KERNEL, cols), f32)],
            axis=0,
        )
        held = grad_glu * valid * gating
        grad_linear = held.astype(bf16)
        grad_gate = (held * linear * (1.0 - gating)).astype(bf16)

        def turned(value):
            first, second = value[lo:mid], value[mid:hi]
            return jnp.concatenate(
                [jnp.where(c == 0, first, second), jnp.where(c == 0, second, first)], axis=0
            )

        grad_linear = turned(grad_linear)
        grad_gate = turned(grad_gate)
        dl_ref[...] = grad_linear
        dg_ref[...] = grad_gate
        part = nt(grad_linear, w0[...]) + nt(grad_gate, w1[...])
        p_own[...] = part[:rows].astype(bf16)
        p_mate[...] = part[rows:].astype(bf16)

    return run(
        kernel,
        [((count, cols), bf16)] * 2 + [((rows, width), bf16)] * 2 + [((8, cols), f32)],
        [who, length, dz, mixture, tallies, sums, affine, taps, linear, gating, weights[0], weights[1]],
        after,
        name,
        in_specs=[SMEM_SPEC, SMEM_SPEC] + [None] * 10,
        room=32,
        work=4 * count * width * cols,
    )


class Links:
    def __init__(self, dp, tensor):
        self.dp, self.tensor, self.ny = dp, tensor, tensor // 2
        self.masks = [1 << bit for bit in range(dp.bit_length() - 1)]

    def core(self, value):
        return lax.ppermute(value, "tensor", [(i, i ^ 1) for i in range(self.tensor)])

    def mate(self, value):
        pieces = 4 if value.shape[0] % 64 == 0 else 1
        rows = value.shape[0] // pieces
        return [self.core(value[i * rows : (i + 1) * rows]) for i in range(pieces)]

    def chip(self, value, k):
        return lax.ppermute(value, "tensor", [(i, i ^ (2 * k)) for i in range(self.tensor)])

    def group(self, value, mask):
        return lax.ppermute(value, "dp", [(i, i ^ mask) for i in range(self.dp)])

    def scatter_grad(self, value):
        return lax.psum_scatter(value, "dp", scatter_dimension=0, tiled=True)

    def sum_group(self, value):
        for mask in self.masks:
            value = value + self.group(value, mask)
        return value

    def sum_stats(self, value, channels):
        return self.sum_group(self.sum_columns(value, channels))

    def sum_columns(self, value, channels):
        def cols(array, k):
            return array[:, k * channels : (k + 1) * channels]

        total = value
        for k in range(1, self.ny):
            other = self.chip(value, k)
            total = total + jnp.concatenate([cols(other, r ^ k) for r in range(self.ny)], axis=1)
        return total

    def offsets(self, turn):
        masks = list(self.masks)
        if turn:
            masks[:2] = masks[1::-1]
        offsets = [0]
        for mask in masks[:0:-1]:
            offsets = offsets + [off ^ mask for off in offsets]
        return offsets, masks

    def borders(self, own, mate):
        count = own.shape[0]
        who = lax.axis_index("tensor")
        y, c = who // 2, who % 2
        if self.ny == 2:
            edge = lax.dynamic_slice_in_dim(own, (1 - y) * (count - MARGIN), MARGIN)
            straight = lax.ppermute(edge, "tensor", [(1, 3), (2, 0)])
            across = lax.ppermute(edge, "tensor", [(1, 2), (2, 1)])
            return [straight, across], [straight, across]
        mate = jnp.concatenate(mate)
        head = jnp.where(c == 0, own, mate)[:MARGIN]
        foot = jnp.where(c == 0, mate, own)[count - MARGIN :]
        down = [(i, i + 2) for i in range(self.tensor - 2)]
        up = [(i + 2, i) for i in range(self.tensor - 2)]
        return [lax.ppermute(foot, "tensor", down)], [lax.ppermute(head, "tensor", up)]


class Pieces:
    def __init__(self, links, pieces, name):
        self.links, self.name = links, name
        self.count = len(pieces)
        self.masks = [links.offsets(i % 2)[1] for i in range(self.count)]
        self.kept = [kept for _, kept in pieces]
        self.at = 0
        self.send([sent for sent, _ in pieces])

    def send(self, sent):
        self.came = [self.links.group(sent[i], self.masks[i][self.at]) for i in range(self.count)]
        self.at += 1

    def step(self, after=()):
        if self.at < len(self.links.masks):
            made = halve_all(list(zip(self.kept, self.came)), self.name + "_half", after)
            self.kept = [kept for _, kept in made]
            self.send([sent for sent, _ in made])
        return self.kept[0]

    def finish(self):
        while self.at < len(self.links.masks):
            self.step()
        return [array for pair in zip(self.kept, self.came) for array in pair]


def finish_one(outs_of, ins_of, width_in, name):
    ins = outs_of + ins_of
    share = ins[0].shape[0]

    def kernel(*refs):
        out = refs[-1]
        parts = [wide(refs[2 * i]) + wide(refs[2 * i + 1]) for i in range(4)]
        out[1] = jnp.concatenate(parts[:2], axis=1)
        out[0] = jnp.concatenate(parts[2:], axis=1)

    return run(kernel, [((2, share, width_in), f32)], ins, (), name)[0]


def split_two(total, hidden, name, after=()):
    share = total.shape[0]

    def kernel(ref, out):
        for m in range(2):
            out[m] = wide(ref)[:, m * hidden : (m + 1) * hidden]

    return run(kernel, [((2, share, hidden), f32)], [total], after, name)[0]


def split_heads(total, begin, cols, name):
    share = total.shape[0]

    def kernel(ref, three, one):
        value = wide(ref)[:, begin:]
        for m in range(3):
            three[m] = value[:, m * cols : (m + 1) * cols]
        one[...] = value[:, 3 * cols :]

    return run(kernel, [((3, share, cols), f32), ((share, cols), f32)], [total], (), name)


def finish_conv(links, total, channels, name):
    share = total.shape[0]
    ny = links.ny

    def split(ref, *others):
        for m in range(3):
            for k in range(1, ny):
                at = (m * ny + k) * channels
                others[k - 1][m] = ref[:, at : at + channels]

    shape = (3, share, channels)
    parts = run(split, [(shape, bf16)] * (ny - 1), [total], (), name)
    came = [links.chip(parts[k - 1], k) for k in range(1, ny)]

    def close(*refs):
        for m in range(3):
            piece = refs[0][:, m * ny * channels : (m * ny + 1) * channels].astype(f32)
            for ref in refs[1:-1]:
                piece = piece + ref[m].astype(f32)
            refs[-1][m] = piece

    return run(close, [(shape, f32)], [total] + came, (), name + "_close")[0]


def arrange(conv_proj, gathered, dp, name):
    _, width, channels = conv_proj.shape
    share = width // dp
    cols = channels * (1 + len(gathered))

    def kernel(own_ref, *refs):
        others, outs = refs[: len(gathered)], refs[len(gathered) :]
        for m in range(3):
            outs[m][:, :channels] = own_ref[m]
            for k, ref in enumerate(others):
                for b in range(dp):
                    at = (b * 3 + m) * share
                    outs[m][b * share : (b + 1) * share, (k + 1) * channels : (k + 2) * channels] = ref[
                        at : at + share, :
                    ]

    return run(kernel, [((width, cols), bf16)] * 3, [conv_proj] + gathered, (), name)


def per_device(
    links,
    x_in,
    cotangent,
    lengths,
    norm_gains,
    ffn_first,
    attn_qkv,
    attn_out,
    rel_table,
    conv_proj,
    depthwise,
    bn_gain,
    bn_bias,
    running,
    ffn_second,
):
    ny = links.ny
    others = list(range(1, ny))
    rows, width = x_in.shape
    channels = bn_gain.shape[0]
    who = lax.axis_index("tensor").astype(jnp.int32)
    who_arr = who.reshape(1)
    y, c = who // 2, who % 2
    gain = [norm_gains[i : i + 1] for i in range(5)]
    begin = [(((y ^ k) * 2 + c) * rows).reshape(1) for k in range(ny)]

    me = lax.axis_index("dp")
    share = width // links.dp
    piece = lax.dynamic_slice_in_dim(conv_proj, me * share, share, axis=1)
    gathered = []
    for k in others:
        other = links.chip(piece, k).reshape(3 * share, channels)
        gathered.append(lax.all_gather(other, "dp", axis=0, tiled=True))
    conv_w = arrange(conv_proj, gathered, links.dp, "conv_weights")
    small = jnp.concatenate([depthwise, bn_gain[None], bn_bias[None], jnp.zeros((1, channels), f32)])
    small = jnp.concatenate([small] + [links.chip(small, k) for k in others], axis=1)
    affine = small[KERNEL : KERNEL + 2]

    def send_sums(parts, name, after=()):
        return add_up([parts[0], links.mate(parts[1])], name, after)

    normed, x_low = norm_rows(x_in, [], 0.0, gain[0], "ln_in", keep=False, low=True)
    x_rows = [x_in] + [links.chip(x_low, k) for k in others]
    na_first, kept_first, sums, came = {}, {}, {}, {}
    token = ()
    for k in range(ny):
        if k:
            (normed,) = norm_rows(x_rows[k], [], 0.0, gain[0], "ln_in", token, keep=False)
        na_first[k] = (normed, links.mate(normed))
        p_own, p_mate, pre, hid, na_first[k] = feed(*na_first[k], ffn_first, "ffn_one")
        kept_first[k] = (pre, hid)
        sums[k] = send_sums((p_own, p_mate), "ffn_one_sum")
        token = (sums[k],)

    def all_parts(sums, k):
        return [sums[k]] + [links.chip(sums[k ^ j], j) for j in others]

    token = ()
    na_attn, first, qkv, cot_low = {}, {}, None, None
    for k in others + [0]:
        also = cotangent if k == 0 else None
        made = norm_rows(
            x_rows[k], all_parts(sums, k), 0.5, gain[1], "ln_attn", token, also=also
        )
        na_attn[k] = (made[0], links.mate(made[0]))
        first[k] = made[1]
        if k == 0:
            cot_low = made[2]
        qkv, na_attn[k] = qkv_rows(*na_attn[k], attn_qkv, k, SLOT, qkv, "qkv")
        token = (qkv,)
    cot_rows = [cotangent] + [links.chip(cot_low, k) for k in others]
    heads_out, probs = attend(qkv, who_arr, lengths, rel_table, rows)
    token = ()
    arrived = []
    for k in others:
        total = send_sums(out_rows(heads_out, attn_out, k, rows, "out_proj", token), "out_sum")
        arrived.append(links.chip(total, k))
        token = (total,)
    p_own, p_mate = out_rows(heads_out, attn_out, 0, rows, "out_proj", token)
    conv_own, after_attn = norm_rows(
        first[0], [p_own, links.mate(p_mate)] + arrived, 1.0, gain[2], "ln_conv"
    )

    conv_mate = links.mate(conv_own)
    before, after_rows = links.borders(conv_own, conv_mate)
    linear, gating, mixture, tallies, conv_in = conv_mix(
        ny, who_arr, lengths, conv_own, conv_mate, before, after_rows, conv_w, small[:KERNEL], "conv_mix"
    )
    tallies = links.sum_stats(tallies, channels)
    active, p_own, p_mate, updated = conv_out(
        who_arr, mixture, tallies, affine, running, conv_w[2], rows, "conv_out"
    )
    normed, after_conv, low = norm_rows(
        after_attn, [p_own, links.mate(p_mate)], 1.0, gain[3], "ln_ffn_two", low=True
    )

    x_rows = [after_conv] + [links.chip(low, k) for k in others]
    na_last, kept_last, sums = {}, {}, {}
    token = ()
    for k in range(ny):
        if k:
            (normed,) = norm_rows(x_rows[k], [], 0.0, gain[3], "ln_ffn_two", token, keep=False)
        na_last[k] = (normed, links.mate(normed))
        p_own, p_mate, pre, hid, na_last[k] = feed(*na_last[k], ffn_second, "ffn_two")
        kept_last[k] = (pre, hid)
        sums[k] = send_sums((p_own, p_mate), "ffn_two_sum")
        token = (sums[k],)

    token = ()
    upper, down, arrived = {}, {}, []
    for k in others + [0]:
        made = norm_last(
            x_rows[k],
            all_parts(sums, k),
            gain[4],
            cot_rows[k],
            begin[k],
            lengths,
            "ln_last",
            k == 0,
            token,
        )
        upper[k] = (made[0], links.mate(made[0]))
        p_own, p_mate, down[k], upper[k] = feed_grad(
            *upper[k], kept_last[k][0], ffn_second, "ffn_two_grad"
        )
        if k:
            total = send_sums((p_own, p_mate), "ffn_two_grad_sum")
            arrived.append(links.chip(total, k))
            token = (total,)
        else:
            grad, output, gain_five = made[1:]
            parts = [p_own, links.mate(p_mate)]

    def every(pieces):
        return [pieces[k] for k in range(ny)]

    hid_last = [kept_last[k][1] for k in range(ny)]
    two_sum = outer(
        [(every(na_last), [every(down)]), (every(upper), [hid_last])], "ffn_two_w", (p_mate,)
    )
    low, grad, gain_four = norm_grad(
        after_conv, parts + arrived, gain[3], grad, "back_ffn_two", (two_sum,), factor=1.0
    )
    two_sum = links.scatter_grad(two_sum)

    up_own = low
    up_mate = links.mate(low)
    before, after_rows = links.borders(up_own, up_mate)
    dz, sums, conv_up = conv_shift_grad(
        ny, who_arr, lengths, up_own, up_mate, before, after_rows, mixture, tallies, affine, conv_w[2], "conv_dz"
    )
    bn_grads = links.sum_stats(sums, channels)
    grad_linear, grad_gate, p_own, p_mate, tap_grad = conv_in_grad(
        who_arr, lengths, dz, mixture, tallies, bn_grads, affine, small[:KERNEL], linear, gating, conv_w, rows, "conv_din"
    )
    low, grad, gain_three = norm_grad(
        after_attn, [p_own, links.mate(p_mate)], gain[2], grad, "back_conv", factor=1.0
    )


    g_rows = [low] + [links.chip(low, k) for k in others]
    token = (low,)
    grad_heads = None
    upper_attn = {}
    for k in range(ny):
        grad_heads, upper_attn[k] = heads_rows(
            g_rows[k], links.mate(g_rows[k]), attn_out, k, SLOT, grad_heads, "dheads", token
        )
        token = ()
    members, table_grad = attend_back(qkv, grad_heads, probs, who_arr, rel_table, rows)
    token = ()
    sums = {}
    for k in range(ny):
        sums[k] = send_sums(members_rows(members, attn_qkv, k, rows, "dqkv", token), "dqkv_sum")
        token = (sums[k],)
    heads_sum = outer(
        [
            ([conv_in], [[grad_linear], [grad_gate]]),
            ([conv_up], [[active]]),
            (every(na_attn), [[(members, m)] for m in range(3)]),
            (every(upper_attn), [[heads_out]]),
        ],
        "attn_w",
        token,
    )
    token = (heads_sum,)
    heads_sum = links.scatter_grad(heads_sum)

    upper, down, arrived = {}, {}, []
    for k in others + [0]:
        made = norm_grad(
            first[k],
            all_parts(sums, k),
            gain[1],
            grad if k == 0 else g_rows[k],
            "back_attn",
            token,
            factor=0.5,
            keep=k == 0,
            sums=k == 0,
        )
        upper[k] = (made[0], links.mate(made[0]))
        p_own, p_mate, down[k], upper[k] = feed_grad(
            *upper[k], kept_first[k][0], ffn_first, "ffn_one_grad"
        )
        if k:
            total = send_sums((p_own, p_mate), "ffn_one_grad_sum")
            arrived.append(links.chip(total, k))
            token = (total,)
        else:
            grad, gain_two = made[1:]
            parts = [p_own, links.mate(p_mate)]
    hid_first = [kept_first[k][1] for k in range(ny)]
    hidden = ffn_first.shape[2]
    half = hidden // 2
    one_down, one_up, one_in = every(down), every(upper), every(na_first)
    token = (p_mate,)
    pairs = []
    if share % 128 == 0:
        for left, right in ((one_up, hid_first), (one_in, one_down)):
            pieces = []
            for turn in range(2):
                columns = [(r, None, turn * half, (turn + 1) * half) for r in right]
                made = outer_halves(links, [(left, [columns])], turn, "ffn_one_w", token)
                token = (made[0],)
                pieces.append(made)
            pairs.append(Pieces(links, pieces, "one"))
    else:
        first_sum = outer([(one_in, [one_down]), (one_up, [hid_first])], "ffn_one_w", token)
        token = (first_sum,)
        first_sum = links.scatter_grad(first_sum)
    last_sum = split_two(two_sum, hidden, "two_end", token)
    grad_input, gain_one = norm_grad(
        x_in, parts + arrived, gain[0], grad, "back_ffn_one", token + (last_sum,)
    )

    gains = [gain_one, gain_two, gain_three, gain_four, gain_five]
    gains = jnp.stack([part[0] for part in gains]).reshape(-1, HEAD)
    bundle = jnp.concatenate([gains, table_grad])
    bundle = jnp.pad(bundle, ((0, -bundle.shape[0] % 8), (0, 0)))
    bundle = bundle + links.core(bundle)
    for k in [1 << bit for bit in range(ny.bit_length() - 1)]:
        bundle = bundle + links.chip(bundle, k)
    taps_at = bundle.shape[0]
    tap_sums = links.sum_columns(tap_grad, channels)[:, :channels]
    bundle = jnp.concatenate([bundle, tap_sums.reshape(-1, HEAD)])
    token = ()
    for mask in links.masks:
        bundle = bundle + links.group(bundle, mask)
        for pair in pairs:
            pair.step((bundle,))
    kernel_grad = bundle[taps_at:].reshape(8, channels)[:KERNEL]
    if pairs:
        first_sum = finish_one(pairs[0].finish(), pairs[1].finish(), hidden, "one_end")
    else:
        first_sum = split_two(first_sum, hidden, "one_end")
    qkv_sum, out_sum = split_heads(heads_sum, 3 * ny * channels, attn_qkv.shape[2], "heads_end")
    conv_sum = finish_conv(links, heads_sum, channels, "conv_end")
    return (
        output,
        grad_input,
        bundle[: gains.shape[0]].reshape(5, width),
        first_sum,
        qkv_sum,
        out_sum,
        bundle[gains.shape[0] : gains.shape[0] + REL],
        conv_sum,
        kernel_grad,
        bn_grads[0, :channels],
        bn_grads[1, :channels],
        updated,
        last_sum,
    )


def solution(mesh):
    links = Links(mesh.shape["dp"], mesh.shape["tensor"])
    placed = (
        P(("dp", "tensor"), None),
        P(("dp", "tensor"), None),
        P("dp"),
        P(),
        P(None, None, "tensor"),
        P(None, None, "tensor"),
        P(None, "tensor"),
        P(),
        P(None, None, "tensor"),
        P(None, "tensor"),
        P("tensor"),
        P("tensor"),
        P(None, "tensor"),
        P(None, None, "tensor"),
    )
    return jax.shard_map(
        functools.partial(per_device, links),
        mesh=mesh,
        in_specs=placed,
        out_specs=(
            P(("dp", "tensor"), None),
            P(("dp", "tensor"), None),
            P(),
            P(None, "dp", "tensor"),
            P(None, "dp", "tensor"),
            P("dp", "tensor"),
            P(),
            P(None, "dp", "tensor"),
            P(None, "tensor"),
            P("tensor"),
            P("tensor"),
            P(None, "tensor"),
            P(None, "dp", "tensor"),
        ),
        check_vma=False,
    )
```

```python
import functools

import jax
import jax.numpy as jnp
from jax import lax
from jax.experimental import pallas as pl
from jax.experimental.pallas import tpu as pltpu
from jax.sharding import PartitionSpec as P

HEAD = 128
KERNEL = 5
LEFT = 64
RIGHT = 8
SLOT = 1024
REL = 73
MARGIN = 16
SUB = 128
BLK = 256
WIN = 3 * SUB
WRAP = 512
LOG2E = 1.4426950408889634
VMEM_CAP = 32 * 1024 * 1024

eps_norm = 1e-05
momentum = 0.5
bf16 = jnp.bfloat16
f32 = jnp.float32


def nn(left_op, right_op):
    return lax.dot_general(
        left_op, right_op, (((1,), (0,)), ((), ())), preferred_element_type=f32
    )


def nt(left_op, right_op):
    return lax.dot_general(
        left_op, right_op, (((1,), (1,)), ((), ())), preferred_element_type=f32
    )


def tn(left_op, right_op):
    return lax.dot_general(
        left_op, right_op, (((0,), (0,)), ((), ())), preferred_element_type=f32
    )


def window_table(rel_table):
    width=rel_table.shape[1]
    def kernel(table_ref, hi_ref, lo_ref):
        pick=spots(0)
        table=table_ref[...]
        hi=table.astype(jnp.bfloat16)
        lo=(table-hi.astype(jnp.float32)).astype(jnp.bfloat16)
        hi_ref[...]=nn(pick,hi).astype(jnp.bfloat16)
        lo_ref[...]=nn(pick,lo).astype(jnp.bfloat16)
    return run(kernel,[((WRAP,width),jnp.bfloat16)]*2,[rel_table],(),"window_table")

def spots(axis):
    shape=(WRAP,128) if axis==0 else (128,WRAP)
    u=lax.broadcasted_iota(jnp.int32,shape,axis)
    row=lax.broadcasted_iota(jnp.int32,shape,1-axis)
    dist=jnp.where(u<=WIN,jnp.clip(u-SUB,-LEFT,RIGHT),-LEFT)+LEFT
    return (dist==row).astype(jnp.bfloat16)

def order_in(dst, src, who, rows):
    for j in range(SLOT//rows):
        dst[j*rows:(j+1)*rows,:]=src[pl.ds(pl.multiple_of((j^who)*rows,rows),rows),:]

def attend_kernel(rows, who_ref, len_ref, q_ref, k_ref, v_ref, hi_ref, lo_ref, o_ref, p_ref, qs, ks, vs):
    who=who_ref[0]
    length=len_ref[0]
    order_in(qs,q_ref.at[0],who,rows); order_in(ks,k_ref.at[0],who,rows); order_in(vs,v_ref.at[0],who,rows)
    factor=HEAD**(-0.5)*LOG2E
    tail=lax.broadcasted_iota(jnp.int32,(SUB,SLOT//2),1)+SLOT//2<length
    for base in range(0,SLOT,BLK):
        q=qs[base:base+BLK,:]
        content=nt(q,ks[...])
        spread=nt(q,hi_ref[...])+nt(q,lo_ref[...])
        for off in range(0,BLK,SUB):
            i0=base+off
            e=spread[off:off+SUB]
            rolled=pltpu.roll(e,0,1,stride=1,stride_axis=0)
            lo_c=max(i0-SUB,0); hi_c=min(i0+2*SUB,SLOT)
            parts=[]
            if lo_c>0: parts.append(content[off:off+SUB,:lo_c]+e[:,0:1])
            parts.append(content[off:off+SUB,lo_c:hi_c]+rolled[:,lo_c-(i0-SUB):hi_c-(i0-SUB)])
            if hi_c<SLOT: parts.append(content[off:off+SUB,hi_c:]+e[:,WIN-1:WIN])
            logit=jnp.concatenate(parts,axis=1)*factor
            logit=jnp.concatenate([logit[:,:SLOT//2],jnp.where(tail,logit[:,SLOT//2:],-1e30)],axis=1)
            peak=jnp.max(logit,axis=1,keepdims=True)
            ex=jnp.exp2(logit-peak)
            tot=jnp.sum(ex,axis=1,keepdims=True)
            p_ref[0,i0:i0+SUB,:]=(ex*(1.0/tot)).astype(jnp.bfloat16)
        out=nn(p_ref[0,base:base+BLK,:],vs[...]).astype(jnp.bfloat16)
        for part in range(0,BLK,rows) if rows<BLK else (0,):
            n=min(rows,BLK)
            j=(base+part)//rows; inner=(base+part)%rows
            o_ref[pl.ds(pl.multiple_of((j^who)*rows+inner,n),n),:]=out[part:part+n]

def attend(qkv, who, length, table, rows):
    heads=qkv.shape[2]//HEAD
    hi,lo=table
    spec=lambda m: pl.BlockSpec((1,SLOT,HEAD),lambda h,m=m:(m,0,h))
    tab=pl.BlockSpec((WRAP,HEAD),lambda h:(0,0))
    return run(
        functools.partial(attend_kernel,rows),
        [((SLOT,heads*HEAD),jnp.bfloat16),((heads,SLOT,SLOT),jnp.bfloat16)],
        [who,length,qkv,qkv,qkv,hi,lo],
        (),"attend",grid=(heads,),
        in_specs=[SMEM_SPEC,SMEM_SPEC,spec(0),spec(1),spec(2),tab,tab],
        out_specs=[pl.BlockSpec((SLOT,HEAD),lambda h:(0,h)),pl.BlockSpec((1,SLOT,SLOT),lambda h:(h,0,0))],
        scratch=[pltpu.VMEM((SLOT,HEAD),jnp.bfloat16)]*3,
        room=28,work=heads*32*SLOT*SLOT*HEAD,
    )

def attend_back_kernel(rows, heads, who_ref, q_ref, k_ref, v_ref, g_ref, p_ref, hi_ref, lo_ref, d_ref, dt_ref, qs, ks, vs, gs, dkt, dvt):
    who=who_ref[0]
    for dst,src in ((qs,q_ref.at[0]),(ks,k_ref.at[0]),(vs,v_ref.at[0]),(gs,g_ref)):
        order_in(dst,src,who,rows)
    factor=HEAD**(-0.5)
    first=hi_ref[0:1,:].astype(jnp.float32)+lo_ref[0:1,:].astype(jnp.float32)
    final=hi_ref[WIN-1:WIN,:].astype(jnp.float32)+lo_ref[WIN-1:WIN,:].astype(jnp.float32)
    zero=jnp.zeros((SUB,SUB),jnp.float32)
    flip=(lax.broadcasted_iota(jnp.int32,(SUB,SUB),0)+lax.broadcasted_iota(jnp.int32,(SUB,SUB),1)==SUB-1).astype(jnp.bfloat16)
    table_acc=jnp.zeros((HEAD,WRAP),jnp.float32)
    left_acc=jnp.zeros((1,HEAD),jnp.float32)
    right_acc=jnp.zeros((1,HEAD),jnp.float32)
    for base in range(0,SLOT,BLK):
        q=qs[base:base+BLK,:]
        g=gs[base:base+BLK,:]
        pb=p_ref[0,base:base+BLK,:]
        p=pb.astype(jnp.float32)
        dp=nt(g,vs[...])
        delta=jnp.sum(p*dp,axis=1,keepdims=True)
        dsb=(p*(dp-delta)).astype(jnp.bfloat16)
        dv_part=tn(g,pb)
        dk_part=tn(q,dsb)
        if base==0:
            dvt[...]=dv_part; dkt[...]=dk_part
        else:
            dvt[...]+=dv_part; dkt[...]+=dk_part
        dq=nn(dsb,ks[...])
        ds=dsb.astype(jnp.float32)
        qf=q.astype(jnp.float32)
        extra=[]
        for off in range(0,BLK,SUB):
            i0=base+off
            d=ds[off:off+SUB]
            lo_c=max(i0-SUB,0); hi_c=min(i0+2*SUB,SLOT)
            turned=nn(flip,dsb[off:off+SUB,lo_c:hi_c])
            win=[zero]*((lo_c-(i0-SUB))//SUB)+[turned]+[zero]*((i0+2*SUB-hi_c)//SUB+1)
            moved=pltpu.roll(jnp.concatenate(win,axis=1),WRAP-SUB+1,1,stride=1,stride_axis=0)
            u=nn(flip,moved.astype(jnp.bfloat16)).astype(jnp.bfloat16)
            add=nn(u,hi_ref[...])+nn(u,lo_ref[...])
            table_acc=table_acc+tn(q[off:off+SUB],u)
            if lo_c>0:
                s=jnp.sum(d[:,:lo_c],axis=1,keepdims=True)
                add=add+s*first
                left_acc=left_acc+jnp.sum(s*qf[off:off+SUB],axis=0,keepdims=True)
            if hi_c<SLOT:
                s=jnp.sum(d[:,hi_c:],axis=1,keepdims=True)
                add=add+s*final
                right_acc=right_acc+jnp.sum(s*qf[off:off+SUB],axis=0,keepdims=True)
            extra.append(add)
        dq=((dq+jnp.concatenate(extra,axis=0))*factor).astype(jnp.bfloat16)
        for part in range(0,BLK,rows) if rows<BLK else (0,):
            n=min(rows,BLK)
            j=(base+part)//rows; inner=(base+part)%rows
            d_ref[0,pl.ds(pl.multiple_of((j^who)*rows+inner,n),n),:]=dq[part:part+n]
    spread=table_acc*factor
    upper=spread.astype(jnp.bfloat16)
    lower=(spread-upper.astype(jnp.float32)).astype(jnp.bfloat16)
    pick=spots(1)
    gathered=nt(pick,upper)+nt(pick,lower)
    row=lax.broadcasted_iota(jnp.int32,(128,1),0)
    gathered=gathered+jnp.where(row==0,left_acc*factor,0.0)+jnp.where(row==LEFT+RIGHT,right_acc*factor,0.0)
    @pl.when(pl.program_id(0)==0)
    def _():
        dt_ref[...]=gathered
    @pl.when(pl.program_id(0)>0)
    def _():
        dt_ref[...]+=gathered
    for j in range(SLOT//rows):
        sl=pl.ds(pl.multiple_of((j^who)*rows,rows),rows)
        d_ref[1,sl,:]=(jnp.transpose(dkt[:,j*rows:(j+1)*rows])*factor).astype(jnp.bfloat16)
        d_ref[2,sl,:]=jnp.transpose(dvt[:,j*rows:(j+1)*rows]).astype(jnp.bfloat16)

def attend_back(qkv, grad, probs, who, table, rows):
    heads=qkv.shape[2]//HEAD
    hi,lo=table
    spec=lambda m: pl.BlockSpec((1,SLOT,HEAD),lambda h,m=m:(m,0,h))
    tab=pl.BlockSpec((WRAP,HEAD),lambda h:(0,0))
    return run(
        functools.partial(attend_back_kernel,rows,heads),
        [((3,SLOT,heads*HEAD),jnp.bfloat16),((128,HEAD),jnp.float32)],
        [who,qkv,qkv,qkv,grad,probs,hi,lo],
        (),"attend_back",grid=(heads,),
        in_specs=[SMEM_SPEC,spec(0),spec(1),spec(2),pl.BlockSpec((SLOT,HEAD),lambda h:(0,h)),pl.BlockSpec((1,SLOT,SLOT),lambda h:(h,0,0)),tab,tab],
        out_specs=[pl.BlockSpec((3,SLOT,HEAD),lambda h:(0,0,h)),pl.BlockSpec((128,HEAD),lambda h:(0,0))],
        scratch=[pltpu.VMEM((SLOT,HEAD),jnp.bfloat16)]*4+[pltpu.VMEM((HEAD,SLOT),jnp.float32)]*2,
        room=28,work=heads*50*SLOT*SLOT*HEAD,
    )


MARKS = {}
PIECES = 4


class Stack:
    def __init__(self, refs):
        self.refs = refs

    def __getitem__(self, index):
        return jnp.concatenate([ref[index] for ref in self.refs], axis=0)


def run(
    kernel,
    outs,
    ins,
    after=(),
    name=None,
    grid=None,
    in_specs=None,
    out_specs=None,
    scratch=(),
    aliases=None,
    room=24,
    work=1 << 20,
    mark=False,
):
    after = [MARKS[id(item)][1] if id(item) in MARKS else item for item in after]
    waits = len(after)
    outs = list(outs) + [((8, 128), f32)] * mark
    sizes = [len(item) if isinstance(item, list) else 0 for item in ins]

    def body(*refs):
        args, at = [], 0
        for size in sizes:
            args.append(Stack(refs[at : at + size]) if size else refs[at])
            at += max(size, 1)
        last = at + waits + len(outs) - mark
        kernel(*args, *refs[at + waits : last], *refs[last + mark :])
        if mark:
            refs[last][...] = jnp.zeros((8, 128), f32)

    def full(shape):
        return pl.BlockSpec(tuple(shape), lambda i: (0,) * len(shape))

    if grid is None:
        grid = (1,)
    given = list(in_specs) if in_specs is not None else [None] * len(ins)
    specs, flat, start = [], [], []
    for item, spec, size in zip(ins, given, sizes):
        start.append(len(flat))
        if spec is None:
            spec = full((item[0] if size else item).shape)
        elif size:
            shape = spec.block_shape
            spec = pl.BlockSpec((shape[0] // size,) + tuple(shape[1:]), spec.index_map)
        specs += [spec] * max(size, 1)
        flat += item if size else [item]
    ins = flat
    if out_specs is None:
        out_specs = [full(shape) for shape, _ in outs]
    else:
        out_specs = list(out_specs) + [pl.BlockSpec((8, 128), lambda i: (0, 0))] * mark
    made = pl.pallas_call(
        body,
        in_specs=specs + [pl.BlockSpec(memory_space=pl.ANY)] * waits,
        out_specs=out_specs,
        out_shape=[jax.ShapeDtypeStruct(shape, dtype) for shape, dtype in outs],
        scratch_shapes=list(scratch),
        input_output_aliases={start[i]: o for i, o in (aliases or {}).items()},
        compiler_params=pltpu.CompilerParams(vmem_limit_bytes=room << 20),
        cost_estimate=pl.CostEstimate(flops=0, bytes_accessed=0, transcendentals=0),
        name=name,
        grid=grid,
    )(*ins, *after)
    if not mark:
        return list(made)
    for array in made[:-1]:
        MARKS[id(array)] = (array, made[-1])
    return list(made[:-1])


SMEM_SPEC = pl.BlockSpec(memory_space=pltpu.SMEM)


def moments(rows):
    centred = rows - jnp.mean(rows, axis=1, keepdims=True)
    inverse = lax.rsqrt(jnp.mean(centred * centred, axis=1, keepdims=True) + eps_norm)
    return centred * inverse, inverse


def back(weighted, normed, inverse):
    first_mean = jnp.mean(weighted, axis=1, keepdims=True)
    second_mean = jnp.mean(weighted * normed, axis=1, keepdims=True)
    return inverse * (weighted - first_mean - normed * second_mean)


def wide(ref):
    return ref[...].astype(f32)


def cut(shape):
    return [((shape[0] // PIECES,) + tuple(shape[1:]), bf16)] * PIECES


def put(refs, value):
    rows = value.shape[0] // len(refs)
    for i, ref in enumerate(refs):
        ref[...] = value[i * rows : (i + 1) * rows].astype(bf16)


def take(items, count):
    return [items.pop(0) for _ in range(count)]


def add_up(parts, name, after=()):
    shape = parts[0].shape

    def kernel(*refs):
        total = wide(refs[0])
        for ref in refs[1:-1]:
            total = total + wide(ref)
        refs[-1][...] = total.astype(bf16)

    return run(kernel, [(shape, bf16)], parts, after, name)[0]


def total_of(refs):
    total = wide(refs[0])
    for ref in refs[1:]:
        total = total + wide(ref)
    return total


def gain_row(ref, index):
    return ref[index : index + 1, :]


def put_edge(ref, who, value):
    value = value.astype(f32)
    ref[...] = jnp.where(who // 2 == 0, value[-MARGIN:], value[:MARGIN]).astype(bf16)


def norm_rows(
    resid, parts, factor, gains, index, name, after=(), keep=True, low=False, also=None, edge=None
):
    shape = resid.shape
    count = len(parts)
    extra = ([also] if also is not None else []) + ([edge] if edge is not None else [])
    ins = [resid, gains] + list(parts) + extra
    outs = [(shape, bf16)] + cut(shape) + [(shape, f32)] * keep + [(shape, bf16)] * low
    outs = outs + [(shape, bf16)] * (also is not None)
    outs = outs + [((MARGIN, shape[1]), bf16)] * (edge is not None)

    def kernel(resid_ref, gain_ref, *refs):
        refs = list(refs)
        part_refs = take(refs, count)
        also_ref = take(refs, also is not None)
        edge_ref = take(refs, edge is not None)
        rows = wide(resid_ref)
        if count:
            rows = rows + factor * total_of(part_refs)
        normed = (moments(rows)[0] * gain_row(gain_ref, index)).astype(bf16)
        refs.pop(0)[...] = normed
        put(take(refs, PIECES), normed)
        if keep:
            refs.pop(0)[...] = rows
        if low:
            refs.pop(0)[...] = rows.astype(bf16)
        if also_ref:
            refs.pop(0)[...] = also_ref[0][...].astype(bf16)
        if edge_ref:
            put_edge(refs.pop(0), edge_ref[0][0], normed)

    specs = [None] * (2 + count + (also is not None)) + [SMEM_SPEC] * (edge is not None)
    made = run(kernel, outs, ins, after, name, in_specs=specs)
    return [(made[0], made[1 : 1 + PIECES])] + made[1 + PIECES :]


def norm_last(resid, parts, gains, upper, who, k, length, name, full, after=()):
    shape = resid.shape
    count = len(parts)
    outs = [(shape, bf16)] + cut(shape)
    if full:
        outs = outs + [(shape, f32), (shape, f32), ((8, shape[1]), f32)]

    def kernel(who_ref, length_ref, resid_ref, gain_ref, upper_ref, *refs):
        refs = list(refs)
        rows = wide(resid_ref) + 0.5 * total_of(take(refs, count))
        gain = gain_row(gain_ref, 4)
        normed, inverse = moments(rows)
        begin = (who_ref[0] ^ (2 * k)) * shape[0]
        place = lax.broadcasted_iota(jnp.int32, (shape[0], 1), 0) + begin
        valid = (place < length_ref[0]).astype(f32)
        seen = wide(upper_ref) * valid
        grad = back(seen * gain, normed, inverse)
        rounded = (0.5 * grad).astype(bf16)
        refs.pop(0)[...] = rounded
        put(take(refs, PIECES), rounded)
        if full:
            refs.pop(0)[...] = grad
            refs.pop(0)[...] = normed * gain * valid
            refs.pop(0)[...] = jnp.broadcast_to(
                jnp.sum(seen * normed, axis=0, keepdims=True), (8, shape[1])
            )

    ins = [who, length, resid, gains, upper] + list(parts)
    specs = [SMEM_SPEC, SMEM_SPEC] + [None] * (3 + count)
    made = run(kernel, outs, ins, after, name, in_specs=specs)
    return [(made[0], made[1 : 1 + PIECES])] + made[1 + PIECES :]


def norm_grad(
    rows_in, parts, gains, index, grad, name, after=(), factor=None, keep=True, sums=True, edge=None
):
    shape = rows_in.shape
    count = len(parts)
    outs = ([(shape, bf16)] + cut(shape)) if factor is not None else []
    outs = outs + [(shape, f32)] * keep + [((8, shape[1]), f32)] * sums
    outs = outs + [((MARGIN, shape[1]), bf16)] * (edge is not None)

    def kernel(rows_ref, gain_ref, grad_ref, *refs):
        refs = list(refs)
        total = total_of(take(refs, count))
        edge_ref = take(refs, edge is not None)
        normed, inverse = moments(wide(rows_ref))
        result = wide(grad_ref) + back(total * gain_row(gain_ref, index), normed, inverse)
        if factor is not None:
            rounded = (factor * result).astype(bf16)
            refs.pop(0)[...] = rounded
            put(take(refs, PIECES), rounded)
        if keep:
            refs.pop(0)[...] = result
        if sums:
            refs.pop(0)[...] = jnp.broadcast_to(
                jnp.sum(total * normed, axis=0, keepdims=True), (8, shape[1])
            )
        if edge_ref:
            put_edge(refs.pop(0), edge_ref[0][0], rounded)

    ins = [rows_in, gains, grad] + list(parts) + ([edge] if edge is not None else [])
    specs = [None] * (3 + count) + [SMEM_SPEC] * (edge is not None)
    made = run(kernel, outs, ins, after, name, in_specs=specs)
    if factor is None:
        return made
    return [(made[0], made[1 : 1 + PIECES])] + made[1 + PIECES :]


def add_stats(value, others, channels, name, after=()):
    cols = value.shape[1]
    ny = cols // channels if channels else 0

    def kernel(*refs):
        total = refs[0][...]
        for k, ref in enumerate(refs[1:-1], 1):
            if channels:
                total = total + jnp.concatenate(
                    [ref[:, (r ^ k) * channels : ((r ^ k) + 1) * channels] for r in range(ny)], axis=1
                )
            else:
                total = total + ref[...]
        refs[-1][...] = total

    return run(kernel, [(value.shape, f32)], [value] + list(others), after, name)[0]


def tile_of(total, most):
    return most if total % most == 0 else total


def feed(own, mate, weights, name, after=()):
    rows, width = own.shape
    hidden = weights.shape[2]
    tile = tile_of(hidden, 1024)
    steps = hidden // tile

    def kernel(own_ref, mate_ref, in_ref, out_ref, p_own, *rest):
        *p_mate, pre, hid, seen = rest[: PIECES + 3]
        acc = rest[PIECES + 3] if steps > 1 else None
        step = pl.program_id(0)
        both = jnp.concatenate([own_ref[...], mate_ref[...]], axis=0)
        seen[...] = both
        value = nn(both, in_ref[0])
        act = (value / (1.0 + jnp.exp(-value))).astype(bf16)
        pre[...] = value.astype(bf16)
        hid[...] = act
        part = nt(act, out_ref[0])
        if steps == 1:
            p_own[...] = part[:rows].astype(bf16)
            put(p_mate, part[rows:])
            return

        @pl.when(step == 0)
        def _():
            acc[...] = part

        @pl.when(step > 0)
        def _():
            acc[...] += part

        @pl.when(step == steps - 1)
        def _():
            p_own[...] = acc[:rows].astype(bf16)
            put(p_mate, acc[rows:])

    fixed = pl.BlockSpec((rows, width), lambda i: (0, 0))
    quarter = [pl.BlockSpec((rows // PIECES, width), lambda i: (0, 0))] * PIECES
    cols = pl.BlockSpec((2 * rows, tile), lambda i: (0, i))
    weight = [pl.BlockSpec((1, width, tile), lambda i, m=m: (m, 0, i)) for m in range(2)]
    return run(
        kernel,
        [((rows, width), bf16)] + cut((rows, width)) + [((2 * rows, hidden), bf16)] * 2 + [((2 * rows, width), bf16)],
        [own, mate, weights, weights],
        after,
        name,
        grid=(steps,),
        in_specs=[fixed, fixed] + weight,
        out_specs=[fixed] + quarter + [cols, cols, pl.BlockSpec((2 * rows, width), lambda i: (0, 0))],
        scratch=[pltpu.VMEM((2 * rows, width), f32)] if steps > 1 else (),
        room=28,
        work=8 * rows * width * hidden,
    )


def feed_grad(own, mate, pre, weights, name, after=()):
    rows, width = own.shape
    hidden = weights.shape[2]
    tile = tile_of(hidden, 1024)
    steps = hidden // tile

    def kernel(own_ref, mate_ref, pre_ref, in_ref, out_ref, p_own, *rest):
        *p_mate, down, seen = rest[: PIECES + 2]
        acc = rest[PIECES + 2] if steps > 1 else None
        step = pl.program_id(0)
        both = jnp.concatenate([own_ref[...], mate_ref[...]], axis=0)
        seen[...] = both
        value = nn(both, out_ref[0])
        preact = wide(pre_ref)
        logistic = 1.0 / (1.0 + jnp.exp(-preact))
        slope = logistic * (1.0 + preact * (1.0 - logistic))
        grad = (value * slope).astype(bf16)
        down[...] = grad
        part = nt(grad, in_ref[0])
        if steps == 1:
            p_own[...] = part[:rows].astype(bf16)
            put(p_mate, part[rows:])
            return

        @pl.when(step == 0)
        def _():
            acc[...] = part

        @pl.when(step > 0)
        def _():
            acc[...] += part

        @pl.when(step == steps - 1)
        def _():
            p_own[...] = acc[:rows].astype(bf16)
            put(p_mate, acc[rows:])

    fixed = pl.BlockSpec((rows, width), lambda i: (0, 0))
    quarter = [pl.BlockSpec((rows // PIECES, width), lambda i: (0, 0))] * PIECES
    cols = pl.BlockSpec((2 * rows, tile), lambda i: (0, i))
    weight = [pl.BlockSpec((1, width, tile), lambda i, m=m: (m, 0, i)) for m in range(2)]
    return run(
        kernel,
        [((rows, width), bf16)] + cut((rows, width)) + [((2 * rows, hidden), bf16), ((2 * rows, width), bf16)],
        [own, mate, pre, weights, weights],
        after,
        name,
        grid=(steps,),
        in_specs=[fixed, fixed, cols] + weight,
        out_specs=[fixed] + quarter + [cols, pl.BlockSpec((2 * rows, width), lambda i: (0, 0))],
        scratch=[pltpu.VMEM((2 * rows, width), f32)] if steps > 1 else (),
        room=28,
        work=8 * rows * width * hidden,
    )


def qkv_rows(own, mate, weights, k, total, held, name, after=()):
    rows, width = own.shape
    cols = weights.shape[2]

    def kernel(own_ref, mate_ref, w_ref, *refs):
        both = jnp.concatenate([own_ref[...], mate_ref[...]], axis=0)
        refs[-1][...] = both
        refs[-2][0] = nn(both, w_ref[0]).astype(bf16)

    fixed = pl.BlockSpec((rows, width), lambda i: (0, 0))
    quarter = [pl.BlockSpec((rows // PIECES, width), lambda i: (0, 0))] * PIECES
    ins = [own, mate, weights] + ([held] if held is not None else [])
    specs = [fixed, fixed, pl.BlockSpec((1, width, cols), lambda i: (i, 0, 0))]
    specs = specs + [pl.BlockSpec(memory_space=pl.ANY)] * (held is not None)
    return run(
        kernel,
        [((3, total, cols), bf16), ((2 * rows, width), bf16)],
        ins,
        after,
        name,
        grid=(3,),
        in_specs=specs,
        out_specs=[
            pl.BlockSpec((1, 2 * rows, cols), lambda i: (i, k, 0)),
            pl.BlockSpec((2 * rows, width), lambda i: (0, 0)),
        ],
        work=12 * rows * width * cols,
        aliases={3: 0} if held is not None else None,
    )


def heads_rows(own, mate, weight, k, total, held, name, after=()):
    rows, width = own.shape
    cols = weight.shape[1]

    def kernel(own_ref, mate_ref, w_ref, *refs):
        both = jnp.concatenate([own_ref[...], mate_ref[...]], axis=0)
        refs[-1][...] = both
        refs[-2][...] = nn(both, w_ref[...]).astype(bf16)

    fixed = pl.BlockSpec((rows, width), lambda i: (0, 0))
    quarter = [pl.BlockSpec((rows // PIECES, width), lambda i: (0, 0))] * PIECES
    ins = [own, mate, weight] + ([held] if held is not None else [])
    specs = [fixed, fixed, pl.BlockSpec((width, cols), lambda i: (0, 0))]
    specs = specs + [pl.BlockSpec(memory_space=pl.ANY)] * (held is not None)
    return run(
        kernel,
        [((total, cols), bf16), ((2 * rows, width), bf16)],
        ins,
        after,
        name,
        grid=(1,),
        in_specs=specs,
        out_specs=[
            pl.BlockSpec((2 * rows, cols), lambda i: (k, 0)),
            pl.BlockSpec((2 * rows, width), lambda i: (0, 0)),
        ],
        work=4 * rows * width * cols,
        aliases={3: 0} if held is not None else None,
    )


def out_rows(values, weight, k, rows, name, after=()):
    width, cols = weight.shape

    def kernel(value_ref, w_ref, p_own, *p_mate):
        part = nt(value_ref[...], w_ref[...])
        p_own[...] = part[:rows].astype(bf16)
        put(p_mate, part[rows:])

    fixed = pl.BlockSpec((rows, width), lambda i: (0, 0))
    quarter = [pl.BlockSpec((rows // PIECES, width), lambda i: (0, 0))] * PIECES
    return run(
        kernel,
        [((rows, width), bf16)] + cut((rows, width)),
        [values, weight],
        after,
        name,
        grid=(1,),
        in_specs=[
            pl.BlockSpec((2 * rows, cols), lambda i: (k, 0)),
            pl.BlockSpec((width, cols), lambda i: (0, 0)),
        ],
        out_specs=[fixed] + quarter,
        work=4 * rows * width * cols,
    )


def members_rows(members, weights, k, rows, name, after=()):
    width, cols = weights.shape[1:]

    def kernel(value_ref, w_ref, p_own, *p_mate):
        part = nt(value_ref[0], w_ref[0])
        for m in range(1, 3):
            part = part + nt(value_ref[m], w_ref[m])
        p_own[...] = part[:rows].astype(bf16)
        put(p_mate, part[rows:])

    fixed = pl.BlockSpec((rows, width), lambda i: (0, 0))
    quarter = [pl.BlockSpec((rows // PIECES, width), lambda i: (0, 0))] * PIECES
    return run(
        kernel,
        [((rows, width), bf16)] + cut((rows, width)),
        [members, weights],
        after,
        name,
        grid=(1,),
        in_specs=[
            pl.BlockSpec((3, 2 * rows, cols), lambda i: (0, k, 0)),
            pl.BlockSpec((3, width, cols), lambda i: (0, 0, 0)),
        ],
        out_specs=[fixed] + quarter,
        work=12 * rows * width * cols,
    )


def part(array, m=None, begin=0, end=None):
    value = array[...] if m is None else array[m]
    return value if end is None else value[:, begin:end]


def plain(item):
    return item[0] if isinstance(item, tuple) else item


def spot(item):
    return item[1:] if isinstance(item, tuple) else ()


def span(item):
    return item[3] - item[2] if len(spot(item)) > 1 else plain(item).shape[-1]


def lay_out(jobs):
    plan, ins = [], []
    for left, rights in jobs:
        picks = [[spot(item) for item in right] for right in rights]
        plan.append((len(left), picks, sum(span(right[0]) for right in rights)))
        ins = ins + list(left) + [plain(item) for right in rights for item in right]
    return plan, ins


def sides(plan, refs):
    at = 0
    for n_left, picks, cols in plan:
        left = refs[at : at + n_left]
        at = at + n_left
        columns = []
        for places in picks:
            values = []
            for place in places:
                values.append(part(refs[at], *place))
                at = at + 1
            columns.append(values[0] if len(values) == 1 else jnp.concatenate(values, axis=0))
        yield left, columns[0] if len(columns) == 1 else jnp.concatenate(columns, axis=1), cols


def outer(jobs, name, after=(), sums=()):
    plan, ins = lay_out(jobs)
    total = sum(cols for _, _, cols in plan) + sum(parts[0].shape[1] for parts in sums)
    width = jobs[0][0][0].shape[1]
    products = len(ins)
    ins = ins + [array for parts in sums for array in parts]

    def kernel(*refs):
        column = 0
        for left, rights, cols in sides(plan, refs):
            rows = [ref[...] for ref in left]
            rows = rows[0] if len(rows) == 1 else jnp.concatenate(rows, axis=0)
            refs[-1][:, column : column + cols] = tn(rows, rights).astype(bf16)
            column = column + cols
        at = products
        for parts in sums:
            value = total_of(refs[at : at + len(parts)])
            refs[-1][:, column : column + parts[0].shape[1]] = value.astype(bf16)
            at = at + len(parts)
            column = column + parts[0].shape[1]

    work = sum(2 * width * cols * sum(r.shape[0] for r in left) for (left, _), (_, _, cols) in zip(jobs, plan))
    return run(kernel, [((width, total), bf16)], ins, after, name, room=36, work=work, mark=True)[0]


def outer_halves(links, jobs, turn, name, after=()):
    offsets, masks = links.offsets(turn)
    width = jobs[0][0][0].shape[1]
    share = width // links.dp
    me = lax.axis_index("dp").reshape(1).astype(jnp.int32)

    plan, ins = lay_out(jobs)
    ins = [me] + ins
    total = sum(cols for _, _, cols in plan)
    half = len(offsets)

    def kernel(me_ref, *refs):
        who = me_ref[0]
        sent_ref, kept_ref = refs[-2], refs[-1]
        column = 0
        for left, rights, cols in sides(plan, refs):
            for flip, dest in ((masks[0], sent_ref), (0, kept_ref)):
                picked = []
                for off in offsets:
                    where = pl.ds(pl.multiple_of((who ^ off ^ flip) * share, 128), share)
                    parts = [ref[:, where] for ref in left]
                    picked.append(parts[0] if len(parts) == 1 else jnp.concatenate(parts, axis=0))
                picked = picked[0] if half == 1 else jnp.concatenate(picked, axis=1)
                dest[:, column : column + cols] = tn(picked, rights).astype(bf16)
            column = column + cols

    return run(
        kernel,
        [((half * share, total), bf16)] * 2,
        ins,
        after,
        name,
        in_specs=[SMEM_SPEC] + [None] * (len(ins) - 1),
        room=24,
        work=2 * SLOT * width * total,
        mark=True,
    )


def halve_all(pairs, name, after=()):
    shapes = [(kept.shape[0] // 2, kept.shape[1]) for kept, _ in pairs]
    count = len(pairs)

    def kernel(*refs):
        for i in range(count):
            total = wide(refs[2 * i]) + wide(refs[2 * i + 1])
            half = shapes[i][0]
            refs[2 * count + 2 * i][...] = total[half:].astype(bf16)
            refs[2 * count + 2 * i + 1][...] = total[:half].astype(bf16)

    outs = [(shape, bf16) for shape in shapes for _ in range(2)]
    made = run(kernel, outs, [array for pair in pairs for array in pair], after, name, mark=True)
    return [(made[2 * i], made[2 * i + 1]) for i in range(count)]


def halves(ref_own, ref_mate, c):
    own, mate = ref_own[...], ref_mate[...]
    first = jnp.where(c == 0, own, mate)
    second = jnp.where(c == 0, mate, own)
    return first, second


def shift_rows(value, offset):
    if offset == 0:
        return value
    return pltpu.roll(value, (-offset) % value.shape[0], 0)


def place_mask(count, y, length):
    place = lax.broadcasted_iota(jnp.int32, (count + 2 * MARGIN, 1), 0) + (y * count - MARGIN)
    return ((place >= 0) & (place < length)).astype(f32)


def bordered(own_ref, mate_ref, before, after, who, ny):
    y, c = who // 2, who % 2
    first, second = halves(own_ref, mate_ref, c)
    above = wide(before[0])
    for ref in before[1:]:
        above = above + wide(ref)
    below = wide(after[0])
    for ref in after[1:]:
        below = below + wide(ref)
    above = jnp.where(y > 0, above, 0.0).astype(bf16)
    below = jnp.where(y < ny - 1, below, 0.0).astype(bf16)
    return jnp.concatenate([above, first, second, below], axis=0)


def conv_mix(ny, who, length, own, mate, before, after_rows, weights, taps, name, after=()):
    rows, width = own.shape
    cols = taps.shape[1]
    count = 2 * rows
    lo, hi = MARGIN, MARGIN + count
    n_before = len(before)

    def kernel(who_ref, len_ref, own_ref, mate_ref, w0, w1, taps_ref, *refs):
        rows_in = bordered(own_ref, mate_ref, refs[:n_before], refs[n_before:-5], who_ref[0], ny)
        lin_ref, gate_ref, mix_ref, tally_ref, seen_ref = refs[-5:]
        seen_ref[...] = jnp.concatenate([own_ref[...], mate_ref[...]], axis=0)
        valid = place_mask(count, who_ref[0] // 2, len_ref[0])
        linear = nn(rows_in, w0[...])
        gating = 1.0 / (1.0 + jnp.exp(-nn(rows_in, w1[...])))
        lin_ref[...] = linear
        gate_ref[...] = gating
        glu = linear * gating * valid
        mixture = taps_ref[0:1, :] * shift_rows(glu, -2)
        for j in range(1, KERNEL):
            mixture = mixture + taps_ref[j : j + 1, :] * shift_rows(glu, j - 2)
        mix_ref[...] = mixture
        inside = (valid * mixture)[lo:hi]
        tally_ref[...] = jnp.concatenate(
            [
                jnp.sum(inside, axis=0, keepdims=True),
                jnp.sum(inside * mixture[lo:hi], axis=0, keepdims=True),
                jnp.broadcast_to(jnp.sum(valid[lo:hi], axis=0, keepdims=True), (1, cols)),
                jnp.zeros((5, cols), f32),
            ],
            axis=0,
        )

    ins = [who, length, own, mate, weights[0], weights[1], taps] + list(before) + list(after_rows)
    shape = (count + 2 * MARGIN, cols)
    return run(
        kernel,
        [(shape, f32)] * 3 + [((8, cols), f32), ((count, width), bf16)],
        ins,
        after,
        name,
        in_specs=[SMEM_SPEC, SMEM_SPEC] + [None] * (len(ins) - 2),
        room=28,
        work=4 * count * width * cols,
    )


def batch_terms(tally_ref):
    count = tally_ref[2:3, :]
    mean = tally_ref[0:1, :] / count
    var = tally_ref[1:2, :] / count - mean * mean
    return count, mean, var, lax.rsqrt(var + eps_norm)


def conv_out(who, mixture, tallies, affine, running, weight, rows, name, after=()):
    width, cols = weight.shape
    channels = running.shape[1]
    lo, mid, hi = MARGIN, MARGIN + rows, MARGIN + 2 * rows

    def kernel(who_ref, mix_ref, tally_ref, affine_ref, run_ref, w_ref, act_ref, p_own, *rest):
        *p_mate, new_ref = rest
        c = who_ref[0] % 2
        count, mean, var, inverse = batch_terms(tally_ref)
        own = pl.ds(pl.multiple_of(lo + c * rows, 16), rows)
        mate = pl.ds(pl.multiple_of(lo + (1 - c) * rows, 16), rows)
        mixture = jnp.concatenate([mix_ref[own, :], mix_ref[mate, :]], axis=0)
        shifted = (mixture - mean) * inverse * affine_ref[KERNEL : KERNEL + 1, :] + affine_ref[KERNEL + 1 : KERNEL + 2, :]
        active = (shifted / (1.0 + jnp.exp(-shifted))).astype(bf16)
        act_ref[...] = active
        part = nt(active, w_ref[...])
        p_own[...] = part[:rows].astype(bf16)
        put(p_mate, part[rows:])
        grown = var * count / (count - 1.0)
        new_ref[...] = (1.0 - momentum) * run_ref[...] + momentum * jnp.concatenate(
            [mean[:, :channels], grown[:, :channels]], axis=0
        )

    return run(
        kernel,
        [((2 * rows, cols), bf16), ((rows, width), bf16)] + cut((rows, width)) + [(running.shape, f32)],
        [who, mixture, tallies, affine, running, weight],
        after,
        name,
        in_specs=[SMEM_SPEC] + [None] * 5,
        room=24,
        work=4 * rows * width * cols,
    )


def conv_shift_grad(ny, who, length, own, mate, before, after_rows, mixture, tallies, affine, weight, name, after=()):
    rows, width = own.shape
    cols = weight.shape[1]
    count = 2 * rows
    lo, hi = MARGIN, MARGIN + count
    n_before = len(before)

    def kernel(who_ref, len_ref, own_ref, mate_ref, mix_ref, tally_ref, affine_ref, w_ref, *refs):
        rows_in = bordered(own_ref, mate_ref, refs[:n_before], refs[n_before:-3], who_ref[0], ny)
        dz_ref, out_ref, seen_ref = refs[-3:]
        seen_ref[...] = jnp.concatenate([own_ref[...], mate_ref[...]], axis=0)
        valid = place_mask(count, who_ref[0] // 2, len_ref[0])
        _, mean, _, inverse = batch_terms(tally_ref)
        centred = (mix_ref[...] - mean) * inverse
        shifted = centred * affine_ref[KERNEL : KERNEL + 1, :] + affine_ref[KERNEL + 1 : KERNEL + 2, :]
        logistic = 1.0 / (1.0 + jnp.exp(-shifted))
        slope = logistic * (1.0 + shifted * (1.0 - logistic))
        grad = jnp.where(valid > 0.0, nn(rows_in, w_ref[...]) * slope, 0.0)
        dz_ref[...] = grad
        inner = grad[lo:hi]
        out_ref[...] = jnp.concatenate(
            [
                jnp.sum(inner * centred[lo:hi], axis=0, keepdims=True),
                jnp.sum(inner, axis=0, keepdims=True),
                jnp.zeros((6, cols), f32),
            ],
            axis=0,
        )

    ins = [who, length, own, mate, mixture, tallies, affine, weight] + list(before) + list(after_rows)
    return run(
        kernel,
        [(mixture.shape, f32), ((8, cols), f32), ((count, width), bf16)],
        ins,
        after,
        name,
        in_specs=[SMEM_SPEC, SMEM_SPEC] + [None] * (len(ins) - 2),
        room=28,
        work=4 * count * width * cols,
    )


def conv_in_grad(who, length, dz, mixture, tallies, sums, affine, taps, linear, gating, weights, rows, name, after=()):
    width, cols = weights[0].shape
    count = 2 * rows
    lo, mid, hi = MARGIN, MARGIN + rows, MARGIN + count

    def kernel(who_ref, len_ref, dz_ref, mix_ref, tally_ref, sum_ref, affine_ref, taps_ref, lin_ref, gate_ref, w0, w1, dl_ref, dg_ref, p_own, *rest):
        *p_mate, tap_ref = rest
        c = who_ref[0] % 2
        valid = place_mask(count, who_ref[0] // 2, len_ref[0])
        total, mean, _, inverse = batch_terms(tally_ref)
        centred = (mix_ref[...] - mean) * inverse
        shrink = affine_ref[KERNEL : KERNEL + 1, :] * inverse
        mixed = (sum_ref[1:2, :] + centred * sum_ref[0:1, :]) / total
        grad_mix = jnp.where(valid > 0.0, shrink * (dz_ref[...] - mixed), 0.0)
        grad_glu = taps_ref[0:1, :] * shift_rows(grad_mix, 2)
        for j in range(1, KERNEL):
            grad_glu = grad_glu + taps_ref[j : j + 1, :] * shift_rows(grad_mix, 2 - j)
        linear = lin_ref[...]
        gating = gate_ref[...]
        glu = linear * gating * valid
        inner = grad_mix[lo:hi]
        tap_ref[...] = jnp.concatenate(
            [
                jnp.sum(inner * shift_rows(glu, j - 2)[lo:hi], axis=0, keepdims=True)
                for j in range(KERNEL)
            ]
            + [jnp.zeros((8 - KERNEL, cols), f32)],
            axis=0,
        )
        held = grad_glu * valid * gating
        grad_linear = held.astype(bf16)
        grad_gate = (held * linear * (1.0 - gating)).astype(bf16)

        def turned(value):
            first, second = value[lo:mid], value[mid:hi]
            return jnp.concatenate(
                [jnp.where(c == 0, first, second), jnp.where(c == 0, second, first)], axis=0
            )

        grad_linear = turned(grad_linear)
        grad_gate = turned(grad_gate)
        dl_ref[...] = grad_linear
        dg_ref[...] = grad_gate
        part = nt(grad_linear, w0[...]) + nt(grad_gate, w1[...])
        p_own[...] = part[:rows].astype(bf16)
        put(p_mate, part[rows:])

    return run(
        kernel,
        [((count, cols), bf16)] * 2 + [((rows, width), bf16)] + cut((rows, width)) + [((8, cols), f32)],
        [who, length, dz, mixture, tallies, sums, affine, taps, linear, gating, weights[0], weights[1]],
        after,
        name,
        in_specs=[SMEM_SPEC, SMEM_SPEC] + [None] * 10,
        room=32,
        work=4 * count * width * cols,
    )


class Links:
    def __init__(self, dp, tensor):
        self.dp, self.tensor, self.ny = dp, tensor, tensor // 2
        self.masks = [1 << bit for bit in range(dp.bit_length() - 1)]

    def core(self, value):
        return lax.ppermute(value, "tensor", [(i, i ^ 1) for i in range(self.tensor)])

    def mate(self, pieces):
        return [self.core(piece) for piece in pieces]

    def chip(self, value, k):
        return lax.ppermute(value, "tensor", [(i, i ^ (2 * k)) for i in range(self.tensor)])

    def group(self, value, mask):
        return lax.ppermute(value, "dp", [(i, i ^ mask) for i in range(self.dp)])

    def scatter_grad(self, value):
        return lax.psum_scatter(value, "dp", scatter_dimension=0, tiled=True)

    def sum_group(self, value, name):
        for mask in self.masks:
            value = add_stats(value, [self.group(value, mask)], 0, name)
        return value

    def sum_stats(self, value, channels, name, after=()):
        others = [self.chip(value, k) for k in range(1, self.ny)]
        return self.sum_group(add_stats(value, others, channels, name, after), name)

    def offsets(self, turn):
        masks = list(self.masks)
        if turn:
            masks[:2] = masks[1::-1]
        offsets = [0]
        for mask in masks[:0:-1]:
            offsets = offsets + [off ^ mask for off in offsets]
        return offsets, masks

    def borders(self, own, mate, edge):
        if self.ny == 2:
            straight = lax.ppermute(edge, "tensor", [(1, 3), (2, 0)])
            across = lax.ppermute(edge, "tensor", [(1, 2), (2, 1)])
            return [straight, across], [straight, across]
        c = lax.axis_index("tensor") % 2
        mate = jnp.concatenate(mate)
        head = jnp.where(c == 0, own, mate)[:MARGIN]
        foot = jnp.where(c == 0, mate, own)[own.shape[0] - MARGIN :]
        down = [(i, i + 2) for i in range(self.tensor - 2)]
        up = [(i + 2, i) for i in range(self.tensor - 2)]
        return [lax.ppermute(foot, "tensor", down)], [lax.ppermute(head, "tensor", up)]


class Pieces:
    def __init__(self, links, pieces, name):
        self.links, self.name = links, name
        self.count = len(pieces)
        self.masks = [links.offsets(i % 2)[1] for i in range(self.count)]
        self.kept = [kept for _, kept in pieces]
        self.at = 0
        self.send([sent for sent, _ in pieces])

    def send(self, sent):
        self.came = [self.links.group(sent[i], self.masks[i][self.at]) for i in range(self.count)]
        self.at += 1

    def step(self, after=()):
        if self.at < len(self.links.masks):
            made = halve_all(list(zip(self.kept, self.came)), self.name + "_half", after)
            self.kept = [kept for _, kept in made]
            self.send([sent for sent, _ in made])
        return self.kept[0]

    def finish(self):
        while self.at < len(self.links.masks):
            self.step()
        return [array for pair in zip(self.kept, self.came) for array in pair]


def finish_one(outs_of, ins_of, width_in, name):
    ins = outs_of + ins_of
    share = ins[0].shape[0]

    def kernel(*refs):
        out = refs[-1]
        parts = [wide(refs[2 * i]) + wide(refs[2 * i + 1]) for i in range(4)]
        out[1] = jnp.concatenate(parts[:2], axis=1)
        out[0] = jnp.concatenate(parts[2:], axis=1)

    return run(kernel, [((2, share, width_in), f32)], ins, (), name)[0]


def split_two(total, hidden, name, after=()):
    share = total.shape[0]

    def kernel(ref, out):
        for m in range(2):
            out[m] = wide(ref)[:, m * hidden : (m + 1) * hidden]

    return run(kernel, [((2, share, hidden), f32)], [total], after, name, mark=True)[0]


def split_heads(total, cols, channels, name):
    share = total.shape[0]

    def kernel(ref, three, one, conv):
        value = wide(ref)
        for m in range(3):
            three[m] = value[:, m * cols : (m + 1) * cols]
            at = 4 * cols + m * channels
            conv[m] = value[:, at : at + channels]
        one[...] = value[:, 3 * cols : 4 * cols]

    outs = [((3, share, cols), f32), ((share, cols), f32), ((3, share, channels), f32)]
    return run(kernel, outs, [total], (), name)


def pack_small(depthwise, bn_gain, bn_bias, name):
    channels = depthwise.shape[1]

    def kernel(taps, gain, bias, out):
        out[...] = jnp.concatenate(
            [taps[...], gain[...], bias[...], jnp.zeros((1, channels), f32)], axis=0
        )

    rows = [depthwise, bn_gain[None], bn_bias[None]]
    return run(kernel, [((8, channels), f32)], rows, (), name)[0]


def side_by_side(arrays, name):
    def kernel(*refs):
        refs[-1][...] = jnp.concatenate([ref[...] for ref in refs[:-1]], axis=1)

    shape = (arrays[0].shape[0], sum(array.shape[1] for array in arrays))
    return run(kernel, [(shape, f32)], arrays, (), name)[0]


def pack_sums(gains, table, name, after=()):
    width = gains[0].shape[1]
    each = width // 128

    def kernel(*refs):
        out = refs[-1]
        for g in range(5):
            for i in range(each):
                out[g * each + i : g * each + i + 1, :] = refs[g][0:1, i * 128 : (i + 1) * 128]
        out[5 * each :, :] = refs[5][...]

    return run(kernel, [((5 * each + 128, 128), f32)], list(gains) + [table], after, name)[0]


def with_taps(sums, taps, channels, name, after=()):
    def kernel(sum_ref, tap_ref, out):
        top = sums.shape[0]
        out[:top, :] = sum_ref[...]
        for i in range(channels // 128):
            out[top + 8 * i : top + 8 * i + 8, :] = tap_ref[:, i * 128 : (i + 1) * 128]

    rows = sums.shape[0] + 8 * (channels // 128)
    return run(kernel, [((rows, 128), f32)], [sums, taps], after, name)[0]


def unpack_sums(sums, bn_grads, width, channels, name):
    each = width // 128
    top = 5 * each + 128

    def kernel(sum_ref, bn_ref, gains, table, kernel_grad, gain_grad, bias_grad):
        for g in range(5):
            for i in range(each):
                gains[g : g + 1, i * 128 : (i + 1) * 128] = sum_ref[g * each + i : g * each + i + 1, :]
        table[...] = sum_ref[5 * each : 5 * each + REL, :]
        for i in range(channels // 128):
            at = top + 8 * i
            kernel_grad[:, i * 128 : (i + 1) * 128] = sum_ref[at : at + KERNEL, :]
        gain_grad[...] = bn_ref[0:1, :channels]
        bias_grad[...] = bn_ref[1:2, :channels]

    outs = [((5, width), f32), ((REL, 128), f32), ((KERNEL, channels), f32)] + [((1, channels), f32)] * 2
    return run(kernel, outs, [sums, bn_grads], (), name)


def own_share(weights, me, share, name, after=()):
    cols = weights.shape[2]

    def kernel(me_ref, ref, out):
        rows = pl.ds(pl.multiple_of(me_ref[0] * share, 16), share)
        for m in range(3):
            out[m * share : (m + 1) * share, :] = ref[m, rows, :]

    return run(
        kernel, [((3 * share, cols), bf16)], [me, weights], after, name, in_specs=[SMEM_SPEC, None]
    )[0]


def arrange(conv_proj, gathered, dp, name, after=()):
    _, width, channels = conv_proj.shape
    share = width // dp
    cols = channels * (1 + len(gathered))

    def kernel(own_ref, *refs):
        others, outs = refs[: len(gathered)], refs[len(gathered) :]
        for m in range(3):
            outs[m][:, :channels] = own_ref[m]
            for k, ref in enumerate(others):
                for b in range(dp):
                    at = (b * 3 + m) * share
                    outs[m][b * share : (b + 1) * share, (k + 1) * channels : (k + 2) * channels] = ref[
                        at : at + share, :
                    ]

    return run(kernel, [((width, cols), bf16)] * 3, [conv_proj] + gathered, after, name, mark=True)


def per_device(
    links,
    x_in,
    cotangent,
    lengths,
    norm_gains,
    ffn_first,
    attn_qkv,
    attn_out,
    rel_table,
    conv_proj,
    depthwise,
    bn_gain,
    bn_bias,
    running,
    ffn_second,
):
    MARKS.clear()
    ny = links.ny
    others = list(range(1, ny))
    rows, width = x_in.shape
    channels = bn_gain.shape[0]
    who = lax.axis_index("tensor").astype(jnp.int32).reshape(1)
    gains = norm_gains
    table = window_table(jnp.pad(rel_table, ((0, 128 - REL), (0, 0))))

    me = lax.axis_index("dp").astype(jnp.int32).reshape(1)
    share = width // links.dp
    halves_fit = share % 128 == 0
    small = pack_small(depthwise, bn_gain, bn_bias, "conv_small")
    small = side_by_side([small] + [links.chip(small, k) for k in others], "conv_small_all")

    def send_sums(parts, name, after=()):
        return add_up([parts[0], links.mate(parts[1])], name, after)

    def every(pieces):
        return [pieces[k] for k in range(ny)]

    def split(made):
        return (made[0], made[1 : 1 + PIECES]), made[1 + PIECES :]

    def all_parts(sums, k):
        return [sums[k]] + [links.chip(sums[k ^ j], j) for j in others]

    (normed, pieces), x_low = norm_rows(x_in, [], 0.0, gains, 0, "ln_in", keep=False, low=True)
    x_rows = [x_in] + [links.chip(x_low, k) for k in others]
    na_first, pre_first, hid_first, sums = {}, {}, {}, {}
    token = ()
    for k in range(ny):
        if k:
            ((normed, pieces),) = norm_rows(
                x_rows[k], [], 0.0, gains, 0, "ln_in", token + (small,), keep=False
            )
        if k == 1:
            piece = own_share(conv_proj, me, share, "conv_share", (normed,))
            gathered = [
                lax.all_gather(links.chip(piece, j), "dp", axis=0, tiled=True) for j in others
            ]
        parts, made = split(feed(normed, links.mate(pieces), ffn_first, "ffn_one"))
        pre_first[k], hid_first[k], na_first[k] = made
        sums[k] = send_sums(parts, "ffn_one_sum")
        token = (sums[k],)

    token = ()
    na_attn, first, qkv, cot_low = {}, {}, None, None
    for k in others + [0]:
        also = cotangent if k == 0 else None
        made = norm_rows(
            x_rows[k], all_parts(sums, k), 0.5, gains, 1, "ln_attn", token, also=also
        )
        (normed, pieces), first[k] = made[:2]
        if k == 0:
            cot_low = made[2]
        qkv, na_attn[k] = qkv_rows(normed, links.mate(pieces), attn_qkv, k, SLOT, qkv, "qkv")
        token = (qkv,)
    cot_rows = [cotangent] + [links.chip(cot_low, k) for k in others]
    heads_out, probs = attend(qkv, who, lengths, table, rows)
    token = tuple(cot_rows[1:])
    arrived = []
    for k in others:
        parts, _ = split(out_rows(heads_out, attn_out, k, rows, "out_proj", token))
        total = send_sums(parts, "out_sum")
        arrived.append(links.chip(total, k))
        token = (total,)
    conv_w = arrange(conv_proj, gathered, links.dp, "conv_weights", token)
    token = token + (conv_w[0],)
    parts, _ = split(out_rows(heads_out, attn_out, 0, rows, "out_proj", token))
    edge = who if ny == 2 else None
    made = norm_rows(
        first[0], [parts[0], links.mate(parts[1])] + arrived, 1.0, gains, 2, "ln_conv", edge=edge
    )
    (normed, pieces), after_attn = made[:2]

    mate = links.mate(pieces)
    before, after_rows = links.borders(normed, mate, made[-1])
    linear, gating, mixture, tallies, conv_in = conv_mix(
        ny, who, lengths, normed, mate, before, after_rows, conv_w, small, "conv_mix"
    )
    tallies = links.sum_stats(tallies, channels, "bn_sum")
    active, *made = conv_out(who, mixture, tallies, small, running, conv_w[2], rows, "conv_out")
    parts, (updated,) = split(made)
    (normed, pieces), after_conv, low = norm_rows(
        after_attn, [parts[0], links.mate(parts[1])], 1.0, gains, 3, "ln_ffn_two", low=True
    )

    x_rows = [after_conv] + [links.chip(low, k) for k in others]
    na_last, pre_last, hid_last, sums = {}, {}, {}, {}
    token = ()
    for k in range(ny):
        if k:
            ((normed, pieces),) = norm_rows(
                x_rows[k], [], 0.0, gains, 3, "ln_ffn_two", token, keep=False
            )
        parts, made = split(feed(normed, links.mate(pieces), ffn_second, "ffn_two"))
        pre_last[k], hid_last[k], na_last[k] = made
        sums[k] = send_sums(parts, "ffn_two_sum")
        token = (sums[k],)

    token = ()
    upper, down, arrived = {}, {}, []
    for k in others + [0]:
        made = norm_last(
            x_rows[k],
            all_parts(sums, k),
            gains,
            cot_rows[k],
            who,
            k,
            lengths,
            "ln_last",
            k == 0,
            token,
        )
        normed, pieces = made[0]
        if k == 0:
            grad, output, gain_five = made[1:]
        parts, made = split(
            feed_grad(normed, links.mate(pieces), pre_last[k], ffn_second, "ffn_two_grad")
        )
        down[k], upper[k] = made
        if k:
            total = send_sums(parts, "ffn_two_grad_sum")
            arrived.append(links.chip(total, k))
            token = (total,)
    made = norm_grad(
        after_conv,
        [parts[0], links.mate(parts[1])] + arrived,
        gains,
        3,
        grad,
        "back_ffn_two",
        factor=1.0,
        edge=edge,
    )
    (low, pieces), grad, gain_four = made[:3]

    mate = links.mate(pieces)
    before, after_rows = links.borders(low, mate, made[-1])
    dz, sums, conv_up = conv_shift_grad(
        ny, who, lengths, low, mate, before, after_rows, mixture, tallies, small, conv_w[2], "conv_dz"
    )
    two_sum = outer(
        [(every(na_last), [every(down)]), (every(upper), [every(hid_last)])], "ffn_two_w", (sums,)
    )
    def by_chip(left, rights, name, after):
        made = []
        for k in range(ny):
            spans = [[(right, None, k * channels, (k + 1) * channels)] for right in rights]
            made.append(outer([([left], spans)], name, after))
        return [made[0]] + [links.chip(made[k], k) for k in others]

    out_grad = by_chip(conv_up, [active], "conv_out_w", (two_sum,))
    bn_grads = links.sum_stats(sums, channels, "bn_grad_sum", (two_sum,))
    two_sum = links.scatter_grad(two_sum)
    grad_linear, grad_gate, *made = conv_in_grad(
        who, lengths, dz, mixture, tallies, bn_grads, small, small, linear, gating, conv_w, rows, "conv_din"
    )
    parts, (tap_grad,) = split(made)
    (low, pieces), grad, gain_three = norm_grad(
        after_attn, [parts[0], links.mate(parts[1])], gains, 2, grad, "back_conv", factor=1.0
    )

    g_rows = [low] + [links.chip(low, k) for k in others]
    in_grads = by_chip(conv_in, [grad_linear, grad_gate], "conv_in_w", (low,))
    token = (in_grads[0],)
    grad_heads = None
    upper_attn = {}
    for k in range(ny):
        mate = links.mate(pieces) if k == 0 else [links.core(g_rows[k])]
        grad_heads, upper_attn[k] = heads_rows(
            g_rows[k], mate, attn_out, k, SLOT, grad_heads, "dheads", token
        )
        token = (grad_heads,)
    members, table_grad = attend_back(qkv, grad_heads, probs, who, table, rows)
    token = ()
    sums = {}
    for k in range(ny):
        parts, _ = split(members_rows(members, attn_qkv, k, rows, "dqkv", token))
        sums[k] = send_sums(parts, "dqkv_sum")
        token = (sums[k],)
    heads_sum = outer(
        [
            (every(na_attn), [[(members, m)] for m in range(3)]),
            (every(upper_attn), [[heads_out]]),
        ],
        "attn_w",
        token,
        [in_grads, out_grad],
    )
    token = (heads_sum,)
    heads_sum = links.scatter_grad(heads_sum)

    upper, down, arrived = {}, {}, []
    for k in others + [0]:
        made = norm_grad(
            first[k],
            all_parts(sums, k),
            gains,
            1,
            grad if k == 0 else g_rows[k],
            "back_attn",
            token,
            factor=0.5,
            keep=k == 0,
            sums=k == 0,
        )
        normed, pieces = made[0]
        if k == 0:
            grad, gain_two = made[1:]
        parts, made = split(
            feed_grad(normed, links.mate(pieces), pre_first[k], ffn_first, "ffn_one_grad")
        )
        down[k], upper[k] = made
        if k:
            total = send_sums(parts, "ffn_one_grad_sum")
            arrived.append(links.chip(total, k))
            token = (total,)
    hidden = ffn_first.shape[2]
    half = hidden // 2
    token = (parts[0],)
    pairs = []
    if halves_fit:
        for left, right in ((every(upper), every(hid_first)), (every(na_first), every(down))):
            halves = []
            for turn in range(2):
                columns = [(r, None, turn * half, (turn + 1) * half) for r in right]
                halves.append(outer_halves(links, [(left, [columns])], turn, "ffn_one_w", token))
                token = (halves[-1][0],)
            pairs.append(Pieces(links, halves, "one"))
    else:
        first_sum = outer(
            [(every(na_first), [every(down)]), (every(upper), [every(hid_first)])], "ffn_one_w", token
        )
        token = (first_sum,)
        first_sum = links.scatter_grad(first_sum)
    for pair in pairs:
        token = (pair.step(token),)
    last_sum = split_two(two_sum, hidden, "two_end", token)
    grad_input, gain_one = norm_grad(
        x_in,
        [parts[0], links.mate(parts[1])] + arrived,
        gains,
        0,
        grad,
        "back_ffn_one",
        token + (last_sum,),
    )

    taps = add_stats(tap_grad, [links.chip(tap_grad, k) for k in others], channels, "taps_sum")
    bundle = pack_sums([gain_one, gain_two, gain_three, gain_four, gain_five], table_grad, "pack")
    bundle = add_stats(bundle, [links.core(bundle)], 0, "bundle_sum")
    for k in [1 << bit for bit in range(ny.bit_length() - 1)]:
        bundle = add_stats(bundle, [links.chip(bundle, k)], 0, "bundle_sum")
    token = (bundle,)
    for _ in links.masks[2:]:
        for pair in pairs:
            token = (pair.step(token),)
    bundle = with_taps(bundle, taps, channels, "pack_taps", token)
    for mask in links.masks:
        bundle = add_stats(bundle, [links.group(bundle, mask)], 0, "bundle_sum")
    norm_sums, table_sums, kernel_grad, gain_grad, bias_grad = unpack_sums(
        bundle, bn_grads, width, channels, "unpack"
    )
    if pairs:
        first_sum = finish_one(pairs[0].finish(), pairs[1].finish(), hidden, "one_end")
    else:
        first_sum = split_two(first_sum, hidden, "one_end")
    qkv_sum, out_sum, conv_sum = split_heads(heads_sum, attn_qkv.shape[2], channels, "heads_end")
    return (
        output,
        grad_input,
        norm_sums,
        first_sum,
        qkv_sum,
        out_sum,
        table_sums,
        conv_sum,
        kernel_grad,
        gain_grad.reshape(-1),
        bias_grad.reshape(-1),
        updated,
        last_sum,
    )


def solution(mesh):
    links = Links(mesh.shape["dp"], mesh.shape["tensor"])
    placed = (
        P(("dp", "tensor"), None),
        P(("dp", "tensor"), None),
        P("dp"),
        P(),
        P(None, None, "tensor"),
        P(None, None, "tensor"),
        P(None, "tensor"),
        P(),
        P(None, None, "tensor"),
        P(None, "tensor"),
        P("tensor"),
        P("tensor"),
        P(None, "tensor"),
        P(None, None, "tensor"),
    )
    return jax.shard_map(
        functools.partial(per_device, links),
        mesh=mesh,
        in_specs=placed,
        out_specs=(
            P(("dp", "tensor"), None),
            P(("dp", "tensor"), None),
            P(),
            P(None, "dp", "tensor"),
            P(None, "dp", "tensor"),
            P("dp", "tensor"),
            P(),
            P(None, "dp", "tensor"),
            P(None, "tensor"),
            P("tensor"),
            P("tensor"),
            P(None, "tensor"),
            P(None, "dp", "tensor"),
        ),
        check_vma=False,
    )
```

```python
import functools

import jax
import jax.numpy as jnp
from jax import lax
from jax.experimental import pallas as pl
from jax.experimental.pallas import tpu as pltpu
from jax.sharding import PartitionSpec as P

HEAD = 128
KERNEL = 5
LEFT = 64
RIGHT = 8
SLOT = 1024
REL = 73
MARGIN = 16
SUB = 128
BLK = 256
WIN = 3 * SUB
WRAP = 512
LOG2E = 1.4426950408889634
VMEM_CAP = 32 * 1024 * 1024

eps_norm = 1e-05
momentum = 0.5
bf16 = jnp.bfloat16
f32 = jnp.float32


def nn(left_op, right_op):
    return lax.dot_general(
        left_op, right_op, (((1,), (0,)), ((), ())), preferred_element_type=f32
    )


def nt(left_op, right_op):
    return lax.dot_general(
        left_op, right_op, (((1,), (1,)), ((), ())), preferred_element_type=f32
    )


def tn(left_op, right_op):
    return lax.dot_general(
        left_op, right_op, (((0,), (0,)), ((), ())), preferred_element_type=f32
    )


def window_table(rel_table):
    width=rel_table.shape[1]
    def kernel(table_ref, hi_ref, lo_ref):
        pick=spots(0)
        table=table_ref[...]
        hi=table.astype(jnp.bfloat16)
        lo=(table-hi.astype(jnp.float32)).astype(jnp.bfloat16)
        hi_ref[...]=nn(pick,hi).astype(jnp.bfloat16)
        lo_ref[...]=nn(pick,lo).astype(jnp.bfloat16)
    return run(kernel,[((WRAP,width),jnp.bfloat16)]*2,[rel_table],(),"window_table")

def spots(axis):
    shape=(WRAP,128) if axis==0 else (128,WRAP)
    u=lax.broadcasted_iota(jnp.int32,shape,axis)
    row=lax.broadcasted_iota(jnp.int32,shape,1-axis)
    dist=jnp.where(u<=WIN,jnp.clip(u-SUB,-LEFT,RIGHT),-LEFT)+LEFT
    return (dist==row).astype(jnp.bfloat16)

def order_in(dst, src, who, rows):
    for j in range(SLOT//rows):
        dst[j*rows:(j+1)*rows,:]=src[pl.ds(pl.multiple_of((j^who)*rows,rows),rows),:]

def attend_kernel(rows, who_ref, len_ref, q_ref, k_ref, v_ref, hi_ref, lo_ref, o_ref, p_ref, qs, ks, vs):
    who=who_ref[0]
    length=len_ref[0]
    order_in(qs,q_ref.at[0],who,rows); order_in(ks,k_ref.at[0],who,rows); order_in(vs,v_ref.at[0],who,rows)
    factor=HEAD**(-0.5)*LOG2E
    tail=lax.broadcasted_iota(jnp.int32,(SUB,SLOT//2),1)+SLOT//2<length
    for base in range(0,SLOT,BLK):
        q=qs[base:base+BLK,:]
        content=nt(q,ks[...])
        spread=nt(q,hi_ref[...])+nt(q,lo_ref[...])
        for off in range(0,BLK,SUB):
            i0=base+off
            e=spread[off:off+SUB]
            rolled=pltpu.roll(e,0,1,stride=1,stride_axis=0)
            lo_c=max(i0-SUB,0); hi_c=min(i0+2*SUB,SLOT)
            parts=[]
            if lo_c>0: parts.append(content[off:off+SUB,:lo_c]+e[:,0:1])
            parts.append(content[off:off+SUB,lo_c:hi_c]+rolled[:,lo_c-(i0-SUB):hi_c-(i0-SUB)])
            if hi_c<SLOT: parts.append(content[off:off+SUB,hi_c:]+e[:,WIN-1:WIN])
            logit=jnp.concatenate(parts,axis=1)*factor
            logit=jnp.concatenate([logit[:,:SLOT//2],jnp.where(tail,logit[:,SLOT//2:],-1e30)],axis=1)
            peak=jnp.max(logit,axis=1,keepdims=True)
            ex=jnp.exp2(logit-peak)
            tot=jnp.sum(ex,axis=1,keepdims=True)
            p_ref[0,i0:i0+SUB,:]=(ex*(1.0/tot)).astype(jnp.bfloat16)
        out=nn(p_ref[0,base:base+BLK,:],vs[...]).astype(jnp.bfloat16)
        for part in range(0,BLK,rows) if rows<BLK else (0,):
            n=min(rows,BLK)
            j=(base+part)//rows; inner=(base+part)%rows
            o_ref[pl.ds(pl.multiple_of((j^who)*rows+inner,n),n),:]=out[part:part+n]

def attend(qkv, who, length, table, rows):
    heads=qkv.shape[2]//HEAD
    hi,lo=table
    spec=lambda m: pl.BlockSpec((1,SLOT,HEAD),lambda h,m=m:(m,0,h))
    tab=pl.BlockSpec((WRAP,HEAD),lambda h:(0,0))
    return run(
        functools.partial(attend_kernel,rows),
        [((SLOT,heads*HEAD),jnp.bfloat16),((heads,SLOT,SLOT),jnp.bfloat16)],
        [who,length,qkv,qkv,qkv,hi,lo],
        (),"attend",grid=(heads,),
        in_specs=[SMEM_SPEC,SMEM_SPEC,spec(0),spec(1),spec(2),tab,tab],
        out_specs=[pl.BlockSpec((SLOT,HEAD),lambda h:(0,h)),pl.BlockSpec((1,SLOT,SLOT),lambda h:(h,0,0))],
        scratch=[pltpu.VMEM((SLOT,HEAD),jnp.bfloat16)]*3,
        room=28,work=heads*32*SLOT*SLOT*HEAD,
    )

def attend_back_kernel(rows, heads, who_ref, q_ref, k_ref, v_ref, g_ref, p_ref, hi_ref, lo_ref, d_ref, dt_ref, qs, ks, vs, gs, dkt, dvt):
    who=who_ref[0]
    for dst,src in ((qs,q_ref.at[0]),(ks,k_ref.at[0]),(vs,v_ref.at[0]),(gs,g_ref)):
        order_in(dst,src,who,rows)
    factor=HEAD**(-0.5)
    first=hi_ref[0:1,:].astype(jnp.float32)+lo_ref[0:1,:].astype(jnp.float32)
    final=hi_ref[WIN-1:WIN,:].astype(jnp.float32)+lo_ref[WIN-1:WIN,:].astype(jnp.float32)
    zero=jnp.zeros((SUB,SUB),jnp.float32)
    flip=(lax.broadcasted_iota(jnp.int32,(SUB,SUB),0)+lax.broadcasted_iota(jnp.int32,(SUB,SUB),1)==SUB-1).astype(jnp.bfloat16)
    table_acc=jnp.zeros((HEAD,WRAP),jnp.float32)
    left_acc=jnp.zeros((1,HEAD),jnp.float32)
    right_acc=jnp.zeros((1,HEAD),jnp.float32)
    for base in range(0,SLOT,BLK):
        q=qs[base:base+BLK,:]
        g=gs[base:base+BLK,:]
        pb=p_ref[0,base:base+BLK,:]
        p=pb.astype(jnp.float32)
        dp=nt(g,vs[...])
        delta=jnp.sum(p*dp,axis=1,keepdims=True)
        dsb=(p*(dp-delta)).astype(jnp.bfloat16)
        dv_part=tn(g,pb)
        dk_part=tn(q,dsb)
        if base==0:
            dvt[...]=dv_part; dkt[...]=dk_part
        else:
            dvt[...]+=dv_part; dkt[...]+=dk_part
        dq=nn(dsb,ks[...])
        ds=dsb.astype(jnp.float32)
        qf=q.astype(jnp.float32)
        extra=[]
        for off in range(0,BLK,SUB):
            i0=base+off
            d=ds[off:off+SUB]
            lo_c=max(i0-SUB,0); hi_c=min(i0+2*SUB,SLOT)
            turned=nn(flip,dsb[off:off+SUB,lo_c:hi_c])
            win=[zero]*((lo_c-(i0-SUB))//SUB)+[turned]+[zero]*((i0+2*SUB-hi_c)//SUB+1)
            moved=pltpu.roll(jnp.concatenate(win,axis=1),WRAP-SUB+1,1,stride=1,stride_axis=0)
            u=nn(flip,moved.astype(jnp.bfloat16)).astype(jnp.bfloat16)
            add=nn(u,hi_ref[...])+nn(u,lo_ref[...])
            table_acc=table_acc+tn(q[off:off+SUB],u)
            if lo_c>0:
                s=jnp.sum(d[:,:lo_c],axis=1,keepdims=True)
                add=add+s*first
                left_acc=left_acc+jnp.sum(s*qf[off:off+SUB],axis=0,keepdims=True)
            if hi_c<SLOT:
                s=jnp.sum(d[:,hi_c:],axis=1,keepdims=True)
                add=add+s*final
                right_acc=right_acc+jnp.sum(s*qf[off:off+SUB],axis=0,keepdims=True)
            extra.append(add)
        dq=((dq+jnp.concatenate(extra,axis=0))*factor).astype(jnp.bfloat16)
        for part in range(0,BLK,rows) if rows<BLK else (0,):
            n=min(rows,BLK)
            j=(base+part)//rows; inner=(base+part)%rows
            d_ref[0,pl.ds(pl.multiple_of((j^who)*rows+inner,n),n),:]=dq[part:part+n]
    spread=table_acc*factor
    upper=spread.astype(jnp.bfloat16)
    lower=(spread-upper.astype(jnp.float32)).astype(jnp.bfloat16)
    pick=spots(1)
    gathered=nt(pick,upper)+nt(pick,lower)
    row=lax.broadcasted_iota(jnp.int32,(128,1),0)
    gathered=gathered+jnp.where(row==0,left_acc*factor,0.0)+jnp.where(row==LEFT+RIGHT,right_acc*factor,0.0)
    @pl.when(pl.program_id(0)==0)
    def _():
        dt_ref[...]=gathered
    @pl.when(pl.program_id(0)>0)
    def _():
        dt_ref[...]+=gathered
    for j in range(SLOT//rows):
        sl=pl.ds(pl.multiple_of((j^who)*rows,rows),rows)
        d_ref[1,sl,:]=(jnp.transpose(dkt[:,j*rows:(j+1)*rows])*factor).astype(jnp.bfloat16)
        d_ref[2,sl,:]=jnp.transpose(dvt[:,j*rows:(j+1)*rows]).astype(jnp.bfloat16)

def attend_back(qkv, grad, probs, who, table, rows):
    heads=qkv.shape[2]//HEAD
    hi,lo=table
    spec=lambda m: pl.BlockSpec((1,SLOT,HEAD),lambda h,m=m:(m,0,h))
    tab=pl.BlockSpec((WRAP,HEAD),lambda h:(0,0))
    return run(
        functools.partial(attend_back_kernel,rows,heads),
        [((3,SLOT,heads*HEAD),jnp.bfloat16),((128,HEAD),jnp.float32)],
        [who,qkv,qkv,qkv,grad,probs,hi,lo],
        (),"attend_back",grid=(heads,),
        in_specs=[SMEM_SPEC,spec(0),spec(1),spec(2),pl.BlockSpec((SLOT,HEAD),lambda h:(0,h)),pl.BlockSpec((1,SLOT,SLOT),lambda h:(h,0,0)),tab,tab],
        out_specs=[pl.BlockSpec((3,SLOT,HEAD),lambda h:(0,0,h)),pl.BlockSpec((128,HEAD),lambda h:(0,0))],
        scratch=[pltpu.VMEM((SLOT,HEAD),jnp.bfloat16)]*4+[pltpu.VMEM((HEAD,SLOT),jnp.float32)]*2,
        room=28,work=heads*50*SLOT*SLOT*HEAD,
    )


MARKS = {}
PIECES = 4


class Stack:
    def __init__(self, refs):
        self.refs = refs

    def __getitem__(self, index):
        return jnp.concatenate([ref[index] for ref in self.refs], axis=0)


def run(
    kernel,
    outs,
    ins,
    after=(),
    name=None,
    grid=None,
    in_specs=None,
    out_specs=None,
    scratch=(),
    aliases=None,
    room=24,
    work=1 << 20,
    mark=False,
):
    after = [MARKS[id(item)][1] if id(item) in MARKS else item for item in after]
    waits = len(after)
    outs = list(outs) + [((8, 128), f32)] * mark
    sizes = [len(item) if isinstance(item, list) else 0 for item in ins]

    def body(*refs):
        args, at = [], 0
        for size in sizes:
            args.append(Stack(refs[at : at + size]) if size else refs[at])
            at += max(size, 1)
        last = at + waits + len(outs) - mark
        kernel(*args, *refs[at + waits : last], *refs[last + mark :])
        if mark:
            refs[last][...] = jnp.zeros((8, 128), f32)

    def full(shape):
        return pl.BlockSpec(tuple(shape), lambda i: (0,) * len(shape))

    if grid is None:
        grid = (1,)
    given = list(in_specs) if in_specs is not None else [None] * len(ins)
    specs, flat, start = [], [], []
    for item, spec, size in zip(ins, given, sizes):
        start.append(len(flat))
        if spec is None:
            spec = full((item[0] if size else item).shape)
        elif size:
            shape = spec.block_shape
            spec = pl.BlockSpec((shape[0] // size,) + tuple(shape[1:]), spec.index_map)
        specs += [spec] * max(size, 1)
        flat += item if size else [item]
    ins = flat
    if out_specs is None:
        out_specs = [full(shape) for shape, _ in outs]
    else:
        out_specs = list(out_specs) + [pl.BlockSpec((8, 128), lambda i: (0, 0))] * mark
    made = pl.pallas_call(
        body,
        in_specs=specs + [pl.BlockSpec(memory_space=pl.ANY)] * waits,
        out_specs=out_specs,
        out_shape=[jax.ShapeDtypeStruct(shape, dtype) for shape, dtype in outs],
        scratch_shapes=list(scratch),
        input_output_aliases={start[i]: o for i, o in (aliases or {}).items()},
        compiler_params=pltpu.CompilerParams(vmem_limit_bytes=room << 20),
        cost_estimate=pl.CostEstimate(flops=0, bytes_accessed=0, transcendentals=0),
        name=name,
        grid=grid,
    )(*ins, *after)
    if not mark:
        return list(made)
    for array in made[:-1]:
        MARKS[id(array)] = (array, made[-1])
    return list(made[:-1])


SMEM_SPEC = pl.BlockSpec(memory_space=pltpu.SMEM)


def moments(rows):
    centred = rows - jnp.mean(rows, axis=1, keepdims=True)
    inverse = lax.rsqrt(jnp.mean(centred * centred, axis=1, keepdims=True) + eps_norm)
    return centred * inverse, inverse


def back(weighted, normed, inverse):
    first_mean = jnp.mean(weighted, axis=1, keepdims=True)
    second_mean = jnp.mean(weighted * normed, axis=1, keepdims=True)
    return inverse * (weighted - first_mean - normed * second_mean)


def wide(ref):
    return ref[...].astype(f32)


def cut(shape):
    return [((shape[0] // PIECES,) + tuple(shape[1:]), bf16)] * PIECES


def put(refs, value):
    rows = value.shape[0] // len(refs)
    for i, ref in enumerate(refs):
        ref[...] = value[i * rows : (i + 1) * rows].astype(bf16)


def take(items, count):
    return [items.pop(0) for _ in range(count)]


def add_up(parts, name, after=()):
    shape = parts[0].shape

    def kernel(*refs):
        total = wide(refs[0])
        for ref in refs[1:-1]:
            total = total + wide(ref)
        refs[-1][...] = total.astype(bf16)

    return run(kernel, [(shape, bf16)], parts, after, name)[0]


def total_of(refs):
    total = wide(refs[0])
    for ref in refs[1:]:
        total = total + wide(ref)
    return total


def gain_row(ref, index):
    return ref[index : index + 1, :]


def put_edge(ref, who, value):
    value = value.astype(f32)
    ref[...] = jnp.where(who // 2 == 0, value[-MARGIN:], value[:MARGIN]).astype(bf16)


def norm_rows(
    resid, parts, factor, gains, index, name, after=(), keep=True, low=False, also=None, edge=None
):
    shape = resid.shape
    count = len(parts)
    extra = ([also] if also is not None else []) + ([edge] if edge is not None else [])
    ins = [resid, gains] + list(parts) + extra
    outs = [(shape, bf16)] + cut(shape) + [(shape, f32)] * keep + [(shape, bf16)] * low
    outs = outs + [(shape, bf16)] * (also is not None)
    outs = outs + [((MARGIN, shape[1]), bf16)] * (edge is not None)

    def kernel(resid_ref, gain_ref, *refs):
        refs = list(refs)
        part_refs = take(refs, count)
        also_ref = take(refs, also is not None)
        edge_ref = take(refs, edge is not None)
        rows = wide(resid_ref)
        if count:
            rows = rows + factor * total_of(part_refs)
        normed = (moments(rows)[0] * gain_row(gain_ref, index)).astype(bf16)
        refs.pop(0)[...] = normed
        put(take(refs, PIECES), normed)
        if keep:
            refs.pop(0)[...] = rows
        if low:
            refs.pop(0)[...] = rows.astype(bf16)
        if also_ref:
            refs.pop(0)[...] = also_ref[0][...].astype(bf16)
        if edge_ref:
            put_edge(refs.pop(0), edge_ref[0][0], normed)

    specs = [None] * (2 + count + (also is not None)) + [SMEM_SPEC] * (edge is not None)
    made = run(kernel, outs, ins, after, name, in_specs=specs)
    return [(made[0], made[1 : 1 + PIECES])] + made[1 + PIECES :]


def norm_last(resid, parts, gains, upper, who, k, length, name, full, after=()):
    shape = resid.shape
    count = len(parts)
    outs = [(shape, bf16)] + cut(shape)
    if full:
        outs = outs + [(shape, f32), (shape, f32), ((8, shape[1]), f32)]

    def kernel(who_ref, length_ref, resid_ref, gain_ref, upper_ref, *refs):
        refs = list(refs)
        rows = wide(resid_ref) + 0.5 * total_of(take(refs, count))
        gain = gain_row(gain_ref, 4)
        normed, inverse = moments(rows)
        begin = (who_ref[0] ^ (2 * k)) * shape[0]
        place = lax.broadcasted_iota(jnp.int32, (shape[0], 1), 0) + begin
        valid = (place < length_ref[0]).astype(f32)
        seen = wide(upper_ref) * valid
        grad = back(seen * gain, normed, inverse)
        rounded = (0.5 * grad).astype(bf16)
        refs.pop(0)[...] = rounded
        put(take(refs, PIECES), rounded)
        if full:
            refs.pop(0)[...] = grad
            refs.pop(0)[...] = normed * gain * valid
            refs.pop(0)[...] = jnp.broadcast_to(
                jnp.sum(seen * normed, axis=0, keepdims=True), (8, shape[1])
            )

    ins = [who, length, resid, gains, upper] + list(parts)
    specs = [SMEM_SPEC, SMEM_SPEC] + [None] * (3 + count)
    made = run(kernel, outs, ins, after, name, in_specs=specs)
    return [(made[0], made[1 : 1 + PIECES])] + made[1 + PIECES :]


def norm_grad(
    rows_in, parts, gains, index, grad, name, after=(), factor=None, keep=True, sums=True, edge=None
):
    shape = rows_in.shape
    count = len(parts)
    outs = ([(shape, bf16)] + cut(shape)) if factor is not None else []
    outs = outs + [(shape, f32)] * keep + [((8, shape[1]), f32)] * sums
    outs = outs + [((MARGIN, shape[1]), bf16)] * (edge is not None)

    def kernel(rows_ref, gain_ref, grad_ref, *refs):
        refs = list(refs)
        total = total_of(take(refs, count))
        edge_ref = take(refs, edge is not None)
        normed, inverse = moments(wide(rows_ref))
        result = wide(grad_ref) + back(total * gain_row(gain_ref, index), normed, inverse)
        if factor is not None:
            rounded = (factor * result).astype(bf16)
            refs.pop(0)[...] = rounded
            put(take(refs, PIECES), rounded)
        if keep:
            refs.pop(0)[...] = result
        if sums:
            refs.pop(0)[...] = jnp.broadcast_to(
                jnp.sum(total * normed, axis=0, keepdims=True), (8, shape[1])
            )
        if edge_ref:
            put_edge(refs.pop(0), edge_ref[0][0], rounded)

    ins = [rows_in, gains, grad] + list(parts) + ([edge] if edge is not None else [])
    specs = [None] * (3 + count) + [SMEM_SPEC] * (edge is not None)
    made = run(kernel, outs, ins, after, name, in_specs=specs)
    if factor is None:
        return made
    return [(made[0], made[1 : 1 + PIECES])] + made[1 + PIECES :]


def add_stats(value, others, channels, name, after=()):
    cols = value.shape[1]
    ny = cols // channels if channels else 0

    def kernel(*refs):
        total = refs[0][...]
        for k, ref in enumerate(refs[1:-1], 1):
            if channels:
                total = total + jnp.concatenate(
                    [ref[:, (r ^ k) * channels : ((r ^ k) + 1) * channels] for r in range(ny)], axis=1
                )
            else:
                total = total + ref[...]
        refs[-1][...] = total

    return run(kernel, [(value.shape, f32)], [value] + list(others), after, name)[0]


def tile_of(total, most):
    return most if total % most == 0 else total


def feed(own, mate, weights, name, after=()):
    rows, width = own.shape
    hidden = weights.shape[2]
    tile = tile_of(hidden, 1024)
    steps = hidden // tile

    def kernel(own_ref, mate_ref, in_ref, out_ref, p_own, *rest):
        *p_mate, pre, hid, seen = rest[: PIECES + 3]
        acc = rest[PIECES + 3] if steps > 1 else None
        step = pl.program_id(0)
        both = jnp.concatenate([own_ref[...], mate_ref[...]], axis=0)
        seen[...] = both
        value = nn(both, in_ref[0])
        act = (value / (1.0 + jnp.exp(-value))).astype(bf16)
        pre[...] = value.astype(bf16)
        hid[...] = act
        part = nt(act, out_ref[0])
        if steps == 1:
            p_own[...] = part[:rows].astype(bf16)
            put(p_mate, part[rows:])
            return

        @pl.when(step == 0)
        def _():
            acc[...] = part

        @pl.when(step > 0)
        def _():
            acc[...] += part

        @pl.when(step == steps - 1)
        def _():
            p_own[...] = acc[:rows].astype(bf16)
            put(p_mate, acc[rows:])

    fixed = pl.BlockSpec((rows, width), lambda i: (0, 0))
    quarter = [pl.BlockSpec((rows // PIECES, width), lambda i: (0, 0))] * PIECES
    cols = pl.BlockSpec((2 * rows, tile), lambda i: (0, i))
    weight = [pl.BlockSpec((1, width, tile), lambda i, m=m: (m, 0, i)) for m in range(2)]
    return run(
        kernel,
        [((rows, width), bf16)] + cut((rows, width)) + [((2 * rows, hidden), bf16)] * 2 + [((2 * rows, width), bf16)],
        [own, mate, weights, weights],
        after,
        name,
        grid=(steps,),
        in_specs=[fixed, fixed] + weight,
        out_specs=[fixed] + quarter + [cols, cols, pl.BlockSpec((2 * rows, width), lambda i: (0, 0))],
        scratch=[pltpu.VMEM((2 * rows, width), f32)] if steps > 1 else (),
        room=28,
        work=8 * rows * width * hidden,
    )


def feed_grad(own, mate, pre, weights, name, after=()):
    rows, width = own.shape
    hidden = weights.shape[2]
    tile = tile_of(hidden, 1024)
    steps = hidden // tile

    def kernel(own_ref, mate_ref, pre_ref, in_ref, out_ref, p_own, *rest):
        *p_mate, down, seen = rest[: PIECES + 2]
        acc = rest[PIECES + 2] if steps > 1 else None
        step = pl.program_id(0)
        both = jnp.concatenate([own_ref[...], mate_ref[...]], axis=0)
        seen[...] = both
        value = nn(both, out_ref[0])
        preact = wide(pre_ref)
        logistic = 1.0 / (1.0 + jnp.exp(-preact))
        slope = logistic * (1.0 + preact * (1.0 - logistic))
        grad = (value * slope).astype(bf16)
        down[...] = grad
        part = nt(grad, in_ref[0])
        if steps == 1:
            p_own[...] = part[:rows].astype(bf16)
            put(p_mate, part[rows:])
            return

        @pl.when(step == 0)
        def _():
            acc[...] = part

        @pl.when(step > 0)
        def _():
            acc[...] += part

        @pl.when(step == steps - 1)
        def _():
            p_own[...] = acc[:rows].astype(bf16)
            put(p_mate, acc[rows:])

    fixed = pl.BlockSpec((rows, width), lambda i: (0, 0))
    quarter = [pl.BlockSpec((rows // PIECES, width), lambda i: (0, 0))] * PIECES
    cols = pl.BlockSpec((2 * rows, tile), lambda i: (0, i))
    weight = [pl.BlockSpec((1, width, tile), lambda i, m=m: (m, 0, i)) for m in range(2)]
    return run(
        kernel,
        [((rows, width), bf16)] + cut((rows, width)) + [((2 * rows, hidden), bf16), ((2 * rows, width), bf16)],
        [own, mate, pre, weights, weights],
        after,
        name,
        grid=(steps,),
        in_specs=[fixed, fixed, cols] + weight,
        out_specs=[fixed] + quarter + [cols, pl.BlockSpec((2 * rows, width), lambda i: (0, 0))],
        scratch=[pltpu.VMEM((2 * rows, width), f32)] if steps > 1 else (),
        room=28,
        work=8 * rows * width * hidden,
    )


def qkv_rows(own, mate, weights, k, total, held, name, after=()):
    rows, width = own.shape
    cols = weights.shape[2]

    def kernel(own_ref, mate_ref, w_ref, *refs):
        both = jnp.concatenate([own_ref[...], mate_ref[...]], axis=0)
        refs[-1][...] = both
        refs[-2][0] = nn(both, w_ref[0]).astype(bf16)

    fixed = pl.BlockSpec((rows, width), lambda i: (0, 0))
    quarter = [pl.BlockSpec((rows // PIECES, width), lambda i: (0, 0))] * PIECES
    ins = [own, mate, weights] + ([held] if held is not None else [])
    specs = [fixed, fixed, pl.BlockSpec((1, width, cols), lambda i: (i, 0, 0))]
    specs = specs + [pl.BlockSpec(memory_space=pl.ANY)] * (held is not None)
    return run(
        kernel,
        [((3, total, cols), bf16), ((2 * rows, width), bf16)],
        ins,
        after,
        name,
        grid=(3,),
        in_specs=specs,
        out_specs=[
            pl.BlockSpec((1, 2 * rows, cols), lambda i: (i, k, 0)),
            pl.BlockSpec((2 * rows, width), lambda i: (0, 0)),
        ],
        work=12 * rows * width * cols,
        aliases={3: 0} if held is not None else None,
    )


def heads_rows(own, mate, weight, k, total, held, name, after=()):
    rows, width = own.shape
    cols = weight.shape[1]

    def kernel(own_ref, mate_ref, w_ref, *refs):
        both = jnp.concatenate([own_ref[...], mate_ref[...]], axis=0)
        refs[-1][...] = both
        refs[-2][...] = nn(both, w_ref[...]).astype(bf16)

    fixed = pl.BlockSpec((rows, width), lambda i: (0, 0))
    quarter = [pl.BlockSpec((rows // PIECES, width), lambda i: (0, 0))] * PIECES
    ins = [own, mate, weight] + ([held] if held is not None else [])
    specs = [fixed, fixed, pl.BlockSpec((width, cols), lambda i: (0, 0))]
    specs = specs + [pl.BlockSpec(memory_space=pl.ANY)] * (held is not None)
    return run(
        kernel,
        [((total, cols), bf16), ((2 * rows, width), bf16)],
        ins,
        after,
        name,
        grid=(1,),
        in_specs=specs,
        out_specs=[
            pl.BlockSpec((2 * rows, cols), lambda i: (k, 0)),
            pl.BlockSpec((2 * rows, width), lambda i: (0, 0)),
        ],
        work=4 * rows * width * cols,
        aliases={3: 0} if held is not None else None,
    )


def out_rows(values, weight, k, rows, name, after=()):
    width, cols = weight.shape

    def kernel(value_ref, w_ref, p_own, *p_mate):
        part = nt(value_ref[...], w_ref[...])
        p_own[...] = part[:rows].astype(bf16)
        put(p_mate, part[rows:])

    fixed = pl.BlockSpec((rows, width), lambda i: (0, 0))
    quarter = [pl.BlockSpec((rows // PIECES, width), lambda i: (0, 0))] * PIECES
    return run(
        kernel,
        [((rows, width), bf16)] + cut((rows, width)),
        [values, weight],
        after,
        name,
        grid=(1,),
        in_specs=[
            pl.BlockSpec((2 * rows, cols), lambda i: (k, 0)),
            pl.BlockSpec((width, cols), lambda i: (0, 0)),
        ],
        out_specs=[fixed] + quarter,
        work=4 * rows * width * cols,
    )


def members_rows(members, weights, k, rows, name, after=()):
    width, cols = weights.shape[1:]

    def kernel(value_ref, w_ref, p_own, *p_mate):
        part = nt(value_ref[0], w_ref[0])
        for m in range(1, 3):
            part = part + nt(value_ref[m], w_ref[m])
        p_own[...] = part[:rows].astype(bf16)
        put(p_mate, part[rows:])

    fixed = pl.BlockSpec((rows, width), lambda i: (0, 0))
    quarter = [pl.BlockSpec((rows // PIECES, width), lambda i: (0, 0))] * PIECES
    return run(
        kernel,
        [((rows, width), bf16)] + cut((rows, width)),
        [members, weights],
        after,
        name,
        grid=(1,),
        in_specs=[
            pl.BlockSpec((3, 2 * rows, cols), lambda i: (0, k, 0)),
            pl.BlockSpec((3, width, cols), lambda i: (0, 0, 0)),
        ],
        out_specs=[fixed] + quarter,
        work=12 * rows * width * cols,
    )


def part(array, m=None, begin=0, end=None):
    value = array[...] if m is None else array[m]
    return value if end is None else value[:, begin:end]


def plain(item):
    return item[0] if isinstance(item, tuple) else item


def spot(item):
    return item[1:] if isinstance(item, tuple) else ()


def span(item):
    return item[3] - item[2] if len(spot(item)) > 1 else plain(item).shape[-1]


def lay_out(jobs):
    plan, ins = [], []
    for left, rights in jobs:
        picks = [[spot(item) for item in right] for right in rights]
        plan.append((len(left), picks, sum(span(right[0]) for right in rights)))
        ins = ins + list(left) + [plain(item) for right in rights for item in right]
    return plan, ins


def sides(plan, refs):
    at = 0
    for n_left, picks, cols in plan:
        left = refs[at : at + n_left]
        at = at + n_left
        columns = []
        for places in picks:
            values = []
            for place in places:
                values.append(part(refs[at], *place))
                at = at + 1
            columns.append(values[0] if len(values) == 1 else jnp.concatenate(values, axis=0))
        yield left, columns[0] if len(columns) == 1 else jnp.concatenate(columns, axis=1), cols


def outer(jobs, name, after=(), sums=()):
    plan, ins = lay_out(jobs)
    total = sum(cols for _, _, cols in plan) + sum(parts[0].shape[1] for parts in sums)
    width = jobs[0][0][0].shape[1]
    products = len(ins)
    ins = ins + [array for parts in sums for array in parts]

    def kernel(*refs):
        column = 0
        for left, rights, cols in sides(plan, refs):
            rows = [ref[...] for ref in left]
            rows = rows[0] if len(rows) == 1 else jnp.concatenate(rows, axis=0)
            refs[-1][:, column : column + cols] = tn(rows, rights).astype(bf16)
            column = column + cols
        at = products
        for parts in sums:
            value = total_of(refs[at : at + len(parts)])
            refs[-1][:, column : column + parts[0].shape[1]] = value.astype(bf16)
            at = at + len(parts)
            column = column + parts[0].shape[1]

    work = sum(2 * width * cols * sum(r.shape[0] for r in left) for (left, _), (_, _, cols) in zip(jobs, plan))
    return run(kernel, [((width, total), bf16)], ins, after, name, room=36, work=work, mark=True)[0]


def outer_halves(links, jobs, turn, name, after=(), sums=()):
    offsets, masks = links.offsets(turn)
    width = jobs[0][0][0].shape[1] if jobs else sums[0][0].shape[0]
    share = width // links.dp
    me = lax.axis_index("dp").reshape(1).astype(jnp.int32)

    plan, ins = lay_out(jobs)
    products = len(ins)
    ins = [me] + ins + [array for parts in sums for array in parts]
    total = sum(cols for _, _, cols in plan) + sum(parts[0].shape[1] for parts in sums)
    half = len(offsets)

    def kernel(me_ref, *refs):
        who = me_ref[0]
        sent_ref, kept_ref = refs[-2], refs[-1]
        ways = ((masks[0], sent_ref), (0, kept_ref))
        column = 0

        def block(off):
            return pl.ds(pl.multiple_of((who ^ off) * share, 128), share)

        for left, rights, cols in sides(plan, refs):
            for flip, dest in ways:
                picked = []
                for off in offsets:
                    parts = [ref[:, block(off ^ flip)] for ref in left]
                    picked.append(parts[0] if len(parts) == 1 else jnp.concatenate(parts, axis=0))
                picked = picked[0] if half == 1 else jnp.concatenate(picked, axis=1)
                dest[:, column : column + cols] = tn(picked, rights).astype(bf16)
            column = column + cols
        at = products
        for parts in sums:
            cols = parts[0].shape[1]
            for flip, dest in ways:
                for i, off in enumerate(offsets):
                    value = total_of([ref.at[block(off ^ flip), :] for ref in refs[at : at + len(parts)]])
                    dest[i * share : (i + 1) * share, column : column + cols] = value.astype(bf16)
            at = at + len(parts)
            column = column + cols

    return run(
        kernel,
        [((half * share, total), bf16)] * 2,
        ins,
        after,
        name,
        in_specs=[SMEM_SPEC] + [None] * (len(ins) - 1),
        room=24,
        work=2 * SLOT * width * total,
        mark=True,
    )


def halve_all(pairs, name, after=()):
    shapes = [(kept.shape[0] // 2, kept.shape[1]) for kept, _ in pairs]
    count = len(pairs)

    def kernel(*refs):
        for i in range(count):
            total = wide(refs[2 * i]) + wide(refs[2 * i + 1])
            half = shapes[i][0]
            refs[2 * count + 2 * i][...] = total[half:].astype(bf16)
            refs[2 * count + 2 * i + 1][...] = total[:half].astype(bf16)

    outs = [(shape, bf16) for shape in shapes for _ in range(2)]
    made = run(kernel, outs, [array for pair in pairs for array in pair], after, name, mark=True)
    return [(made[2 * i], made[2 * i + 1]) for i in range(count)]


def halves(ref_own, ref_mate, c):
    own, mate = ref_own[...], ref_mate[...]
    first = jnp.where(c == 0, own, mate)
    second = jnp.where(c == 0, mate, own)
    return first, second


def shift_rows(value, offset):
    if offset == 0:
        return value
    return pltpu.roll(value, (-offset) % value.shape[0], 0)


def place_mask(count, y, length):
    place = lax.broadcasted_iota(jnp.int32, (count + 2 * MARGIN, 1), 0) + (y * count - MARGIN)
    return ((place >= 0) & (place < length)).astype(f32)


def bordered(own_ref, mate_ref, before, after, who, ny):
    y, c = who // 2, who % 2
    first, second = halves(own_ref, mate_ref, c)
    above = wide(before[0])
    for ref in before[1:]:
        above = above + wide(ref)
    below = wide(after[0])
    for ref in after[1:]:
        below = below + wide(ref)
    above = jnp.where(y > 0, above, 0.0).astype(bf16)
    below = jnp.where(y < ny - 1, below, 0.0).astype(bf16)
    return jnp.concatenate([above, first, second, below], axis=0)


def conv_mix(ny, who, length, own, mate, before, after_rows, weights, taps, name, after=()):
    rows, width = own.shape
    cols = taps.shape[1]
    count = 2 * rows
    lo, hi = MARGIN, MARGIN + count
    n_before = len(before)

    def kernel(who_ref, len_ref, own_ref, mate_ref, w0, w1, taps_ref, *refs):
        rows_in = bordered(own_ref, mate_ref, refs[:n_before], refs[n_before:-5], who_ref[0], ny)
        lin_ref, gate_ref, mix_ref, tally_ref, seen_ref = refs[-5:]
        seen_ref[...] = jnp.concatenate([own_ref[...], mate_ref[...]], axis=0)
        valid = place_mask(count, who_ref[0] // 2, len_ref[0])
        linear = nn(rows_in, w0[...])
        gating = 1.0 / (1.0 + jnp.exp(-nn(rows_in, w1[...])))
        lin_ref[...] = linear
        gate_ref[...] = gating
        glu = linear * gating * valid
        mixture = taps_ref[0:1, :] * shift_rows(glu, -2)
        for j in range(1, KERNEL):
            mixture = mixture + taps_ref[j : j + 1, :] * shift_rows(glu, j - 2)
        mix_ref[...] = mixture
        inside = (valid * mixture)[lo:hi]
        tally_ref[...] = jnp.concatenate(
            [
                jnp.sum(inside, axis=0, keepdims=True),
                jnp.sum(inside * mixture[lo:hi], axis=0, keepdims=True),
                jnp.broadcast_to(jnp.sum(valid[lo:hi], axis=0, keepdims=True), (1, cols)),
                jnp.zeros((5, cols), f32),
            ],
            axis=0,
        )

    ins = [who, length, own, mate, weights[0], weights[1], taps] + list(before) + list(after_rows)
    shape = (count + 2 * MARGIN, cols)
    return run(
        kernel,
        [(shape, f32)] * 3 + [((8, cols), f32), ((count, width), bf16)],
        ins,
        after,
        name,
        in_specs=[SMEM_SPEC, SMEM_SPEC] + [None] * (len(ins) - 2),
        room=28,
        work=4 * count * width * cols,
    )


def batch_terms(tally_ref):
    count = tally_ref[2:3, :]
    mean = tally_ref[0:1, :] / count
    var = tally_ref[1:2, :] / count - mean * mean
    return count, mean, var, lax.rsqrt(var + eps_norm)


def conv_out(who, mixture, tallies, affine, running, weight, rows, name, after=()):
    width, cols = weight.shape
    channels = running.shape[1]
    lo, mid, hi = MARGIN, MARGIN + rows, MARGIN + 2 * rows

    def kernel(who_ref, mix_ref, tally_ref, affine_ref, run_ref, w_ref, act_ref, p_own, *rest):
        *p_mate, new_ref = rest
        c = who_ref[0] % 2
        count, mean, var, inverse = batch_terms(tally_ref)
        own = pl.ds(pl.multiple_of(lo + c * rows, 16), rows)
        mate = pl.ds(pl.multiple_of(lo + (1 - c) * rows, 16), rows)
        mixture = jnp.concatenate([mix_ref[own, :], mix_ref[mate, :]], axis=0)
        shifted = (mixture - mean) * inverse * affine_ref[KERNEL : KERNEL + 1, :] + affine_ref[KERNEL + 1 : KERNEL + 2, :]
        active = (shifted / (1.0 + jnp.exp(-shifted))).astype(bf16)
        act_ref[...] = active
        part = nt(active, w_ref[...])
        p_own[...] = part[:rows].astype(bf16)
        put(p_mate, part[rows:])
        grown = var * count / (count - 1.0)
        new_ref[...] = (1.0 - momentum) * run_ref[...] + momentum * jnp.concatenate(
            [mean[:, :channels], grown[:, :channels]], axis=0
        )

    return run(
        kernel,
        [((2 * rows, cols), bf16), ((rows, width), bf16)] + cut((rows, width)) + [(running.shape, f32)],
        [who, mixture, tallies, affine, running, weight],
        after,
        name,
        in_specs=[SMEM_SPEC] + [None] * 5,
        room=24,
        work=4 * rows * width * cols,
    )


def conv_shift_grad(ny, who, length, own, mate, before, after_rows, mixture, tallies, affine, weight, name, after=()):
    rows, width = own.shape
    cols = weight.shape[1]
    count = 2 * rows
    lo, hi = MARGIN, MARGIN + count
    n_before = len(before)

    def kernel(who_ref, len_ref, own_ref, mate_ref, mix_ref, tally_ref, affine_ref, w_ref, *refs):
        rows_in = bordered(own_ref, mate_ref, refs[:n_before], refs[n_before:-3], who_ref[0], ny)
        dz_ref, out_ref, seen_ref = refs[-3:]
        seen_ref[...] = jnp.concatenate([own_ref[...], mate_ref[...]], axis=0)
        valid = place_mask(count, who_ref[0] // 2, len_ref[0])
        _, mean, _, inverse = batch_terms(tally_ref)
        centred = (mix_ref[...] - mean) * inverse
        shifted = centred * affine_ref[KERNEL : KERNEL + 1, :] + affine_ref[KERNEL + 1 : KERNEL + 2, :]
        logistic = 1.0 / (1.0 + jnp.exp(-shifted))
        slope = logistic * (1.0 + shifted * (1.0 - logistic))
        grad = jnp.where(valid > 0.0, nn(rows_in, w_ref[...]) * slope, 0.0)
        dz_ref[...] = grad
        inner = grad[lo:hi]
        out_ref[...] = jnp.concatenate(
            [
                jnp.sum(inner * centred[lo:hi], axis=0, keepdims=True),
                jnp.sum(inner, axis=0, keepdims=True),
                jnp.zeros((6, cols), f32),
            ],
            axis=0,
        )

    ins = [who, length, own, mate, mixture, tallies, affine, weight] + list(before) + list(after_rows)
    return run(
        kernel,
        [(mixture.shape, f32), ((8, cols), f32), ((count, width), bf16)],
        ins,
        after,
        name,
        in_specs=[SMEM_SPEC, SMEM_SPEC] + [None] * (len(ins) - 2),
        room=28,
        work=4 * count * width * cols,
    )


def conv_in_grad(who, length, dz, mixture, tallies, sums, affine, taps, linear, gating, weights, rows, name, after=()):
    width, cols = weights[0].shape
    count = 2 * rows
    lo, mid, hi = MARGIN, MARGIN + rows, MARGIN + count

    def kernel(who_ref, len_ref, dz_ref, mix_ref, tally_ref, sum_ref, affine_ref, taps_ref, lin_ref, gate_ref, w0, w1, dl_ref, dg_ref, p_own, *rest):
        *p_mate, tap_ref = rest
        c = who_ref[0] % 2
        valid = place_mask(count, who_ref[0] // 2, len_ref[0])
        total, mean, _, inverse = batch_terms(tally_ref)
        centred = (mix_ref[...] - mean) * inverse
        shrink = affine_ref[KERNEL : KERNEL + 1, :] * inverse
        mixed = (sum_ref[1:2, :] + centred * sum_ref[0:1, :]) / total
        grad_mix = jnp.where(valid > 0.0, shrink * (dz_ref[...] - mixed), 0.0)
        grad_glu = taps_ref[0:1, :] * shift_rows(grad_mix, 2)
        for j in range(1, KERNEL):
            grad_glu = grad_glu + taps_ref[j : j + 1, :] * shift_rows(grad_mix, 2 - j)
        linear = lin_ref[...]
        gating = gate_ref[...]
        glu = linear * gating * valid
        inner = grad_mix[lo:hi]
        tap_ref[...] = jnp.concatenate(
            [
                jnp.sum(inner * shift_rows(glu, j - 2)[lo:hi], axis=0, keepdims=True)
                for j in range(KERNEL)
            ]
            + [jnp.zeros((8 - KERNEL, cols), f32)],
            axis=0,
        )
        held = grad_glu * valid * gating
        grad_linear = held.astype(bf16)
        grad_gate = (held * linear * (1.0 - gating)).astype(bf16)

        def turned(value):
            first, second = value[lo:mid], value[mid:hi]
            return jnp.concatenate(
                [jnp.where(c == 0, first, second), jnp.where(c == 0, second, first)], axis=0
            )

        grad_linear = turned(grad_linear)
        grad_gate = turned(grad_gate)
        dl_ref[...] = grad_linear
        dg_ref[...] = grad_gate
        part = nt(grad_linear, w0[...]) + nt(grad_gate, w1[...])
        p_own[...] = part[:rows].astype(bf16)
        put(p_mate, part[rows:])

    return run(
        kernel,
        [((count, cols), bf16)] * 2 + [((rows, width), bf16)] + cut((rows, width)) + [((8, cols), f32)],
        [who, length, dz, mixture, tallies, sums, affine, taps, linear, gating, weights[0], weights[1]],
        after,
        name,
        in_specs=[SMEM_SPEC, SMEM_SPEC] + [None] * 10,
        room=32,
        work=4 * count * width * cols,
    )


class Links:
    def __init__(self, dp, tensor):
        self.dp, self.tensor, self.ny = dp, tensor, tensor // 2
        self.masks = [1 << bit for bit in range(dp.bit_length() - 1)]

    def core(self, value):
        return lax.ppermute(value, "tensor", [(i, i ^ 1) for i in range(self.tensor)])

    def mate(self, pieces):
        return [self.core(piece) for piece in pieces]

    def chip(self, value, k):
        return lax.ppermute(value, "tensor", [(i, i ^ (2 * k)) for i in range(self.tensor)])

    def group(self, value, mask):
        return lax.ppermute(value, "dp", [(i, i ^ mask) for i in range(self.dp)])

    def scatter_grad(self, value):
        return lax.psum_scatter(value, "dp", scatter_dimension=0, tiled=True)

    def sum_group(self, value, name):
        for mask in self.masks:
            value = add_stats(value, [self.group(value, mask)], 0, name)
        return value

    def sum_stats(self, value, channels, name, after=()):
        others = [self.chip(value, k) for k in range(1, self.ny)]
        return self.sum_group(add_stats(value, others, channels, name, after), name)

    def offsets(self, turn):
        masks = list(self.masks)
        if turn:
            masks[:2] = masks[1::-1]
        offsets = [0]
        for mask in masks[:0:-1]:
            offsets = offsets + [off ^ mask for off in offsets]
        return offsets, masks

    def borders(self, own, mate, edge):
        if self.ny == 2:
            straight = lax.ppermute(edge, "tensor", [(1, 3), (2, 0)])
            across = lax.ppermute(edge, "tensor", [(1, 2), (2, 1)])
            return [straight, across], [straight, across]
        c = lax.axis_index("tensor") % 2
        mate = jnp.concatenate(mate)
        head = jnp.where(c == 0, own, mate)[:MARGIN]
        foot = jnp.where(c == 0, mate, own)[own.shape[0] - MARGIN :]
        down = [(i, i + 2) for i in range(self.tensor - 2)]
        up = [(i + 2, i) for i in range(self.tensor - 2)]
        return [lax.ppermute(foot, "tensor", down)], [lax.ppermute(head, "tensor", up)]


class Pieces:
    def __init__(self, links, pieces, turns, name):
        self.links, self.name = links, name
        self.count = len(pieces)
        self.masks = [links.offsets(turn)[1] for turn in turns]
        self.kept = [kept for _, kept in pieces]
        self.at = 0
        self.send([sent for sent, _ in pieces])

    def send(self, sent):
        self.came = [self.links.group(sent[i], self.masks[i][self.at]) for i in range(self.count)]
        self.at += 1

    def step(self, after=()):
        if self.at < len(self.links.masks):
            made = halve_all(list(zip(self.kept, self.came)), self.name + "_half", after)
            self.kept = [kept for _, kept in made]
            self.send([sent for sent, _ in made])
        return self.kept[0]

    def finish(self):
        while self.at < len(self.links.masks):
            self.step()
        return [array for pair in zip(self.kept, self.came) for array in pair]


def finish_one(outs_of, ins_of, width_in, name):
    ins = outs_of + ins_of
    share = ins[0].shape[0]

    def kernel(*refs):
        out = refs[-1]
        parts = [wide(refs[2 * i]) + wide(refs[2 * i + 1]) for i in range(4)]
        out[1] = jnp.concatenate(parts[:2], axis=1)
        out[0] = jnp.concatenate(parts[2:], axis=1)

    return run(kernel, [((2, share, width_in), f32)], ins, (), name)[0]


def split_two(total, hidden, name, after=()):
    share = total.shape[0]

    def kernel(ref, out):
        for m in range(2):
            out[m] = wide(ref)[:, m * hidden : (m + 1) * hidden]

    return run(kernel, [((2, share, hidden), f32)], [total], after, name, mark=True)[0]


def split_heads(ins, cols, channels, name, after=()):
    share = ins[0].shape[0]

    def kernel(*refs):
        three, one, conv = refs[-3:]
        if len(ins) == 1:
            value, rest = wide(refs[0]), wide(refs[0])[:, 4 * cols :]
        else:
            value, rest = wide(refs[0]) + wide(refs[1]), wide(refs[2]) + wide(refs[3])
        for m in range(3):
            three[m] = value[:, m * cols : (m + 1) * cols]
            conv[m] = rest[:, m * channels : (m + 1) * channels]
        one[...] = value[:, 3 * cols : 4 * cols]

    outs = [((3, share, cols), f32), ((share, cols), f32), ((3, share, channels), f32)]
    return run(kernel, outs, list(ins), after, name, mark=True)


def pack_small(depthwise, bn_gain, bn_bias, name):
    channels = depthwise.shape[1]

    def kernel(taps, gain, bias, out):
        out[...] = jnp.concatenate(
            [taps[...], gain[...], bias[...], jnp.zeros((1, channels), f32)], axis=0
        )

    rows = [depthwise, bn_gain[None], bn_bias[None]]
    return run(kernel, [((8, channels), f32)], rows, (), name)[0]


def side_by_side(arrays, name):
    def kernel(*refs):
        refs[-1][...] = jnp.concatenate([ref[...] for ref in refs[:-1]], axis=1)

    shape = (arrays[0].shape[0], sum(array.shape[1] for array in arrays))
    return run(kernel, [(shape, f32)], arrays, (), name)[0]


def pack_sums(gains, table, name, after=()):
    width = gains[0].shape[1]
    each = width // 128

    def kernel(*refs):
        out = refs[-1]
        for g in range(5):
            for i in range(each):
                out[g * each + i : g * each + i + 1, :] = refs[g][0:1, i * 128 : (i + 1) * 128]
        out[5 * each :, :] = refs[5][...]

    return run(kernel, [((5 * each + 128, 128), f32)], list(gains) + [table], after, name)[0]


def with_taps(sums, taps, channels, name, after=()):
    def kernel(sum_ref, tap_ref, out):
        top = sums.shape[0]
        out[:top, :] = sum_ref[...]
        for i in range(channels // 128):
            out[top + 8 * i : top + 8 * i + 8, :] = tap_ref[:, i * 128 : (i + 1) * 128]

    rows = sums.shape[0] + 8 * (channels // 128)
    return run(kernel, [((rows, 128), f32)], [sums, taps], after, name)[0]


def unpack_sums(sums, bn_grads, width, channels, name):
    each = width // 128
    top = 5 * each + 128

    def kernel(sum_ref, bn_ref, gains, table, kernel_grad, gain_grad, bias_grad):
        for g in range(5):
            for i in range(each):
                gains[g : g + 1, i * 128 : (i + 1) * 128] = sum_ref[g * each + i : g * each + i + 1, :]
        table[...] = sum_ref[5 * each : 5 * each + REL, :]
        for i in range(channels // 128):
            at = top + 8 * i
            kernel_grad[:, i * 128 : (i + 1) * 128] = sum_ref[at : at + KERNEL, :]
        gain_grad[...] = bn_ref[0:1, :channels]
        bias_grad[...] = bn_ref[1:2, :channels]

    outs = [((5, width), f32), ((REL, 128), f32), ((KERNEL, channels), f32)] + [((1, channels), f32)] * 2
    return run(kernel, outs, [sums, bn_grads], (), name)


def own_share(weights, me, share, name, after=()):
    cols = weights.shape[2]

    def kernel(me_ref, ref, out):
        rows = pl.ds(pl.multiple_of(me_ref[0] * share, 16), share)
        for m in range(3):
            out[m * share : (m + 1) * share, :] = ref[m, rows, :]

    return run(
        kernel, [((3 * share, cols), bf16)], [me, weights], after, name, in_specs=[SMEM_SPEC, None]
    )[0]


def arrange(conv_proj, gathered, dp, name, after=()):
    _, width, channels = conv_proj.shape
    share = width // dp
    cols = channels * (1 + len(gathered))

    def kernel(own_ref, *refs):
        others, outs = refs[: len(gathered)], refs[len(gathered) :]
        for m in range(3):
            outs[m][:, :channels] = own_ref[m]
            for k, ref in enumerate(others):
                for b in range(dp):
                    at = (b * 3 + m) * share
                    outs[m][b * share : (b + 1) * share, (k + 1) * channels : (k + 2) * channels] = ref[
                        at : at + share, :
                    ]

    return run(kernel, [((width, cols), bf16)] * 3, [conv_proj] + gathered, after, name, mark=True)


def per_device(
    links,
    x_in,
    cotangent,
    lengths,
    norm_gains,
    ffn_first,
    attn_qkv,
    attn_out,
    rel_table,
    conv_proj,
    depthwise,
    bn_gain,
    bn_bias,
    running,
    ffn_second,
):
    MARKS.clear()
    ny = links.ny
    others = list(range(1, ny))
    rows, width = x_in.shape
    channels = bn_gain.shape[0]
    who = lax.axis_index("tensor").astype(jnp.int32).reshape(1)
    gains = norm_gains
    table = window_table(jnp.pad(rel_table, ((0, 128 - REL), (0, 0))))

    me = lax.axis_index("dp").astype(jnp.int32).reshape(1)
    share = width // links.dp
    halves_fit = share % 128 == 0
    small = pack_small(depthwise, bn_gain, bn_bias, "conv_small")
    small = side_by_side([small] + [links.chip(small, k) for k in others], "conv_small_all")

    def send_sums(parts, name, after=()):
        return add_up([parts[0], links.mate(parts[1])], name, after)

    def every(pieces):
        return [pieces[k] for k in range(ny)]

    def split(made):
        return (made[0], made[1 : 1 + PIECES]), made[1 + PIECES :]

    def all_parts(sums, k):
        return [sums[k]] + [links.chip(sums[k ^ j], j) for j in others]

    piece = own_share(conv_proj, me, share, "conv_share")
    came = [links.chip(piece, k) for k in others]
    gathered = [lax.all_gather(other, "dp", axis=0, tiled=True) for other in came]

    (normed, pieces), x_low = norm_rows(x_in, [], 0.0, gains, 0, "ln_in", keep=False, low=True)
    x_rows = [x_in] + [links.chip(x_low, k) for k in others]
    na_first, pre_first, hid_first, sums = {}, {}, {}, {}
    token = ()
    for k in range(ny):
        if k:
            ((normed, pieces),) = norm_rows(
                x_rows[k], [], 0.0, gains, 0, "ln_in", token + (small,), keep=False
            )
        parts, made = split(
            feed(normed, links.mate(pieces), ffn_first, "ffn_one", tuple(came) if k == 0 else ())
        )
        pre_first[k], hid_first[k], na_first[k] = made
        sums[k] = send_sums(parts, "ffn_one_sum")
        token = (sums[k],)

    token = ()
    na_attn, first, qkv, cot_low = {}, {}, None, None
    for k in others + [0]:
        also = cotangent if k == 0 else None
        made = norm_rows(
            x_rows[k], all_parts(sums, k), 0.5, gains, 1, "ln_attn", token, also=also
        )
        (normed, pieces), first[k] = made[:2]
        if k == 0:
            cot_low = made[2]
        qkv, na_attn[k] = qkv_rows(normed, links.mate(pieces), attn_qkv, k, SLOT, qkv, "qkv")
        token = (qkv,)
    cot_rows = [cotangent] + [links.chip(cot_low, k) for k in others]
    heads_out, probs = attend(qkv, who, lengths, table, rows)
    token = tuple(cot_rows[1:])
    arrived = []
    for k in others:
        parts, _ = split(out_rows(heads_out, attn_out, k, rows, "out_proj", token))
        total = send_sums(parts, "out_sum")
        arrived.append(links.chip(total, k))
        token = (total,)
    conv_w = arrange(conv_proj, gathered, links.dp, "conv_weights", token)
    token = token + (conv_w[0],)
    parts, _ = split(out_rows(heads_out, attn_out, 0, rows, "out_proj", token))
    edge = who if ny == 2 else None
    made = norm_rows(
        first[0], [parts[0], links.mate(parts[1])] + arrived, 1.0, gains, 2, "ln_conv", edge=edge
    )
    (normed, pieces), after_attn = made[:2]

    mate = links.mate(pieces)
    before, after_rows = links.borders(normed, mate, made[-1])
    linear, gating, mixture, tallies, conv_in = conv_mix(
        ny, who, lengths, normed, mate, before, after_rows, conv_w, small, "conv_mix"
    )
    tallies = links.sum_stats(tallies, channels, "bn_sum")
    active, *made = conv_out(who, mixture, tallies, small, running, conv_w[2], rows, "conv_out")
    parts, (updated,) = split(made)
    (normed, pieces), after_conv, low = norm_rows(
        after_attn, [parts[0], links.mate(parts[1])], 1.0, gains, 3, "ln_ffn_two", low=True
    )

    x_rows = [after_conv] + [links.chip(low, k) for k in others]
    na_last, pre_last, hid_last, sums = {}, {}, {}, {}
    token = ()
    for k in range(ny):
        if k:
            ((normed, pieces),) = norm_rows(
                x_rows[k], [], 0.0, gains, 3, "ln_ffn_two", token, keep=False
            )
        parts, made = split(feed(normed, links.mate(pieces), ffn_second, "ffn_two"))
        pre_last[k], hid_last[k], na_last[k] = made
        sums[k] = send_sums(parts, "ffn_two_sum")
        token = (sums[k],)

    token = ()
    upper, down, arrived = {}, {}, []
    for k in others + [0]:
        made = norm_last(
            x_rows[k],
            all_parts(sums, k),
            gains,
            cot_rows[k],
            who,
            k,
            lengths,
            "ln_last",
            k == 0,
            token,
        )
        normed, pieces = made[0]
        if k == 0:
            grad, output, gain_five = made[1:]
        parts, made = split(
            feed_grad(normed, links.mate(pieces), pre_last[k], ffn_second, "ffn_two_grad")
        )
        down[k], upper[k] = made
        if k:
            total = send_sums(parts, "ffn_two_grad_sum")
            arrived.append(links.chip(total, k))
            token = (total,)
    made = norm_grad(
        after_conv,
        [parts[0], links.mate(parts[1])] + arrived,
        gains,
        3,
        grad,
        "back_ffn_two",
        factor=1.0,
        edge=edge,
    )
    (low, pieces), grad, gain_four = made[:3]

    mate = links.mate(pieces)
    before, after_rows = links.borders(low, mate, made[-1])
    dz, sums, conv_up = conv_shift_grad(
        ny, who, lengths, low, mate, before, after_rows, mixture, tallies, small, conv_w[2], "conv_dz"
    )
    two_sum = outer(
        [(every(na_last), [every(down)]), (every(upper), [every(hid_last)])], "ffn_two_w", (sums,)
    )
    def by_chip(left, rights, name, after):
        made = []
        for k in range(ny):
            spans = [[(right, None, k * channels, (k + 1) * channels)] for right in rights]
            made.append(outer([([left], spans)], name, after))
        return [made[0]] + [links.chip(made[k], k) for k in others]

    came = [links.chip(sums, k) for k in others]
    bn_grads = add_stats(sums, came, channels, "bn_grad_sum", (two_sum,))
    out_grad = by_chip(conv_up, [active], "conv_out_w", (bn_grads,))
    bn_grads = links.sum_group(bn_grads, "bn_grad_sum")
    two_sum = links.scatter_grad(two_sum)
    grad_linear, grad_gate, *made = conv_in_grad(
        who,
        lengths,
        dz,
        mixture,
        tallies,
        bn_grads,
        small,
        small,
        linear,
        gating,
        conv_w,
        rows,
        "conv_din",
        tuple(out_grad[1:]),
    )
    parts, (tap_grad,) = split(made)
    (low, pieces), grad, gain_three = norm_grad(
        after_attn, [parts[0], links.mate(parts[1])], gains, 2, grad, "back_conv", factor=1.0
    )

    g_rows = [low] + [links.chip(low, k) for k in others]
    in_grads = by_chip(conv_in, [grad_linear, grad_gate], "conv_in_w", (low,))
    token = (in_grads[0],)
    grad_heads = None
    upper_attn = {}
    for k in range(ny):
        mate = links.mate(pieces) if k == 0 else [links.core(g_rows[k])]
        grad_heads, upper_attn[k] = heads_rows(
            g_rows[k], mate, attn_out, k, SLOT, grad_heads, "dheads", token
        )
        token = (grad_heads,)
    members, table_grad = attend_back(qkv, grad_heads, probs, who, table, rows)
    token = ()
    sums = {}
    for k in range(ny):
        parts, _ = split(members_rows(members, attn_qkv, k, rows, "dqkv", token))
        sums[k] = send_sums(parts, "dqkv_sum")
        token = (sums[k],)
    heads_jobs = [
        (every(na_attn), [[(members, m)] for m in range(3)]),
        (every(upper_attn), [[heads_out]]),
    ]
    conv_grads = [in_grads, out_grad]
    if halves_fit:
        made = outer_halves(links, heads_jobs, 0, "attn_w", token)
        halves = [made, outer_halves(links, [], 1, "conv_w", (made[0],), conv_grads)]
        heads_sum = Pieces(links, halves, (0, 1), "heads")
        token = (halves[1][0],)
    else:
        heads_sum = outer(heads_jobs, "attn_w", token, conv_grads)
        token = (heads_sum,)
        heads_sum = links.scatter_grad(heads_sum)

    upper, down, arrived = {}, {}, []
    for k in others + [0]:
        made = norm_grad(
            first[k],
            all_parts(sums, k),
            gains,
            1,
            grad if k == 0 else g_rows[k],
            "back_attn",
            token,
            factor=0.5,
            keep=k == 0,
            sums=k == 0,
        )
        normed, pieces = made[0]
        if k == 0:
            grad, gain_two = made[1:]
        parts, made = split(
            feed_grad(normed, links.mate(pieces), pre_first[k], ffn_first, "ffn_one_grad")
        )
        down[k], upper[k] = made
        if k:
            total = send_sums(parts, "ffn_one_grad_sum")
            arrived.append(links.chip(total, k))
            token = (total,)
            if halves_fit and k == others[-1]:
                token = (heads_sum.step(token),)
    hidden = ffn_first.shape[2]
    half = hidden // 2
    token = (parts[0],)
    pairs = []
    if halves_fit:
        sides_of = ((every(upper), every(hid_first), (0, 0)), (every(na_first), every(down), (1, 0)))
        for left, right, turns in sides_of:
            halves = []
            for i, turn in enumerate(turns):
                columns = [(r, None, i * half, (i + 1) * half) for r in right]
                halves.append(outer_halves(links, [(left, [columns])], turn, "ffn_one_w", token))
                token = (halves[-1][0],)
            pairs.append(Pieces(links, halves, turns, "one"))
    else:
        first_sum = outer(
            [(every(na_first), [every(down)]), (every(upper), [every(hid_first)])], "ffn_one_w", token
        )
        token = (first_sum,)
        first_sum = links.scatter_grad(first_sum)
    if halves_fit:
        token = (heads_sum.step(token),)
    for pair in pairs:
        token = (pair.step(token),)
    heads_parts = heads_sum.finish() if halves_fit else [heads_sum]
    qkv_sum, out_sum, conv_sum = split_heads(
        heads_parts, attn_qkv.shape[2], channels, "heads_end", token
    )
    token = (out_sum,)
    for pair in pairs[:1]:
        token = (pair.step(token),)
    grad_input, gain_one = norm_grad(
        x_in, [parts[0], links.mate(parts[1])] + arrived, gains, 0, grad, "back_ffn_one", token
    )

    taps = add_stats(tap_grad, [links.chip(tap_grad, k) for k in others], channels, "taps_sum")
    bundle = pack_sums([gain_one, gain_two, gain_three, gain_four, gain_five], table_grad, "pack")
    bundle = add_stats(bundle, [links.core(bundle)], 0, "bundle_sum")
    for k in [1 << bit for bit in range(ny.bit_length() - 1)]:
        bundle = add_stats(bundle, [links.chip(bundle, k)], 0, "bundle_sum")
    token = (bundle,)
    for pair in pairs[1:]:
        token = (pair.step(token),)
    bundle = with_taps(bundle, taps, channels, "pack_taps", token)
    last_sum = split_two(two_sum, hidden, "two_end", token)
    for mask in links.masks:
        bundle = add_stats(bundle, [links.group(bundle, mask)], 0, "bundle_sum")
    norm_sums, table_sums, kernel_grad, gain_grad, bias_grad = unpack_sums(
        bundle, bn_grads, width, channels, "unpack"
    )
    if pairs:
        first_sum = finish_one(pairs[0].finish(), pairs[1].finish(), hidden, "one_end")
    else:
        first_sum = split_two(first_sum, hidden, "one_end")
    return (
        output,
        grad_input,
        norm_sums,
        first_sum,
        qkv_sum,
        out_sum,
        table_sums,
        conv_sum,
        kernel_grad,
        gain_grad.reshape(-1),
        bias_grad.reshape(-1),
        updated,
        last_sum,
    )


def solution(mesh):
    links = Links(mesh.shape["dp"], mesh.shape["tensor"])
    placed = (
        P(("dp", "tensor"), None),
        P(("dp", "tensor"), None),
        P("dp"),
        P(),
        P(None, None, "tensor"),
        P(None, None, "tensor"),
        P(None, "tensor"),
        P(),
        P(None, None, "tensor"),
        P(None, "tensor"),
        P("tensor"),
        P("tensor"),
        P(None, "tensor"),
        P(None, None, "tensor"),
    )
    return jax.shard_map(
        functools.partial(per_device, links),
        mesh=mesh,
        in_specs=placed,
        out_specs=(
            P(("dp", "tensor"), None),
            P(("dp", "tensor"), None),
            P(),
            P(None, "dp", "tensor"),
            P(None, "dp", "tensor"),
            P("dp", "tensor"),
            P(),
            P(None, "dp", "tensor"),
            P(None, "tensor"),
            P("tensor"),
            P("tensor"),
            P(None, "tensor"),
            P(None, "dp", "tensor"),
        ),
        check_vma=False,
    )
```

```python
import functools

import jax
import jax.numpy as jnp
from jax import lax
from jax.experimental import pallas as pl
from jax.experimental.pallas import tpu as pltpu
from jax.sharding import PartitionSpec as P

HEAD = 128
KERNEL = 5
LEFT = 64
RIGHT = 8
SLOT = 1024
REL = 73
MARGIN = 16
SUB = 128
BLK = 256
WIN = 3 * SUB
WRAP = 512
LOG2E = 1.4426950408889634
VMEM_CAP = 32 * 1024 * 1024

eps_norm = 1e-05
momentum = 0.5
bf16 = jnp.bfloat16
f32 = jnp.float32


def nn(left_op, right_op):
    return lax.dot_general(
        left_op, right_op, (((1,), (0,)), ((), ())), preferred_element_type=f32
    )


def nt(left_op, right_op):
    return lax.dot_general(
        left_op, right_op, (((1,), (1,)), ((), ())), preferred_element_type=f32
    )


def tn(left_op, right_op):
    return lax.dot_general(
        left_op, right_op, (((0,), (0,)), ((), ())), preferred_element_type=f32
    )


def window_table(rel_table):
    width=rel_table.shape[1]
    def kernel(table_ref, hi_ref, lo_ref):
        pick=spots(0)
        table=table_ref[...]
        hi=table.astype(jnp.bfloat16)
        lo=(table-hi.astype(jnp.float32)).astype(jnp.bfloat16)
        hi_ref[...]=nn(pick,hi).astype(jnp.bfloat16)
        lo_ref[...]=nn(pick,lo).astype(jnp.bfloat16)
    return run(kernel,[((WRAP,width),jnp.bfloat16)]*2,[rel_table],(),"window_table")

def spots(axis):
    shape=(WRAP,128) if axis==0 else (128,WRAP)
    u=lax.broadcasted_iota(jnp.int32,shape,axis)
    row=lax.broadcasted_iota(jnp.int32,shape,1-axis)
    dist=jnp.where(u<=WIN,jnp.clip(u-SUB,-LEFT,RIGHT),-LEFT)+LEFT
    return (dist==row).astype(jnp.bfloat16)

def order_in(dst, src, who, rows):
    for j in range(SLOT//rows):
        dst[j*rows:(j+1)*rows,:]=src[pl.ds(pl.multiple_of((j^who)*rows,rows),rows),:]

def attend_kernel(rows, who_ref, len_ref, q_ref, k_ref, v_ref, hi_ref, lo_ref, o_ref, p_ref, qs, ks, vs):
    who=who_ref[0]
    length=len_ref[0]
    order_in(qs,q_ref.at[0],who,rows); order_in(ks,k_ref.at[0],who,rows); order_in(vs,v_ref.at[0],who,rows)
    factor=HEAD**(-0.5)*LOG2E
    tail=lax.broadcasted_iota(jnp.int32,(SUB,SLOT//2),1)+SLOT//2<length
    for base in range(0,SLOT,BLK):
        q=qs[base:base+BLK,:]
        content=nt(q,ks[...])
        spread=nt(q,hi_ref[...])+nt(q,lo_ref[...])
        for off in range(0,BLK,SUB):
            i0=base+off
            e=spread[off:off+SUB]
            rolled=pltpu.roll(e,0,1,stride=1,stride_axis=0)
            lo_c=max(i0-SUB,0); hi_c=min(i0+2*SUB,SLOT)
            parts=[]
            if lo_c>0: parts.append(content[off:off+SUB,:lo_c]+e[:,0:1])
            parts.append(content[off:off+SUB,lo_c:hi_c]+rolled[:,lo_c-(i0-SUB):hi_c-(i0-SUB)])
            if hi_c<SLOT: parts.append(content[off:off+SUB,hi_c:]+e[:,WIN-1:WIN])
            logit=jnp.concatenate(parts,axis=1)*factor
            logit=jnp.concatenate([logit[:,:SLOT//2],jnp.where(tail,logit[:,SLOT//2:],-1e30)],axis=1)
            peak=jnp.max(logit,axis=1,keepdims=True)
            ex=jnp.exp2(logit-peak)
            tot=jnp.sum(ex,axis=1,keepdims=True)
            p_ref[0,i0:i0+SUB,:]=(ex*(1.0/tot)).astype(jnp.bfloat16)
        out=nn(p_ref[0,base:base+BLK,:],vs[...]).astype(jnp.bfloat16)
        for part in range(0,BLK,rows) if rows<BLK else (0,):
            n=min(rows,BLK)
            j=(base+part)//rows; inner=(base+part)%rows
            o_ref[pl.ds(pl.multiple_of((j^who)*rows+inner,n),n),:]=out[part:part+n]

def attend(qkv, who, length, table, rows):
    heads=qkv.shape[2]//HEAD
    hi,lo=table
    spec=lambda m: pl.BlockSpec((1,SLOT,HEAD),lambda h,m=m:(m,0,h))
    tab=pl.BlockSpec((WRAP,HEAD),lambda h:(0,0))
    return run(
        functools.partial(attend_kernel,rows),
        [((SLOT,heads*HEAD),jnp.bfloat16),((heads,SLOT,SLOT),jnp.bfloat16)],
        [who,length,qkv,qkv,qkv,hi,lo],
        (),"attend",grid=(heads,),
        in_specs=[SMEM_SPEC,SMEM_SPEC,spec(0),spec(1),spec(2),tab,tab],
        out_specs=[pl.BlockSpec((SLOT,HEAD),lambda h:(0,h)),pl.BlockSpec((1,SLOT,SLOT),lambda h:(h,0,0))],
        scratch=[pltpu.VMEM((SLOT,HEAD),jnp.bfloat16)]*3,
        room=28,work=heads*32*SLOT*SLOT*HEAD,
    )

def attend_back_kernel(rows, heads, who_ref, q_ref, k_ref, v_ref, g_ref, p_ref, hi_ref, lo_ref, d_ref, dt_ref, qs, ks, vs, gs, dkt, dvt):
    who=who_ref[0]
    for dst,src in ((qs,q_ref.at[0]),(ks,k_ref.at[0]),(vs,v_ref.at[0]),(gs,g_ref)):
        order_in(dst,src,who,rows)
    factor=HEAD**(-0.5)
    first=hi_ref[0:1,:].astype(jnp.float32)+lo_ref[0:1,:].astype(jnp.float32)
    final=hi_ref[WIN-1:WIN,:].astype(jnp.float32)+lo_ref[WIN-1:WIN,:].astype(jnp.float32)
    zero=jnp.zeros((SUB,SUB),jnp.float32)
    flip=(lax.broadcasted_iota(jnp.int32,(SUB,SUB),0)+lax.broadcasted_iota(jnp.int32,(SUB,SUB),1)==SUB-1).astype(jnp.bfloat16)
    table_acc=jnp.zeros((HEAD,WRAP),jnp.float32)
    left_acc=jnp.zeros((1,HEAD),jnp.float32)
    right_acc=jnp.zeros((1,HEAD),jnp.float32)
    for base in range(0,SLOT,BLK):
        q=qs[base:base+BLK,:]
        g=gs[base:base+BLK,:]
        pb=p_ref[0,base:base+BLK,:]
        p=pb.astype(jnp.float32)
        dp=nt(g,vs[...])
        delta=jnp.sum(p*dp,axis=1,keepdims=True)
        dsb=(p*(dp-delta)).astype(jnp.bfloat16)
        dv_part=tn(g,pb)
        dk_part=tn(q,dsb)
        if base==0:
            dvt[...]=dv_part; dkt[...]=dk_part
        else:
            dvt[...]+=dv_part; dkt[...]+=dk_part
        dq=nn(dsb,ks[...])
        ds=dsb.astype(jnp.float32)
        qf=q.astype(jnp.float32)
        extra=[]
        for off in range(0,BLK,SUB):
            i0=base+off
            d=ds[off:off+SUB]
            lo_c=max(i0-SUB,0); hi_c=min(i0+2*SUB,SLOT)
            turned=nn(flip,dsb[off:off+SUB,lo_c:hi_c])
            win=[zero]*((lo_c-(i0-SUB))//SUB)+[turned]+[zero]*((i0+2*SUB-hi_c)//SUB+1)
            moved=pltpu.roll(jnp.concatenate(win,axis=1),WRAP-SUB+1,1,stride=1,stride_axis=0)
            u=nn(flip,moved.astype(jnp.bfloat16)).astype(jnp.bfloat16)
            add=nn(u,hi_ref[...])+nn(u,lo_ref[...])
            table_acc=table_acc+tn(q[off:off+SUB],u)
            if lo_c>0:
                s=jnp.sum(d[:,:lo_c],axis=1,keepdims=True)
                add=add+s*first
                left_acc=left_acc+jnp.sum(s*qf[off:off+SUB],axis=0,keepdims=True)
            if hi_c<SLOT:
                s=jnp.sum(d[:,hi_c:],axis=1,keepdims=True)
                add=add+s*final
                right_acc=right_acc+jnp.sum(s*qf[off:off+SUB],axis=0,keepdims=True)
            extra.append(add)
        dq=((dq+jnp.concatenate(extra,axis=0))*factor).astype(jnp.bfloat16)
        for part in range(0,BLK,rows) if rows<BLK else (0,):
            n=min(rows,BLK)
            j=(base+part)//rows; inner=(base+part)%rows
            d_ref[0,pl.ds(pl.multiple_of((j^who)*rows+inner,n),n),:]=dq[part:part+n]
    spread=table_acc*factor
    upper=spread.astype(jnp.bfloat16)
    lower=(spread-upper.astype(jnp.float32)).astype(jnp.bfloat16)
    pick=spots(1)
    gathered=nt(pick,upper)+nt(pick,lower)
    row=lax.broadcasted_iota(jnp.int32,(128,1),0)
    gathered=gathered+jnp.where(row==0,left_acc*factor,0.0)+jnp.where(row==LEFT+RIGHT,right_acc*factor,0.0)
    @pl.when(pl.program_id(0)==0)
    def _():
        dt_ref[...]=gathered
    @pl.when(pl.program_id(0)>0)
    def _():
        dt_ref[...]+=gathered
    for j in range(SLOT//rows):
        sl=pl.ds(pl.multiple_of((j^who)*rows,rows),rows)
        d_ref[1,sl,:]=(jnp.transpose(dkt[:,j*rows:(j+1)*rows])*factor).astype(jnp.bfloat16)
        d_ref[2,sl,:]=jnp.transpose(dvt[:,j*rows:(j+1)*rows]).astype(jnp.bfloat16)

def attend_back(qkv, grad, probs, who, table, rows):
    heads=qkv.shape[2]//HEAD
    hi,lo=table
    spec=lambda m: pl.BlockSpec((1,SLOT,HEAD),lambda h,m=m:(m,0,h))
    tab=pl.BlockSpec((WRAP,HEAD),lambda h:(0,0))
    return run(
        functools.partial(attend_back_kernel,rows,heads),
        [((3,SLOT,heads*HEAD),jnp.bfloat16),((128,HEAD),jnp.float32)],
        [who,qkv,qkv,qkv,grad,probs,hi,lo],
        (),"attend_back",grid=(heads,),
        in_specs=[SMEM_SPEC,spec(0),spec(1),spec(2),pl.BlockSpec((SLOT,HEAD),lambda h:(0,h)),pl.BlockSpec((1,SLOT,SLOT),lambda h:(h,0,0)),tab,tab],
        out_specs=[pl.BlockSpec((3,SLOT,HEAD),lambda h:(0,0,h)),pl.BlockSpec((128,HEAD),lambda h:(0,0))],
        scratch=[pltpu.VMEM((SLOT,HEAD),jnp.bfloat16)]*4+[pltpu.VMEM((HEAD,SLOT),jnp.float32)]*2,
        room=28,work=heads*50*SLOT*SLOT*HEAD,
    )


MARKS = {}
PIECES = 4


class Stack:
    def __init__(self, refs):
        self.refs = refs

    def __getitem__(self, index):
        return jnp.concatenate([ref[index] for ref in self.refs], axis=0)


def run(
    kernel,
    outs,
    ins,
    after=(),
    name=None,
    grid=None,
    in_specs=None,
    out_specs=None,
    scratch=(),
    aliases=None,
    room=24,
    work=1 << 20,
    mark=False,
):
    after = [MARKS[id(item)][1] if id(item) in MARKS else item for item in after]
    waits = len(after)
    outs = list(outs) + [((8, 128), f32)] * mark
    sizes = [len(item) if isinstance(item, list) else 0 for item in ins]

    def body(*refs):
        args, at = [], 0
        for size in sizes:
            args.append(Stack(refs[at : at + size]) if size else refs[at])
            at += max(size, 1)
        last = at + waits + len(outs) - mark
        kernel(*args, *refs[at + waits : last], *refs[last + mark :])
        if mark:
            refs[last][...] = jnp.zeros((8, 128), f32)

    def full(shape):
        return pl.BlockSpec(tuple(shape), lambda i: (0,) * len(shape))

    if grid is None:
        grid = (1,)
    given = list(in_specs) if in_specs is not None else [None] * len(ins)
    specs, flat, start = [], [], []
    for item, spec, size in zip(ins, given, sizes):
        start.append(len(flat))
        if spec is None:
            spec = full((item[0] if size else item).shape)
        elif size:
            shape = spec.block_shape
            spec = pl.BlockSpec((shape[0] // size,) + tuple(shape[1:]), spec.index_map)
        specs += [spec] * max(size, 1)
        flat += item if size else [item]
    ins = flat
    if out_specs is None:
        out_specs = [full(shape) for shape, _ in outs]
    else:
        out_specs = list(out_specs) + [pl.BlockSpec((8, 128), lambda i: (0, 0))] * mark
    made = pl.pallas_call(
        body,
        in_specs=specs + [pl.BlockSpec(memory_space=pl.ANY)] * waits,
        out_specs=out_specs,
        out_shape=[jax.ShapeDtypeStruct(shape, dtype) for shape, dtype in outs],
        scratch_shapes=list(scratch),
        input_output_aliases={start[i]: o for i, o in (aliases or {}).items()},
        compiler_params=pltpu.CompilerParams(vmem_limit_bytes=room << 20),
        cost_estimate=pl.CostEstimate(flops=0, bytes_accessed=0, transcendentals=0),
        name=name,
        grid=grid,
    )(*ins, *after)
    if not mark:
        return list(made)
    for array in made[:-1]:
        MARKS[id(array)] = (array, made[-1])
    return list(made[:-1])


SMEM_SPEC = pl.BlockSpec(memory_space=pltpu.SMEM)


def moments(rows):
    centred = rows - jnp.mean(rows, axis=1, keepdims=True)
    inverse = lax.rsqrt(jnp.mean(centred * centred, axis=1, keepdims=True) + eps_norm)
    return centred * inverse, inverse


def back(weighted, normed, inverse):
    first_mean = jnp.mean(weighted, axis=1, keepdims=True)
    second_mean = jnp.mean(weighted * normed, axis=1, keepdims=True)
    return inverse * (weighted - first_mean - normed * second_mean)


def wide(ref):
    return ref[...].astype(f32)


def cut(shape):
    return [((shape[0] // PIECES,) + tuple(shape[1:]), bf16)] * PIECES


def put(refs, value):
    rows = value.shape[0] // len(refs)
    for i, ref in enumerate(refs):
        ref[...] = value[i * rows : (i + 1) * rows].astype(bf16)


def take(items, count):
    return [items.pop(0) for _ in range(count)]


def add_up(parts, name, after=()):
    shape = parts[0].shape

    def kernel(*refs):
        total = wide(refs[0])
        for ref in refs[1:-1]:
            total = total + wide(ref)
        refs[-1][...] = total.astype(bf16)

    return run(kernel, [(shape, bf16)], parts, after, name)[0]


def total_of(refs):
    total = wide(refs[0])
    for ref in refs[1:]:
        total = total + wide(ref)
    return total


def gain_row(ref, index):
    return ref[index : index + 1, :]


def put_edge(ref, who, value):
    value = value.astype(f32)
    ref[...] = jnp.where(who // 2 == 0, value[-MARGIN:], value[:MARGIN]).astype(bf16)


def norm_rows(
    resid, parts, factor, gains, index, name, after=(), keep=True, low=False, also=None, edge=None
):
    shape = resid.shape
    count = len(parts)
    extra = ([also] if also is not None else []) + ([edge] if edge is not None else [])
    ins = [resid, gains] + list(parts) + extra
    outs = [(shape, bf16)] + cut(shape) + [(shape, f32)] * keep + [(shape, bf16)] * low
    outs = outs + [(shape, bf16)] * (also is not None)
    outs = outs + [((MARGIN, shape[1]), bf16)] * (edge is not None)

    def kernel(resid_ref, gain_ref, *refs):
        refs = list(refs)
        part_refs = take(refs, count)
        also_ref = take(refs, also is not None)
        edge_ref = take(refs, edge is not None)
        rows = wide(resid_ref)
        if count:
            rows = rows + factor * total_of(part_refs)
        normed = (moments(rows)[0] * gain_row(gain_ref, index)).astype(bf16)
        refs.pop(0)[...] = normed
        put(take(refs, PIECES), normed)
        if keep:
            refs.pop(0)[...] = rows
        if low:
            refs.pop(0)[...] = rows.astype(bf16)
        if also_ref:
            refs.pop(0)[...] = also_ref[0][...].astype(bf16)
        if edge_ref:
            put_edge(refs.pop(0), edge_ref[0][0], normed)

    specs = [None] * (2 + count + (also is not None)) + [SMEM_SPEC] * (edge is not None)
    made = run(kernel, outs, ins, after, name, in_specs=specs)
    return [(made[0], made[1 : 1 + PIECES])] + made[1 + PIECES :]


def norm_last(resid, parts, gains, upper, who, k, length, name, full, after=()):
    shape = resid.shape
    count = len(parts)
    outs = [(shape, bf16)] + cut(shape)
    if full:
        outs = outs + [(shape, f32), (shape, f32), ((8, shape[1]), f32)]

    def kernel(who_ref, length_ref, resid_ref, gain_ref, upper_ref, *refs):
        refs = list(refs)
        rows = wide(resid_ref) + 0.5 * total_of(take(refs, count))
        gain = gain_row(gain_ref, 4)
        normed, inverse = moments(rows)
        begin = (who_ref[0] ^ (2 * k)) * shape[0]
        place = lax.broadcasted_iota(jnp.int32, (shape[0], 1), 0) + begin
        valid = (place < length_ref[0]).astype(f32)
        seen = wide(upper_ref) * valid
        grad = back(seen * gain, normed, inverse)
        rounded = (0.5 * grad).astype(bf16)
        refs.pop(0)[...] = rounded
        put(take(refs, PIECES), rounded)
        if full:
            refs.pop(0)[...] = grad
            refs.pop(0)[...] = normed * gain * valid
            refs.pop(0)[...] = jnp.broadcast_to(
                jnp.sum(seen * normed, axis=0, keepdims=True), (8, shape[1])
            )

    ins = [who, length, resid, gains, upper] + list(parts)
    specs = [SMEM_SPEC, SMEM_SPEC] + [None] * (3 + count)
    made = run(kernel, outs, ins, after, name, in_specs=specs)
    return [(made[0], made[1 : 1 + PIECES])] + made[1 + PIECES :]


def norm_grad(
    rows_in, parts, gains, index, grad, name, after=(), factor=None, keep=True, sums=True, edge=None
):
    shape = rows_in.shape
    count = len(parts)
    outs = ([(shape, bf16)] + cut(shape)) if factor is not None else []
    outs = outs + [(shape, f32)] * keep + [((8, shape[1]), f32)] * sums
    outs = outs + [((MARGIN, shape[1]), bf16)] * (edge is not None)

    def kernel(rows_ref, gain_ref, grad_ref, *refs):
        refs = list(refs)
        total = total_of(take(refs, count))
        edge_ref = take(refs, edge is not None)
        normed, inverse = moments(wide(rows_ref))
        result = wide(grad_ref) + back(total * gain_row(gain_ref, index), normed, inverse)
        if factor is not None:
            rounded = (factor * result).astype(bf16)
            refs.pop(0)[...] = rounded
            put(take(refs, PIECES), rounded)
        if keep:
            refs.pop(0)[...] = result
        if sums:
            refs.pop(0)[...] = jnp.broadcast_to(
                jnp.sum(total * normed, axis=0, keepdims=True), (8, shape[1])
            )
        if edge_ref:
            put_edge(refs.pop(0), edge_ref[0][0], rounded)

    ins = [rows_in, gains, grad] + list(parts) + ([edge] if edge is not None else [])
    specs = [None] * (3 + count) + [SMEM_SPEC] * (edge is not None)
    made = run(kernel, outs, ins, after, name, in_specs=specs)
    if factor is None:
        return made
    return [(made[0], made[1 : 1 + PIECES])] + made[1 + PIECES :]


def add_stats(value, others, channels, name, after=()):
    cols = value.shape[1]
    ny = cols // channels if channels else 0

    def kernel(*refs):
        total = refs[0][...]
        for k, ref in enumerate(refs[1:-1], 1):
            if channels:
                total = total + jnp.concatenate(
                    [ref[:, (r ^ k) * channels : ((r ^ k) + 1) * channels] for r in range(ny)], axis=1
                )
            else:
                total = total + ref[...]
        refs[-1][...] = total

    return run(kernel, [(value.shape, f32)], [value] + list(others), after, name)[0]


def add_four(value, others, channels, name, after=()):
    def kernel(a, b, c, d, out):
        rest = c[...] + d[...]
        if channels:
            rest = jnp.concatenate([rest[:, channels:], rest[:, :channels]], axis=1)
        out[...] = (a[...] + b[...]) + rest

    return run(kernel, [(value.shape, f32)], [value] + others, after, name)[0]


def tile_of(total, most):
    return most if total % most == 0 else total


def feed(own, mate, weights, name, after=()):
    rows, width = own.shape
    hidden = weights.shape[2]
    tile = tile_of(hidden, 1024)
    steps = hidden // tile

    def kernel(own_ref, mate_ref, in_ref, out_ref, p_own, *rest):
        *p_mate, pre, hid, seen = rest[: PIECES + 3]
        acc = rest[PIECES + 3] if steps > 1 else None
        step = pl.program_id(0)
        both = jnp.concatenate([own_ref[...], mate_ref[...]], axis=0)
        seen[...] = both
        value = nn(both, in_ref[0])
        act = (value / (1.0 + jnp.exp(-value))).astype(bf16)
        pre[...] = value.astype(bf16)
        hid[...] = act
        part = nt(act, out_ref[0])
        if steps == 1:
            p_own[...] = part[:rows].astype(bf16)
            put(p_mate, part[rows:])
            return

        @pl.when(step == 0)
        def _():
            acc[...] = part

        @pl.when(step > 0)
        def _():
            acc[...] += part

        @pl.when(step == steps - 1)
        def _():
            p_own[...] = acc[:rows].astype(bf16)
            put(p_mate, acc[rows:])

    fixed = pl.BlockSpec((rows, width), lambda i: (0, 0))
    quarter = [pl.BlockSpec((rows // PIECES, width), lambda i: (0, 0))] * PIECES
    cols = pl.BlockSpec((2 * rows, tile), lambda i: (0, i))
    weight = [pl.BlockSpec((1, width, tile), lambda i, m=m: (m, 0, i)) for m in range(2)]
    return run(
        kernel,
        [((rows, width), bf16)] + cut((rows, width)) + [((2 * rows, hidden), bf16)] * 2 + [((2 * rows, width), bf16)],
        [own, mate, weights, weights],
        after,
        name,
        grid=(steps,),
        in_specs=[fixed, fixed] + weight,
        out_specs=[fixed] + quarter + [cols, cols, pl.BlockSpec((2 * rows, width), lambda i: (0, 0))],
        scratch=[pltpu.VMEM((2 * rows, width), f32)] if steps > 1 else (),
        room=28,
        work=8 * rows * width * hidden,
    )


def feed_grad(own, mate, pre, weights, name, after=()):
    rows, width = own.shape
    hidden = weights.shape[2]
    tile = tile_of(hidden, 1024)
    steps = hidden // tile

    def kernel(own_ref, mate_ref, pre_ref, in_ref, out_ref, p_own, *rest):
        *p_mate, down, seen = rest[: PIECES + 2]
        acc = rest[PIECES + 2] if steps > 1 else None
        step = pl.program_id(0)
        both = jnp.concatenate([own_ref[...], mate_ref[...]], axis=0)
        seen[...] = both
        value = nn(both, out_ref[0])
        preact = wide(pre_ref)
        logistic = 1.0 / (1.0 + jnp.exp(-preact))
        slope = logistic * (1.0 + preact * (1.0 - logistic))
        grad = (value * slope).astype(bf16)
        down[...] = grad
        part = nt(grad, in_ref[0])
        if steps == 1:
            p_own[...] = part[:rows].astype(bf16)
            put(p_mate, part[rows:])
            return

        @pl.when(step == 0)
        def _():
            acc[...] = part

        @pl.when(step > 0)
        def _():
            acc[...] += part

        @pl.when(step == steps - 1)
        def _():
            p_own[...] = acc[:rows].astype(bf16)
            put(p_mate, acc[rows:])

    fixed = pl.BlockSpec((rows, width), lambda i: (0, 0))
    quarter = [pl.BlockSpec((rows // PIECES, width), lambda i: (0, 0))] * PIECES
    cols = pl.BlockSpec((2 * rows, tile), lambda i: (0, i))
    weight = [pl.BlockSpec((1, width, tile), lambda i, m=m: (m, 0, i)) for m in range(2)]
    return run(
        kernel,
        [((rows, width), bf16)] + cut((rows, width)) + [((2 * rows, hidden), bf16), ((2 * rows, width), bf16)],
        [own, mate, pre, weights, weights],
        after,
        name,
        grid=(steps,),
        in_specs=[fixed, fixed, cols] + weight,
        out_specs=[fixed] + quarter + [cols, pl.BlockSpec((2 * rows, width), lambda i: (0, 0))],
        scratch=[pltpu.VMEM((2 * rows, width), f32)] if steps > 1 else (),
        room=28,
        work=8 * rows * width * hidden,
    )


def qkv_rows(own, mate, weights, k, total, held, name, after=()):
    rows, width = own.shape
    cols = weights.shape[2]

    def kernel(own_ref, mate_ref, w_ref, *refs):
        both = jnp.concatenate([own_ref[...], mate_ref[...]], axis=0)
        refs[-1][...] = both
        refs[-2][0] = nn(both, w_ref[0]).astype(bf16)

    fixed = pl.BlockSpec((rows, width), lambda i: (0, 0))
    quarter = [pl.BlockSpec((rows // PIECES, width), lambda i: (0, 0))] * PIECES
    ins = [own, mate, weights] + ([held] if held is not None else [])
    specs = [fixed, fixed, pl.BlockSpec((1, width, cols), lambda i: (i, 0, 0))]
    specs = specs + [pl.BlockSpec(memory_space=pl.ANY)] * (held is not None)
    return run(
        kernel,
        [((3, total, cols), bf16), ((2 * rows, width), bf16)],
        ins,
        after,
        name,
        grid=(3,),
        in_specs=specs,
        out_specs=[
            pl.BlockSpec((1, 2 * rows, cols), lambda i: (i, k, 0)),
            pl.BlockSpec((2 * rows, width), lambda i: (0, 0)),
        ],
        work=12 * rows * width * cols,
        aliases={3: 0} if held is not None else None,
    )


def heads_rows(own, mate, weight, k, total, held, name, after=()):
    rows, width = own.shape
    cols = weight.shape[1]

    def kernel(own_ref, mate_ref, w_ref, *refs):
        both = jnp.concatenate([own_ref[...], mate_ref[...]], axis=0)
        refs[-1][...] = both
        refs[-2][...] = nn(both, w_ref[...]).astype(bf16)

    fixed = pl.BlockSpec((rows, width), lambda i: (0, 0))
    quarter = [pl.BlockSpec((rows // PIECES, width), lambda i: (0, 0))] * PIECES
    ins = [own, mate, weight] + ([held] if held is not None else [])
    specs = [fixed, fixed, pl.BlockSpec((width, cols), lambda i: (0, 0))]
    specs = specs + [pl.BlockSpec(memory_space=pl.ANY)] * (held is not None)
    return run(
        kernel,
        [((total, cols), bf16), ((2 * rows, width), bf16)],
        ins,
        after,
        name,
        grid=(1,),
        in_specs=specs,
        out_specs=[
            pl.BlockSpec((2 * rows, cols), lambda i: (k, 0)),
            pl.BlockSpec((2 * rows, width), lambda i: (0, 0)),
        ],
        work=4 * rows * width * cols,
        aliases={3: 0} if held is not None else None,
    )


def out_rows(values, weight, k, rows, name, after=()):
    width, cols = weight.shape

    def kernel(value_ref, w_ref, p_own, *p_mate):
        part = nt(value_ref[...], w_ref[...])
        p_own[...] = part[:rows].astype(bf16)
        put(p_mate, part[rows:])

    fixed = pl.BlockSpec((rows, width), lambda i: (0, 0))
    quarter = [pl.BlockSpec((rows // PIECES, width), lambda i: (0, 0))] * PIECES
    return run(
        kernel,
        [((rows, width), bf16)] + cut((rows, width)),
        [values, weight],
        after,
        name,
        grid=(1,),
        in_specs=[
            pl.BlockSpec((2 * rows, cols), lambda i: (k, 0)),
            pl.BlockSpec((width, cols), lambda i: (0, 0)),
        ],
        out_specs=[fixed] + quarter,
        work=4 * rows * width * cols,
    )


def members_rows(members, weights, k, rows, name, after=()):
    width, cols = weights.shape[1:]

    def kernel(value_ref, w_ref, p_own, *p_mate):
        part = nt(value_ref[0], w_ref[0])
        for m in range(1, 3):
            part = part + nt(value_ref[m], w_ref[m])
        p_own[...] = part[:rows].astype(bf16)
        put(p_mate, part[rows:])

    fixed = pl.BlockSpec((rows, width), lambda i: (0, 0))
    quarter = [pl.BlockSpec((rows // PIECES, width), lambda i: (0, 0))] * PIECES
    return run(
        kernel,
        [((rows, width), bf16)] + cut((rows, width)),
        [members, weights],
        after,
        name,
        grid=(1,),
        in_specs=[
            pl.BlockSpec((3, 2 * rows, cols), lambda i: (0, k, 0)),
            pl.BlockSpec((3, width, cols), lambda i: (0, 0, 0)),
        ],
        out_specs=[fixed] + quarter,
        work=12 * rows * width * cols,
    )


def part(array, m=None, begin=0, end=None):
    value = array[...] if m is None else array[m]
    return value if end is None else value[:, begin:end]


def plain(item):
    return item[0] if isinstance(item, tuple) else item


def spot(item):
    return item[1:] if isinstance(item, tuple) else ()


def span(item):
    return item[3] - item[2] if len(spot(item)) > 1 else plain(item).shape[-1]


def lay_out(jobs):
    plan, ins = [], []
    for left, rights in jobs:
        picks = [[spot(item) for item in right] for right in rights]
        plan.append((len(left), picks, sum(span(right[0]) for right in rights)))
        ins = ins + list(left) + [plain(item) for right in rights for item in right]
    return plan, ins


def sides(plan, refs):
    at = 0
    for n_left, picks, cols in plan:
        left = refs[at : at + n_left]
        at = at + n_left
        columns = []
        for places in picks:
            values = []
            for place in places:
                values.append(part(refs[at], *place))
                at = at + 1
            columns.append(values[0] if len(values) == 1 else jnp.concatenate(values, axis=0))
        yield left, columns[0] if len(columns) == 1 else jnp.concatenate(columns, axis=1), cols


def outer(jobs, name, after=(), sums=()):
    plan, ins = lay_out(jobs)
    total = sum(cols for _, _, cols in plan) + sum(parts[0].shape[1] for parts in sums)
    width = jobs[0][0][0].shape[1]
    products = len(ins)
    ins = ins + [array for parts in sums for array in parts]

    def kernel(*refs):
        column = 0
        for left, rights, cols in sides(plan, refs):
            rows = [ref[...] for ref in left]
            rows = rows[0] if len(rows) == 1 else jnp.concatenate(rows, axis=0)
            refs[-1][:, column : column + cols] = tn(rows, rights).astype(bf16)
            column = column + cols
        at = products
        for parts in sums:
            value = total_of(refs[at : at + len(parts)])
            refs[-1][:, column : column + parts[0].shape[1]] = value.astype(bf16)
            at = at + len(parts)
            column = column + parts[0].shape[1]

    work = sum(2 * width * cols * sum(r.shape[0] for r in left) for (left, _), (_, _, cols) in zip(jobs, plan))
    return run(kernel, [((width, total), bf16)], ins, after, name, room=36, work=work, mark=True)[0]


def outer_halves(links, jobs, turn, name, after=(), sums=()):
    offsets, masks = links.offsets(turn)
    width = jobs[0][0][0].shape[1] if jobs else sums[0][0].shape[0]
    share = width // links.dp
    me = lax.axis_index("dp").reshape(1).astype(jnp.int32)

    plan, ins = lay_out(jobs)
    products = len(ins)
    ins = [me] + ins + [array for parts in sums for array in parts]
    total = sum(cols for _, _, cols in plan) + sum(parts[0].shape[1] for parts in sums)
    half = len(offsets)

    def kernel(me_ref, *refs):
        who = me_ref[0]
        sent_ref, kept_ref = refs[-2], refs[-1]
        ways = ((masks[0], sent_ref), (0, kept_ref))
        column = 0

        def block(off):
            return pl.ds(pl.multiple_of((who ^ off) * share, 128), share)

        for left, rights, cols in sides(plan, refs):
            for flip, dest in ways:
                picked = []
                for off in offsets:
                    parts = [ref[:, block(off ^ flip)] for ref in left]
                    picked.append(parts[0] if len(parts) == 1 else jnp.concatenate(parts, axis=0))
                picked = picked[0] if half == 1 else jnp.concatenate(picked, axis=1)
                dest[:, column : column + cols] = tn(picked, rights).astype(bf16)
            column = column + cols
        at = products
        for parts in sums:
            cols = parts[0].shape[1]
            for flip, dest in ways:
                for i, off in enumerate(offsets):
                    value = total_of([ref.at[block(off ^ flip), :] for ref in refs[at : at + len(parts)]])
                    dest[i * share : (i + 1) * share, column : column + cols] = value.astype(bf16)
            at = at + len(parts)
            column = column + cols

    return run(
        kernel,
        [((half * share, total), bf16)] * 2,
        ins,
        after,
        name,
        in_specs=[SMEM_SPEC] + [None] * (len(ins) - 1),
        room=24,
        work=2 * SLOT * width * total,
        mark=True,
    )


def halve_all(pairs, name, after=()):
    shapes = [(kept.shape[0] // 2, kept.shape[1]) for kept, _ in pairs]
    count = len(pairs)

    def kernel(*refs):
        for i in range(count):
            total = wide(refs[2 * i]) + wide(refs[2 * i + 1])
            half = shapes[i][0]
            refs[2 * count + 2 * i][...] = total[half:].astype(bf16)
            refs[2 * count + 2 * i + 1][...] = total[:half].astype(bf16)

    outs = [(shape, bf16) for shape in shapes for _ in range(2)]
    made = run(kernel, outs, [array for pair in pairs for array in pair], after, name, mark=True)
    return [(made[2 * i], made[2 * i + 1]) for i in range(count)]


def halves(ref_own, ref_mate, c):
    own, mate = ref_own[...], ref_mate[...]
    first = jnp.where(c == 0, own, mate)
    second = jnp.where(c == 0, mate, own)
    return first, second


def shift_rows(value, offset):
    if offset == 0:
        return value
    return pltpu.roll(value, (-offset) % value.shape[0], 0)


def place_mask(count, y, length):
    place = lax.broadcasted_iota(jnp.int32, (count + 2 * MARGIN, 1), 0) + (y * count - MARGIN)
    return ((place >= 0) & (place < length)).astype(f32)


def bordered(own_ref, mate_ref, before, after, who, ny):
    y, c = who // 2, who % 2
    first, second = halves(own_ref, mate_ref, c)
    above = wide(before[0])
    for ref in before[1:]:
        above = above + wide(ref)
    below = wide(after[0])
    for ref in after[1:]:
        below = below + wide(ref)
    above = jnp.where(y > 0, above, 0.0).astype(bf16)
    below = jnp.where(y < ny - 1, below, 0.0).astype(bf16)
    return jnp.concatenate([above, first, second, below], axis=0)


def conv_mix(ny, who, length, own, mate, before, after_rows, weights, taps, name, after=()):
    rows, width = own.shape
    cols = taps.shape[1]
    count = 2 * rows
    lo, hi = MARGIN, MARGIN + count
    n_before = len(before)

    def kernel(who_ref, len_ref, own_ref, mate_ref, w0, w1, taps_ref, *refs):
        rows_in = bordered(own_ref, mate_ref, refs[:n_before], refs[n_before:-5], who_ref[0], ny)
        lin_ref, gate_ref, mix_ref, tally_ref, seen_ref = refs[-5:]
        seen_ref[...] = jnp.concatenate([own_ref[...], mate_ref[...]], axis=0)
        valid = place_mask(count, who_ref[0] // 2, len_ref[0])
        linear = nn(rows_in, w0[...])
        gating = 1.0 / (1.0 + jnp.exp(-nn(rows_in, w1[...])))
        lin_ref[...] = linear
        gate_ref[...] = gating
        glu = linear * gating * valid
        mixture = taps_ref[0:1, :] * shift_rows(glu, -2)
        for j in range(1, KERNEL):
            mixture = mixture + taps_ref[j : j + 1, :] * shift_rows(glu, j - 2)
        mix_ref[...] = mixture
        inside = (valid * mixture)[lo:hi]
        tally_ref[...] = jnp.concatenate(
            [
                jnp.sum(inside, axis=0, keepdims=True),
                jnp.sum(inside * mixture[lo:hi], axis=0, keepdims=True),
                jnp.broadcast_to(jnp.sum(valid[lo:hi], axis=0, keepdims=True), (1, cols)),
                jnp.zeros((5, cols), f32),
            ],
            axis=0,
        )

    ins = [who, length, own, mate, weights[0], weights[1], taps] + list(before) + list(after_rows)
    shape = (count + 2 * MARGIN, cols)
    return run(
        kernel,
        [(shape, f32)] * 3 + [((8, cols), f32), ((count, width), bf16)],
        ins,
        after,
        name,
        in_specs=[SMEM_SPEC, SMEM_SPEC] + [None] * (len(ins) - 2),
        room=28,
        work=4 * count * width * cols,
    )


def batch_terms(tally_ref):
    count = tally_ref[2:3, :]
    mean = tally_ref[0:1, :] / count
    var = tally_ref[1:2, :] / count - mean * mean
    return count, mean, var, lax.rsqrt(var + eps_norm)


def conv_out(who, mixture, tallies, affine, running, weight, rows, name, after=()):
    width, cols = weight.shape
    channels = running.shape[1]
    lo, mid, hi = MARGIN, MARGIN + rows, MARGIN + 2 * rows

    def kernel(who_ref, mix_ref, tally_ref, affine_ref, run_ref, w_ref, act_ref, p_own, *rest):
        *p_mate, new_ref = rest
        c = who_ref[0] % 2
        count, mean, var, inverse = batch_terms(tally_ref)
        own = pl.ds(pl.multiple_of(lo + c * rows, 16), rows)
        mate = pl.ds(pl.multiple_of(lo + (1 - c) * rows, 16), rows)
        mixture = jnp.concatenate([mix_ref[own, :], mix_ref[mate, :]], axis=0)
        shifted = (mixture - mean) * inverse * affine_ref[KERNEL : KERNEL + 1, :] + affine_ref[KERNEL + 1 : KERNEL + 2, :]
        active = (shifted / (1.0 + jnp.exp(-shifted))).astype(bf16)
        act_ref[...] = active
        part = nt(active, w_ref[...])
        p_own[...] = part[:rows].astype(bf16)
        put(p_mate, part[rows:])
        grown = var * count / (count - 1.0)
        new_ref[...] = (1.0 - momentum) * run_ref[...] + momentum * jnp.concatenate(
            [mean[:, :channels], grown[:, :channels]], axis=0
        )

    return run(
        kernel,
        [((2 * rows, cols), bf16), ((rows, width), bf16)] + cut((rows, width)) + [(running.shape, f32)],
        [who, mixture, tallies, affine, running, weight],
        after,
        name,
        in_specs=[SMEM_SPEC] + [None] * 5,
        room=24,
        work=4 * rows * width * cols,
    )


def conv_shift_grad(ny, who, length, own, mate, before, after_rows, mixture, tallies, affine, weight, name, after=()):
    rows, width = own.shape
    cols = weight.shape[1]
    count = 2 * rows
    lo, hi = MARGIN, MARGIN + count
    n_before = len(before)

    def kernel(who_ref, len_ref, own_ref, mate_ref, mix_ref, tally_ref, affine_ref, w_ref, *refs):
        rows_in = bordered(own_ref, mate_ref, refs[:n_before], refs[n_before:-3], who_ref[0], ny)
        dz_ref, out_ref, seen_ref = refs[-3:]
        seen_ref[...] = jnp.concatenate([own_ref[...], mate_ref[...]], axis=0)
        valid = place_mask(count, who_ref[0] // 2, len_ref[0])
        _, mean, _, inverse = batch_terms(tally_ref)
        centred = (mix_ref[...] - mean) * inverse
        shifted = centred * affine_ref[KERNEL : KERNEL + 1, :] + affine_ref[KERNEL + 1 : KERNEL + 2, :]
        logistic = 1.0 / (1.0 + jnp.exp(-shifted))
        slope = logistic * (1.0 + shifted * (1.0 - logistic))
        grad = jnp.where(valid > 0.0, nn(rows_in, w_ref[...]) * slope, 0.0)
        dz_ref[...] = grad
        inner = grad[lo:hi]
        out_ref[...] = jnp.concatenate(
            [
                jnp.sum(inner * centred[lo:hi], axis=0, keepdims=True),
                jnp.sum(inner, axis=0, keepdims=True),
                jnp.zeros((6, cols), f32),
            ],
            axis=0,
        )

    ins = [who, length, own, mate, mixture, tallies, affine, weight] + list(before) + list(after_rows)
    return run(
        kernel,
        [(mixture.shape, f32), ((8, cols), f32), ((count, width), bf16)],
        ins,
        after,
        name,
        in_specs=[SMEM_SPEC, SMEM_SPEC] + [None] * (len(ins) - 2),
        room=28,
        work=4 * count * width * cols,
    )


def conv_in_grad(who, length, dz, mixture, tallies, sums, affine, taps, linear, gating, weights, rows, name, after=()):
    width, cols = weights[0].shape
    count = 2 * rows
    lo, mid, hi = MARGIN, MARGIN + rows, MARGIN + count

    def kernel(who_ref, len_ref, dz_ref, mix_ref, tally_ref, sum_ref, affine_ref, taps_ref, lin_ref, gate_ref, w0, w1, dl_ref, dg_ref, p_own, *rest):
        *p_mate, tap_ref = rest
        c = who_ref[0] % 2
        valid = place_mask(count, who_ref[0] // 2, len_ref[0])
        total, mean, _, inverse = batch_terms(tally_ref)
        centred = (mix_ref[...] - mean) * inverse
        shrink = affine_ref[KERNEL : KERNEL + 1, :] * inverse
        mixed = (sum_ref[1:2, :] + centred * sum_ref[0:1, :]) / total
        grad_mix = jnp.where(valid > 0.0, shrink * (dz_ref[...] - mixed), 0.0)
        grad_glu = taps_ref[0:1, :] * shift_rows(grad_mix, 2)
        for j in range(1, KERNEL):
            grad_glu = grad_glu + taps_ref[j : j + 1, :] * shift_rows(grad_mix, 2 - j)
        linear = lin_ref[...]
        gating = gate_ref[...]
        glu = linear * gating * valid
        inner = grad_mix[lo:hi]
        tap_ref[...] = jnp.concatenate(
            [
                jnp.sum(inner * shift_rows(glu, j - 2)[lo:hi], axis=0, keepdims=True)
                for j in range(KERNEL)
            ]
            + [jnp.zeros((8 - KERNEL, cols), f32)],
            axis=0,
        )
        held = grad_glu * valid * gating
        grad_linear = held.astype(bf16)
        grad_gate = (held * linear * (1.0 - gating)).astype(bf16)

        def turned(value):
            first, second = value[lo:mid], value[mid:hi]
            return jnp.concatenate(
                [jnp.where(c == 0, first, second), jnp.where(c == 0, second, first)], axis=0
            )

        grad_linear = turned(grad_linear)
        grad_gate = turned(grad_gate)
        dl_ref[...] = grad_linear
        dg_ref[...] = grad_gate
        part = nt(grad_linear, w0[...]) + nt(grad_gate, w1[...])
        p_own[...] = part[:rows].astype(bf16)
        put(p_mate, part[rows:])

    return run(
        kernel,
        [((count, cols), bf16)] * 2 + [((rows, width), bf16)] + cut((rows, width)) + [((8, cols), f32)],
        [who, length, dz, mixture, tallies, sums, affine, taps, linear, gating, weights[0], weights[1]],
        after,
        name,
        in_specs=[SMEM_SPEC, SMEM_SPEC] + [None] * 10,
        room=32,
        work=4 * count * width * cols,
    )


class Links:
    def __init__(self, dp, tensor):
        self.dp, self.tensor, self.ny = dp, tensor, tensor // 2
        self.masks = [1 << bit for bit in range(dp.bit_length() - 1)]

    def core(self, value):
        return lax.ppermute(value, "tensor", [(i, i ^ 1) for i in range(self.tensor)])

    def mate(self, pieces):
        return [self.core(piece) for piece in pieces]

    def chip(self, value, k):
        return lax.ppermute(value, "tensor", [(i, i ^ (2 * k)) for i in range(self.tensor)])

    def group(self, value, mask):
        return lax.ppermute(value, "dp", [(i, i ^ mask) for i in range(self.dp)])

    def scatter_grad(self, value):
        return lax.psum_scatter(value, "dp", scatter_dimension=0, tiled=True)

    def two_rounds(self):
        return self.ny == 2 and len(self.masks) == 3

    def first_sums(self, value, channels, name, after=()):
        if not self.two_rounds():
            others = [self.chip(value, k) for k in range(1, self.ny)]
            return add_stats(value, others, channels, name, after)
        size = self.dp * self.tensor
        far = [(i, i ^ (self.masks[0] * self.tensor + 2)) for i in range(size)]
        others = [
            self.group(value, self.masks[0]),
            self.chip(value, 1),
            lax.ppermute(value, ("dp", "tensor"), far),
        ]
        return add_four(value, others, channels, name, after)

    def last_sums(self, value, name):
        if not self.two_rounds():
            return self.sum_group(value, name)
        one, two = self.masks[1:]
        return add_four(value, [self.group(value, mask) for mask in (one, two, one ^ two)], 0, name)

    def sum_group(self, value, name):
        for mask in self.masks:
            value = add_stats(value, [self.group(value, mask)], 0, name)
        return value

    def sum_stats(self, value, channels, name):
        return self.last_sums(self.first_sums(value, channels, name), name)

    def offsets(self, turn):
        masks = list(self.masks)
        if turn:
            masks[:2] = masks[1::-1]
        offsets = [0]
        for mask in masks[:0:-1]:
            offsets = offsets + [off ^ mask for off in offsets]
        return offsets, masks

    def borders(self, own, mate, edge):
        if self.ny == 2:
            straight = lax.ppermute(edge, "tensor", [(1, 3), (2, 0)])
            across = lax.ppermute(edge, "tensor", [(1, 2), (2, 1)])
            return [straight, across], [straight, across]
        c = lax.axis_index("tensor") % 2
        mate = jnp.concatenate(mate)
        head = jnp.where(c == 0, own, mate)[:MARGIN]
        foot = jnp.where(c == 0, mate, own)[own.shape[0] - MARGIN :]
        down = [(i, i + 2) for i in range(self.tensor - 2)]
        up = [(i + 2, i) for i in range(self.tensor - 2)]
        return [lax.ppermute(foot, "tensor", down)], [lax.ppermute(head, "tensor", up)]


class Pieces:
    def __init__(self, links, pieces, turns, name):
        self.links, self.name = links, name
        self.count = len(pieces)
        self.masks = [links.offsets(turn)[1] for turn in turns]
        self.kept = [kept for _, kept in pieces]
        self.at = 0
        self.send([sent for sent, _ in pieces])

    def send(self, sent):
        self.came = [self.links.group(sent[i], self.masks[i][self.at]) for i in range(self.count)]
        self.at += 1

    def step(self, after=()):
        if self.at < len(self.links.masks):
            made = halve_all(list(zip(self.kept, self.came)), self.name + "_half", after)
            self.kept = [kept for _, kept in made]
            self.send([sent for sent, _ in made])
        return self.kept[0]

    def finish(self):
        while self.at < len(self.links.masks):
            self.step()
        return [array for pair in zip(self.kept, self.came) for array in pair]


def finish_one(outs_of, ins_of, width_in, name):
    ins = outs_of + ins_of
    share = ins[0].shape[0]

    def kernel(*refs):
        out = refs[-1]
        parts = [wide(refs[2 * i]) + wide(refs[2 * i + 1]) for i in range(4)]
        out[1] = jnp.concatenate(parts[:2], axis=1)
        out[0] = jnp.concatenate(parts[2:], axis=1)

    return run(kernel, [((2, share, width_in), f32)], ins, (), name)[0]


def split_two(total, hidden, name, after=()):
    share = total.shape[0]

    def kernel(ref, out):
        for m in range(2):
            out[m] = wide(ref)[:, m * hidden : (m + 1) * hidden]

    return run(kernel, [((2, share, hidden), f32)], [total], after, name, mark=True)[0]


def split_heads(ins, cols, channels, name, after=()):
    share = ins[0].shape[0]

    def kernel(*refs):
        three, one, conv = refs[-3:]
        if len(ins) == 1:
            value, rest = wide(refs[0]), wide(refs[0])[:, 4 * cols :]
        else:
            value, rest = wide(refs[0]) + wide(refs[1]), wide(refs[2]) + wide(refs[3])
        for m in range(3):
            three[m] = value[:, m * cols : (m + 1) * cols]
            conv[m] = rest[:, m * channels : (m + 1) * channels]
        one[...] = value[:, 3 * cols : 4 * cols]

    outs = [((3, share, cols), f32), ((share, cols), f32), ((3, share, channels), f32)]
    return run(kernel, outs, list(ins), after, name, mark=True)


def pack_small(depthwise, bn_gain, bn_bias, name):
    channels = depthwise.shape[1]

    def kernel(taps, gain, bias, out):
        out[...] = jnp.concatenate(
            [taps[...], gain[...], bias[...], jnp.zeros((1, channels), f32)], axis=0
        )

    rows = [depthwise, bn_gain[None], bn_bias[None]]
    return run(kernel, [((8, channels), f32)], rows, (), name)[0]


def side_by_side(arrays, name):
    def kernel(*refs):
        refs[-1][...] = jnp.concatenate([ref[...] for ref in refs[:-1]], axis=1)

    shape = (arrays[0].shape[0], sum(array.shape[1] for array in arrays))
    return run(kernel, [(shape, f32)], arrays, (), name)[0]


def pack_sums(gains, table, name, after=()):
    width = gains[0].shape[1]
    each = width // 128

    def kernel(*refs):
        out = refs[-1]
        for g in range(5):
            for i in range(each):
                out[g * each + i : g * each + i + 1, :] = refs[g][0:1, i * 128 : (i + 1) * 128]
        out[5 * each :, :] = refs[5][...]

    return run(kernel, [((5 * each + 128, 128), f32)], list(gains) + [table], after, name)[0]


def with_taps(sums, taps, channels, name, after=()):
    def kernel(sum_ref, tap_ref, out):
        top = sums.shape[0]
        out[:top, :] = sum_ref[...]
        for i in range(channels // 128):
            out[top + 8 * i : top + 8 * i + 8, :] = tap_ref[:, i * 128 : (i + 1) * 128]

    rows = sums.shape[0] + 8 * (channels // 128)
    return run(kernel, [((rows, 128), f32)], [sums, taps], after, name)[0]


def unpack_sums(sums, bn_grads, width, channels, name):
    each = width // 128
    top = 5 * each + 128

    def kernel(sum_ref, bn_ref, gains, table, kernel_grad, gain_grad, bias_grad):
        for g in range(5):
            for i in range(each):
                gains[g : g + 1, i * 128 : (i + 1) * 128] = sum_ref[g * each + i : g * each + i + 1, :]
        table[...] = sum_ref[5 * each : 5 * each + REL, :]
        for i in range(channels // 128):
            at = top + 8 * i
            kernel_grad[:, i * 128 : (i + 1) * 128] = sum_ref[at : at + KERNEL, :]
        gain_grad[...] = bn_ref[0:1, :channels]
        bias_grad[...] = bn_ref[1:2, :channels]

    outs = [((5, width), f32), ((REL, 128), f32), ((KERNEL, channels), f32)] + [((1, channels), f32)] * 2
    return run(kernel, outs, [sums, bn_grads], (), name)


def own_share(weights, me, share, name, after=()):
    cols = weights.shape[2]

    def kernel(me_ref, ref, out):
        rows = pl.ds(pl.multiple_of(me_ref[0] * share, 16), share)
        for m in range(3):
            out[m * share : (m + 1) * share, :] = ref[m, rows, :]

    return run(
        kernel, [((3 * share, cols), bf16)], [me, weights], after, name, in_specs=[SMEM_SPEC, None]
    )[0]


def arrange(conv_proj, gathered, dp, name, after=()):
    _, width, channels = conv_proj.shape
    share = width // dp
    cols = channels * (1 + len(gathered))

    def kernel(own_ref, *refs):
        others, outs = refs[: len(gathered)], refs[len(gathered) :]
        for m in range(3):
            outs[m][:, :channels] = own_ref[m]
            for k, ref in enumerate(others):
                for b in range(dp):
                    at = (b * 3 + m) * share
                    outs[m][b * share : (b + 1) * share, (k + 1) * channels : (k + 2) * channels] = ref[
                        at : at + share, :
                    ]

    return run(kernel, [((width, cols), bf16)] * 3, [conv_proj] + gathered, after, name, mark=True)


def per_device(
    links,
    x_in,
    cotangent,
    lengths,
    norm_gains,
    ffn_first,
    attn_qkv,
    attn_out,
    rel_table,
    conv_proj,
    depthwise,
    bn_gain,
    bn_bias,
    running,
    ffn_second,
):
    MARKS.clear()
    ny = links.ny
    others = list(range(1, ny))
    rows, width = x_in.shape
    channels = bn_gain.shape[0]
    who = lax.axis_index("tensor").astype(jnp.int32).reshape(1)
    gains = norm_gains
    table = window_table(jnp.pad(rel_table, ((0, 128 - REL), (0, 0))))

    me = lax.axis_index("dp").astype(jnp.int32).reshape(1)
    share = width // links.dp
    halves_fit = share % 128 == 0
    small = pack_small(depthwise, bn_gain, bn_bias, "conv_small")
    small = side_by_side([small] + [links.chip(small, k) for k in others], "conv_small_all")

    def send_sums(parts, name, after=()):
        return add_up([parts[0], links.mate(parts[1])], name, after)

    def every(pieces):
        return [pieces[k] for k in range(ny)]

    def split(made):
        return (made[0], made[1 : 1 + PIECES]), made[1 + PIECES :]

    def all_parts(sums, k):
        return [sums[k]] + [links.chip(sums[k ^ j], j) for j in others]

    piece = own_share(conv_proj, me, share, "conv_share")
    came = [links.chip(piece, k) for k in others]
    gathered = [lax.all_gather(other, "dp", axis=0, tiled=True) for other in came]

    (normed, pieces), x_low = norm_rows(x_in, [], 0.0, gains, 0, "ln_in", keep=False, low=True)
    x_rows = [x_in] + [links.chip(x_low, k) for k in others]
    na_first, pre_first, hid_first, sums = {}, {}, {}, {}
    token = ()
    for k in range(ny):
        if k:
            ((normed, pieces),) = norm_rows(
                x_rows[k], [], 0.0, gains, 0, "ln_in", token + (small,), keep=False
            )
        parts, made = split(
            feed(normed, links.mate(pieces), ffn_first, "ffn_one", tuple(came) if k == 0 else ())
        )
        pre_first[k], hid_first[k], na_first[k] = made
        sums[k] = send_sums(parts, "ffn_one_sum")
        token = (sums[k],)

    token = ()
    na_attn, first, qkv, cot_low = {}, {}, None, None
    for k in others + [0]:
        also = cotangent if k == 0 else None
        made = norm_rows(
            x_rows[k], all_parts(sums, k), 0.5, gains, 1, "ln_attn", token, also=also
        )
        (normed, pieces), first[k] = made[:2]
        if k == 0:
            cot_low = made[2]
        qkv, na_attn[k] = qkv_rows(normed, links.mate(pieces), attn_qkv, k, SLOT, qkv, "qkv")
        token = (qkv,)
    cot_rows = [cotangent] + [links.chip(cot_low, k) for k in others]
    heads_out, probs = attend(qkv, who, lengths, table, rows)
    token = tuple(cot_rows[1:])
    arrived = []
    for k in others:
        parts, _ = split(out_rows(heads_out, attn_out, k, rows, "out_proj", token))
        total = send_sums(parts, "out_sum")
        arrived.append(links.chip(total, k))
        token = (total,)
    conv_w = arrange(conv_proj, gathered, links.dp, "conv_weights", token)
    token = token + (conv_w[0],)
    parts, _ = split(out_rows(heads_out, attn_out, 0, rows, "out_proj", token))
    edge = who if ny == 2 else None
    made = norm_rows(
        first[0], [parts[0], links.mate(parts[1])] + arrived, 1.0, gains, 2, "ln_conv", edge=edge
    )
    (normed, pieces), after_attn = made[:2]

    mate = links.mate(pieces)
    before, after_rows = links.borders(normed, mate, made[-1])
    linear, gating, mixture, tallies, conv_in = conv_mix(
        ny, who, lengths, normed, mate, before, after_rows, conv_w, small, "conv_mix"
    )
    tallies = links.sum_stats(tallies, channels, "bn_sum")
    active, *made = conv_out(who, mixture, tallies, small, running, conv_w[2], rows, "conv_out")
    parts, (updated,) = split(made)
    (normed, pieces), after_conv, low = norm_rows(
        after_attn, [parts[0], links.mate(parts[1])], 1.0, gains, 3, "ln_ffn_two", low=True
    )

    x_rows = [after_conv] + [links.chip(low, k) for k in others]
    na_last, pre_last, hid_last, sums = {}, {}, {}, {}
    token = ()
    for k in range(ny):
        if k:
            ((normed, pieces),) = norm_rows(
                x_rows[k], [], 0.0, gains, 3, "ln_ffn_two", token, keep=False
            )
        parts, made = split(feed(normed, links.mate(pieces), ffn_second, "ffn_two"))
        pre_last[k], hid_last[k], na_last[k] = made
        sums[k] = send_sums(parts, "ffn_two_sum")
        token = (sums[k],)

    token = ()
    upper, down, arrived = {}, {}, []
    for k in others + [0]:
        made = norm_last(
            x_rows[k],
            all_parts(sums, k),
            gains,
            cot_rows[k],
            who,
            k,
            lengths,
            "ln_last",
            k == 0,
            token,
        )
        normed, pieces = made[0]
        if k == 0:
            grad, output, gain_five = made[1:]
        parts, made = split(
            feed_grad(normed, links.mate(pieces), pre_last[k], ffn_second, "ffn_two_grad")
        )
        down[k], upper[k] = made
        if k:
            total = send_sums(parts, "ffn_two_grad_sum")
            arrived.append(links.chip(total, k))
            token = (total,)
    made = norm_grad(
        after_conv,
        [parts[0], links.mate(parts[1])] + arrived,
        gains,
        3,
        grad,
        "back_ffn_two",
        factor=1.0,
        edge=edge,
    )
    (low, pieces), grad, gain_four = made[:3]

    mate = links.mate(pieces)
    before, after_rows = links.borders(low, mate, made[-1])
    dz, sums, conv_up = conv_shift_grad(
        ny, who, lengths, low, mate, before, after_rows, mixture, tallies, small, conv_w[2], "conv_dz"
    )
    two_sum = outer(
        [(every(na_last), [every(down)]), (every(upper), [every(hid_last)])], "ffn_two_w", (sums,)
    )
    def by_chip(left, rights, name, after):
        made = []
        for k in range(ny):
            spans = [[(right, None, k * channels, (k + 1) * channels)] for right in rights]
            made.append(outer([([left], spans)], name, after))
        return [made[0]] + [links.chip(made[k], k) for k in others]

    bn_grads = links.first_sums(sums, channels, "bn_grad_sum", (two_sum,))
    out_grad = by_chip(conv_up, [active], "conv_out_w", (bn_grads,))
    bn_grads = links.last_sums(bn_grads, "bn_grad_sum")
    two_sum = links.scatter_grad(two_sum)
    grad_linear, grad_gate, *made = conv_in_grad(
        who,
        lengths,
        dz,
        mixture,
        tallies,
        bn_grads,
        small,
        small,
        linear,
        gating,
        conv_w,
        rows,
        "conv_din",
        tuple(out_grad[1:]),
    )
    parts, (tap_grad,) = split(made)
    (low, pieces), grad, gain_three = norm_grad(
        after_attn, [parts[0], links.mate(parts[1])], gains, 2, grad, "back_conv", factor=1.0
    )

    g_rows = [low] + [links.chip(low, k) for k in others]
    in_grads = by_chip(conv_in, [grad_linear, grad_gate], "conv_in_w", (low,))
    token = (in_grads[0],)
    grad_heads = None
    upper_attn = {}
    for k in range(ny):
        mate = links.mate(pieces) if k == 0 else [links.core(g_rows[k])]
        grad_heads, upper_attn[k] = heads_rows(
            g_rows[k], mate, attn_out, k, SLOT, grad_heads, "dheads", token
        )
        token = (grad_heads,)
    members, table_grad = attend_back(qkv, grad_heads, probs, who, table, rows)
    token = ()
    sums = {}
    for k in range(ny):
        parts, _ = split(members_rows(members, attn_qkv, k, rows, "dqkv", token))
        sums[k] = send_sums(parts, "dqkv_sum")
        token = (sums[k],)
    heads_jobs = [
        (every(na_attn), [[(members, m)] for m in range(3)]),
        (every(upper_attn), [[heads_out]]),
    ]
    conv_grads = [in_grads, out_grad]
    if halves_fit:
        made = outer_halves(links, heads_jobs, 0, "attn_w", token)
        halves = [made, outer_halves(links, [], 1, "conv_w", (made[0],), conv_grads)]
        heads_sum = Pieces(links, halves, (0, 1), "heads")
        token = (halves[1][0],)
    else:
        heads_sum = outer(heads_jobs, "attn_w", token, conv_grads)
        token = (heads_sum,)
        heads_sum = links.scatter_grad(heads_sum)

    upper, down, arrived = {}, {}, []
    for k in others + [0]:
        made = norm_grad(
            first[k],
            all_parts(sums, k),
            gains,
            1,
            grad if k == 0 else g_rows[k],
            "back_attn",
            token,
            factor=0.5,
            keep=k == 0,
            sums=k == 0,
        )
        normed, pieces = made[0]
        if k == 0:
            grad, gain_two = made[1:]
        parts, made = split(
            feed_grad(normed, links.mate(pieces), pre_first[k], ffn_first, "ffn_one_grad")
        )
        down[k], upper[k] = made
        if k:
            total = send_sums(parts, "ffn_one_grad_sum")
            arrived.append(links.chip(total, k))
            token = (total,)
            if halves_fit and k == others[-1]:
                token = (heads_sum.step(token),)
    hidden = ffn_first.shape[2]
    half = hidden // 2
    token = (parts[0],)
    pairs = []
    if halves_fit:
        sides_of = ((every(upper), every(hid_first), (0, 0)), (every(na_first), every(down), (1, 0)))
        for left, right, turns in sides_of:
            halves = []
            for i, turn in enumerate(turns):
                columns = [(r, None, i * half, (i + 1) * half) for r in right]
                halves.append(outer_halves(links, [(left, [columns])], turn, "ffn_one_w", token))
                token = (halves[-1][0],)
            pairs.append(Pieces(links, halves, turns, "one"))
    else:
        first_sum = outer(
            [(every(na_first), [every(down)]), (every(upper), [every(hid_first)])], "ffn_one_w", token
        )
        token = (first_sum,)
        first_sum = links.scatter_grad(first_sum)
    if halves_fit:
        token = (heads_sum.step(token),)
    for pair in pairs:
        token = (pair.step(token),)
    heads_parts = heads_sum.finish() if halves_fit else [heads_sum]
    qkv_sum, out_sum, conv_sum = split_heads(
        heads_parts, attn_qkv.shape[2], channels, "heads_end", token
    )
    token = (out_sum,)
    for pair in pairs[:1]:
        token = (pair.step(token),)
    grad_input, gain_one = norm_grad(
        x_in, [parts[0], links.mate(parts[1])] + arrived, gains, 0, grad, "back_ffn_one", token
    )

    taps = add_stats(tap_grad, [links.chip(tap_grad, k) for k in others], channels, "taps_sum")
    bundle = pack_sums([gain_one, gain_two, gain_three, gain_four, gain_five], table_grad, "pack")
    bundle = add_stats(bundle, [links.core(bundle)], 0, "bundle_sum")
    for k in [1 << bit for bit in range(ny.bit_length() - 1)]:
        bundle = add_stats(bundle, [links.chip(bundle, k)], 0, "bundle_sum")
    token = (bundle,)
    for pair in pairs[1:]:
        token = (pair.step(token),)
    bundle = with_taps(bundle, taps, channels, "pack_taps", token)
    last_sum = split_two(two_sum, hidden, "two_end", token)
    for mask in links.masks:
        bundle = add_stats(bundle, [links.group(bundle, mask)], 0, "bundle_sum")
    norm_sums, table_sums, kernel_grad, gain_grad, bias_grad = unpack_sums(
        bundle, bn_grads, width, channels, "unpack"
    )
    if pairs:
        first_sum = finish_one(pairs[0].finish(), pairs[1].finish(), hidden, "one_end")
    else:
        first_sum = split_two(first_sum, hidden, "one_end")
    return (
        output,
        grad_input,
        norm_sums,
        first_sum,
        qkv_sum,
        out_sum,
        table_sums,
        conv_sum,
        kernel_grad,
        gain_grad.reshape(-1),
        bias_grad.reshape(-1),
        updated,
        last_sum,
    )


def solution(mesh):
    links = Links(mesh.shape["dp"], mesh.shape["tensor"])
    placed = (
        P(("dp", "tensor"), None),
        P(("dp", "tensor"), None),
        P("dp"),
        P(),
        P(None, None, "tensor"),
        P(None, None, "tensor"),
        P(None, "tensor"),
        P(),
        P(None, None, "tensor"),
        P(None, "tensor"),
        P("tensor"),
        P("tensor"),
        P(None, "tensor"),
        P(None, None, "tensor"),
    )
    return jax.shard_map(
        functools.partial(per_device, links),
        mesh=mesh,
        in_specs=placed,
        out_specs=(
            P(("dp", "tensor"), None),
            P(("dp", "tensor"), None),
            P(),
            P(None, "dp", "tensor"),
            P(None, "dp", "tensor"),
            P("dp", "tensor"),
            P(),
            P(None, "dp", "tensor"),
            P(None, "tensor"),
            P("tensor"),
            P("tensor"),
            P(None, "tensor"),
            P(None, "dp", "tensor"),
        ),
        check_vma=False,
    )
```
